32 devices in a mesh: dp: 8 (over z, y), mp: 4 (over x, core).
Axes of the slice: x: 2, y: 2, z: 4, core: 2. Of those that a mesh axis runs over, the one named last changes fastest.
Arguments:
- patches: bfloat16 [96, 196, 768], P(('dp', 'mp')), may hold values from -6 to 6
- partners: int32 [96], P(('dp', 'mp')), may hold values from 0 to 2
- mix_weight: float32 [96], P(('dp', 'mp')), may hold values from 0 to 1
- labels: int32 [96], P(('dp', 'mp')), may hold values from 0 to 999
- teacher_logits: float32 [96, 1000], P(('dp', 'mp')), may hold values from -60 to 60
- patch_weight: float32 [768, 384], P(('dp', 'mp')), may hold values from -0.21875 to 0.21875
- attn_weight: float32 [3, 384, 1536], P(None, None, ('dp', 'mp')), may hold values from -0.4082483 to 0.4082483
- mlp_weight: float32 [3, 2, 384, 1536], P(None, None, 'dp', 'mp'), may hold values from -0.3125 to 0.3125
- positions: float32 [198, 384], replicated, may hold values from -6 to 6
- head_weight: float32 [384, 2000], replicated, may hold values from -2 to 2
- norm_params: float32 [14, 384], replicated, may hold values from -1.2 to 1.4
- patch_first: float32 [768, 384], P(('dp', 'mp')), may hold values from -1.335144e-05 to 1.335144e-05
- attn_first: float32 [3, 384, 1536], P(None, None, ('dp', 'mp')), may hold values from -1.335144e-05 to 1.335144e-05
- mlp_first: float32 [3, 2, 384, 1536], P(None, None, 'dp', 'mp'), may hold values from -1.335144e-05 to 1.335144e-05
- pos_first: float32 [198, 384], replicated, may hold values from -1.335144e-05 to 1.335144e-05
- head_first: float32 [384, 2000], replicated, may hold values from -1.335144e-05 to 1.335144e-05
- norm_first: float32 [14, 384], replicated, may hold values from -1.335144e-05 to 1.335144e-05
- patch_second: float32 [768, 384], P(('dp', 'mp')), may hold values from 6.20512e-14 to 2.482048e-13
- attn_second: float32 [3, 384, 1536], P(None, None, ('dp', 'mp')), may hold values from 6.20512e-14 to 2.482048e-13
- mlp_second: float32 [3, 2, 384, 1536], P(None, None, 'dp', 'mp'), may hold values from 6.20512e-14 to 2.482048e-13
- pos_second: float32 [198, 384], replicated, may hold values from 6.20512e-14 to 2.482048e-13
- head_second: float32 [384, 2000], replicated, may hold values from 6.20512e-14 to 2.482048e-13
- norm_second: float32 [14, 384], replicated, may hold values from 6.20512e-14 to 2.482048e-13
Outputs:
- loss_sum: float32 [], replicated
- global_norm: float32 [], replicated
- new_patch: float32 [768, 384], P(('dp', 'mp'))
- new_attn: float32 [3, 384, 1536], P(None, None, ('dp', 'mp'))
- new_mlp: float32 [3, 2, 384, 1536], P(None, None, 'dp', 'mp')
- new_pos: float32 [198, 384], replicated
- new_head: float32 [384, 2000], replicated
- new_norms: float32 [14, 384], replicated
- patch_first_new: float32 [768, 384], P(('dp', 'mp'))
- attn_first_new: float32 [3, 384, 1536], P(None, None, ('dp', 'mp'))
- mlp_first_new: float32 [3, 2, 384, 1536], P(None, None, 'dp', 'mp')
- pos_first_new: float32 [198, 384], replicated
- head_first_new: float32 [384, 2000], replicated
- norm_first_new: float32 [14, 384], replicated
- patch_second_new: float32 [768, 384], P(('dp', 'mp'))
- attn_second_new: float32 [3, 384, 1536], P(None, None, ('dp', 'mp'))
- mlp_second_new: float32 [3, 2, 384, 1536], P(None, None, 'dp', 'mp')
- pos_second_new: float32 [198, 384], replicated
- head_second_new: float32 [384, 2000], replicated
- norm_second_new: float32 [14, 384], replicated
The draws below stay inside these ranges and needn't reach their ends.
Inputs may be any that keep to these rules, and one draw needn't show every extreme that they name: `partners`: an image's partner is the image at this index among the 3 images of its aligned block.
All inputs are finite; a program needn't handle non-finite values.
Results may differ from the reference program's by a relative error of at most 0.025.
Values may be sent and summed in bfloat16 or wider, within the bound.
A program may use at most 256 MiB of HBM per device.

```python
import math
import jax
import jax.numpy as jnp
from jax import lax

D = 384
HEADS = 6
FF = 1536
C = 1000
PATCH_DIM = 768
NPATCH = 196
L = 3
IMG_DEV = 3
HD = 64
TOK = 198
GROUP = 12
IMAGES = 96
P_ALL = 6452736
N_DP = 8


def draw_attn_weight(key, part):
    columns = jnp.arange(4 * D)
    factor = jnp.where(columns < 2 * D, 1.4, jnp.where(columns < 3 * D, 1.0, 2.0))
    normal_draw = jax.random.truncated_normal(key, -4.0, 4.0, (L, D, 4 * D), jnp.float32)
    return normal_draw * factor * D ** (-0.5)


def draw_norm_params(key, part):
    gain_key = jax.random.fold_in(key, 11)
    shift_key = jax.random.fold_in(key, 12)
    row_ids = jnp.arange(4 * L + 2)[:, None]
    gain_rows = jax.random.uniform(gain_key, (4 * L + 2, D), jnp.float32, 0.6, 1.4)
    shift_rows = 0.3 * jax.random.truncated_normal(shift_key, -4.0, 4.0, (4 * L + 2, D), jnp.float32)
    return jnp.where(row_ids % 2 == 0, gain_rows, shift_rows)


def rising_scale(growth):
    image_ids = jnp.arange(IMAGES)
    outer_count = IMAGES // GROUP
    inner_count = GROUP // IMG_DEV
    outer_pos = (image_ids // GROUP).astype(jnp.float32) / max(outer_count - 1, 1)
    inner_pos = (image_ids % GROUP // IMG_DEV).astype(jnp.float32) / max(inner_count - 1, 1)
    return 1.3 * (1.0 + growth * outer_pos) * (1.0 + growth * inner_pos)


def draw_teacher_logits(key, part):
    key = jax.random.fold_in(key, 21)
    values = jax.random.truncated_normal(key, -3.0, 3.0, (IMAGES, C), jnp.float32)
    return values * rising_scale(2.0)[:, None]


def with_ends(values, rng, low, largest):
    dims = values.shape
    index_at = [jax.random.randint(jax.random.fold_in(rng, axis), (), 0, dims[axis]) for axis in range(len(dims))]
    values = values.at[tuple(index_at)].set(low)
    longest = dims.index(max(dims))
    index_at[longest] = (index_at[longest] + 1) % dims[longest]
    return values.at[tuple(index_at)].set(largest)


def block_scale(key, dims, cuts, smallest, high):
    def one(dim, blocks):
        heights = jax.random.uniform(jax.random.fold_in(jax.random.fold_in(key, 6), dim), (blocks,), jnp.float32, smallest / len(cuts), high / len(cuts))
        return jnp.repeat(jnp.exp(heights), dims[dim] // blocks).reshape((-1,) + (1,) * (len(dims) - dim - 1))

    factor_of = one(*cuts[0])
    for cut in cuts[1:]:
        factor_of = factor_of * one(*cut)
    return factor_of


def gaussian(rng, shape, deviation, limit, shards=(), kind=jnp.bfloat16):
    array = deviation * jax.random.normal(rng, shape, jnp.float32)
    if shards:
        array = array * block_scale(rng, shape, shards, -0.22, 0.18)
    return jnp.clip(array, -limit, limit).astype(kind)


def setup_inputs(seed: int = 0) -> dict:
    seeds = jax.random.split(jax.random.key(seed), 24)
    patches = gaussian(seeds[0], (IMAGES, NPATCH, PATCH_DIM), 1.0, 6.0, ((0, 32),))
    partners = with_ends(jax.random.randint(seeds[1], (IMAGES,), 0, IMG_DEV), jax.random.fold_in(seeds[1], 1), 0, IMG_DEV - 1).astype(jnp.int32)
    mix_weight = jnp.clip(1.0 * jax.random.uniform(seeds[2], (IMAGES,), jnp.float32) ** block_scale(seeds[2], (IMAGES,), ((0, 32),), -0.2, 0.2), 0.0, 1.0)
    labels = with_ends(jax.random.randint(seeds[3], (IMAGES,), 0, C), jax.random.fold_in(seeds[3], 1), 0, C - 1).astype(jnp.int32)
    teacher_logits = draw_teacher_logits(jax.random.fold_in(seeds[23], 71), 0)
    patch_weight = gaussian(seeds[5], (PATCH_DIM, D), PATCH_DIM ** -0.5, 0.21875, ((0, 32),), jnp.float32)
    attn_weight = draw_attn_weight(jax.random.fold_in(seeds[23], 71), 0)
    mlp_weight = gaussian(seeds[7], (L, 2, D, FF), D ** -0.5, 0.3125, ((2, 8), (3, 4)), jnp.float32)
    positions = gaussian(seeds[8], (TOK, D), 0.5, 6.0, (), jnp.float32)
    head_weight = gaussian(seeds[9], (D, 2 * C), (3.0 / D ** 0.5), 2.0, (), jnp.float32)
    norm_params = draw_norm_params(jax.random.fold_in(seeds[23], 71), 0)
    patch_first = gaussian(seeds[11], (PATCH_DIM, D), (0.002222 / P_ALL ** 0.5), 1.33514404296875e-05, ((0, 32),), jnp.float32)
    attn_first = gaussian(seeds[12], (L, D, 4 * D), (0.002222 / P_ALL ** 0.5), 1.33514404296875e-05, ((2, 32),), jnp.float32)
    mlp_first = gaussian(seeds[13], (L, 2, D, FF), (0.002222 / P_ALL ** 0.5), 1.33514404296875e-05, ((2, 8), (3, 4)), jnp.float32)
    pos_first = gaussian(seeds[14], (TOK, D), (0.002222 / P_ALL ** 0.5), 1.33514404296875e-05, (), jnp.float32)
    head_first = gaussian(seeds[15], (D, 2 * C), (0.002222 / P_ALL ** 0.5), 1.33514404296875e-05, (), jnp.float32)
    norm_first = gaussian(seeds[16], (4 * L + 2, D), (0.002222 / P_ALL ** 0.5), 1.33514404296875e-05, (), jnp.float32)
    patch_second = jnp.clip(jnp.exp(math.log(2.482048041489021e-13) - 1.3862944 * jax.random.uniform(seeds[17], (PATCH_DIM, D), jnp.float32) ** block_scale(seeds[17], (PATCH_DIM, D), ((0, 32),), -0.2, 0.2)), 6.205120103722553e-14, 2.482048041489021e-13)
    attn_second = jnp.clip(jnp.exp(math.log(2.482048041489021e-13) - 1.3862944 * jax.random.uniform(seeds[18], (L, D, 4 * D), jnp.float32) ** block_scale(seeds[18], (L, D, 4 * D), ((2, 32),), -0.2, 0.2)), 6.205120103722553e-14, 2.482048041489021e-13)
    mlp_second = jnp.clip(jnp.exp(math.log(2.482048041489021e-13) - 1.3862944 * jax.random.uniform(seeds[19], (L, 2, D, FF), jnp.float32) ** block_scale(seeds[19], (L, 2, D, FF), ((2, 8), (3, 4)), -0.2, 0.2)), 6.205120103722553e-14, 2.482048041489021e-13)
    pos_second = jnp.clip(jnp.exp(jax.random.uniform(seeds[20], (TOK, D), jnp.float32, math.log(6.205120103722553e-14), math.log(2.482048041489021e-13))), 6.205120103722553e-14, 2.482048041489021e-13)
    head_second = jnp.clip(jnp.exp(jax.random.uniform(seeds[21], (D, 2 * C), jnp.float32, math.log(6.205120103722553e-14), math.log(2.482048041489021e-13))), 6.205120103722553e-14, 2.482048041489021e-13)
    norm_second = jnp.clip(jnp.exp(jax.random.uniform(seeds[22], (4 * L + 2, D), jnp.float32, math.log(6.205120103722553e-14), math.log(2.482048041489021e-13))), 6.205120103722553e-14, 2.482048041489021e-13)
    return dict(patches=patches, partners=partners, mix_weight=mix_weight, labels=labels, teacher_logits=teacher_logits, patch_weight=patch_weight, attn_weight=attn_weight, mlp_weight=mlp_weight, positions=positions, head_weight=head_weight, norm_params=norm_params, patch_first=patch_first, attn_first=attn_first, mlp_first=mlp_first, pos_first=pos_first, head_first=head_first, norm_first=norm_first, patch_second=patch_second, attn_second=attn_second, mlp_second=mlp_second, pos_second=pos_second, head_second=head_second, norm_second=norm_second)


@jax.custom_vjp
def low(v):
    return lax.optimization_barrier(v.astype(jnp.bfloat16)).astype(jnp.float32)

@jax.custom_vjp
def low_back(v):
    return v

def low_keep(v):
    return (low(v), None)

def low_pass(kept, grad):
    return (grad,)

def back_keep(v):
    return (v, None)

def back_low(kept, grad):
    return (low(grad),)
low.defvjp(low_keep, low_pass)
low_back.defvjp(back_keep, back_low)
HIGHEST = lax.Precision.HIGHEST
LN_EPS = 1e-06
TEMPER = 3.0
MAX_NORM = 0.02
BETA_ONE = 0.9
BETA_TWO = 0.999
STEP_RATES = (0.05, 0.05, 0.05, 0.4, 0.12, 0.5)
DECAY = 0.05
ADAM_EPS = 1e-08
ADAM_STEP = 10.0

def matmul(left_side, right_side):
    return jnp.matmul(left_side, right_side, precision=HIGHEST)

def layer_norm(inputs, norm_gain, norm_shift):
    centred = inputs - lax.optimization_barrier(jnp.mean(inputs, axis=-1, keepdims=True))
    inverse = lax.rsqrt(lax.optimization_barrier(jnp.mean(centred * centred, axis=-1, keepdims=True)) + LN_EPS)
    return centred * inverse * norm_gain + norm_shift

def group_loss(weights, group_block):
    patch_w, attn_w, mlp_w, pos_rows, head_w, norm_rows = weights
    patch_block, partner_block, mix_block, label_block, teacher_block = group_block
    image_count = patch_block.shape[0]
    partner_index = jnp.arange(image_count, dtype=jnp.int32) // IMG_DEV * IMG_DEV + partner_block
    own_rows = patch_block.astype(jnp.float32)
    partner_rows = own_rows[partner_index]
    mix_rows = mix_block[:, None, None]
    mixed_rows = low(mix_rows * own_rows + (1.0 - mix_rows) * partner_rows)
    embedded = low_back(matmul(mixed_rows, patch_w)) + pos_rows[2:]
    lead_rows = jnp.broadcast_to(pos_rows[:2], (image_count, 2, D))
    stream = jnp.concatenate([lead_rows, embedded], axis=1)
    for depth_index in range(L):
        norm_here = norm_rows[4 * depth_index:4 * depth_index + 4]
        attn_layer = attn_w[depth_index]
        proj_qkv = low(low_back(matmul(low(layer_norm(stream, norm_here[0], norm_here[1])), attn_layer[:, :3 * D])))
        proj_qkv = proj_qkv.reshape(image_count, TOK, 3, HEADS, HD)
        scores = low_back(jnp.einsum('bqhe,bkhe->bhqk', proj_qkv[:, :, 0], proj_qkv[:, :, 1], precision=HIGHEST) * HD ** (-0.5))
        attn_probs = jax.nn.softmax(scores, axis=-1)
        attended = jnp.einsum('bhqk,bkhe->bqhe', low(attn_probs), proj_qkv[:, :, 2], precision=HIGHEST)
        attended = low(low_back(attended)).reshape(image_count, TOK, D)
        stream = stream + low_back(matmul(attended, attn_layer[:, 3 * D:]))
        hidden = low_back(matmul(low(layer_norm(stream, norm_here[2], norm_here[3])), mlp_w[depth_index, 0]))
        activated = low(jax.nn.gelu(hidden, approximate=False))
        stream = stream + low_back(jnp.einsum('bte,de->btd', activated, mlp_w[depth_index, 1], precision=HIGHEST))
    final_rows = low(layer_norm(stream[:, :2], norm_rows[4 * L], norm_rows[4 * L + 1]))
    logits_cls = low_back(matmul(final_rows[:, 0], head_w[:, :C]))
    logits_dist = low_back(matmul(final_rows[:, 1], head_w[:, C:]))
    partner_labels = label_block[partner_index]
    target = mix_block[:, None] * jax.nn.one_hot(label_block, C, dtype=jnp.float32) + (1.0 - mix_block[:, None]) * jax.nn.one_hot(partner_labels, C, dtype=jnp.float32)
    cross = -lax.optimization_barrier(jnp.sum(target * jax.nn.log_softmax(logits_cls, axis=-1), axis=-1))
    teacher_log = jax.nn.log_softmax(teacher_block / TEMPER, axis=-1)
    student_log = jax.nn.log_softmax(logits_dist / TEMPER, axis=-1)
    diverge = TEMPER * TEMPER * lax.optimization_barrier(jnp.sum(jnp.exp(teacher_log) * (teacher_log - student_log), axis=-1))
    return jnp.sum(0.5 * cross + 0.5 * diverge)

def adam_update(weight, first_moment, second, grad_in, factor, step_rate):
    clipped = grad_in * factor
    first_moment = BETA_ONE * first_moment + (1.0 - BETA_ONE) * clipped
    second = BETA_TWO * second + (1.0 - BETA_TWO) * clipped * clipped
    adam_move = first_moment / (1.0 - BETA_ONE ** ADAM_STEP) / (jnp.sqrt(second / (1.0 - BETA_TWO ** ADAM_STEP)) + ADAM_EPS)
    return (weight - step_rate * (adam_move + DECAY * weight), first_moment, second)

def reference(patches, partners, mix_weight, labels, teacher_logits, patch_weight, attn_weight, mlp_weight, positions, head_weight, norm_params, patch_first, attn_first, mlp_first, pos_first, head_first, norm_first, patch_second, attn_second, mlp_second, pos_second, head_second, norm_second):
    masters = (patch_weight, attn_weight, mlp_weight, positions, head_weight, norm_params)
    blocks = (patches.reshape(N_DP, GROUP, NPATCH, PATCH_DIM), partners.reshape(N_DP, GROUP), mix_weight.reshape(N_DP, GROUP), labels.reshape(N_DP, GROUP), teacher_logits.reshape(N_DP, GROUP, C))

    def total_loss(weights):
        rounded = (low(weights[0]), low(weights[1]), low(weights[2]), weights[3], low(weights[4]), weights[5])

        def per_group(group_block):
            return jax.checkpoint(group_loss)(rounded, group_block)
        summed = jnp.sum(lax.map(per_group, blocks))
        return (summed / IMAGES, summed)
    mean_loss, pullback, loss_sum = jax.vjp(total_loss, masters, has_aux=True)
    gradients = pullback(jnp.ones_like(mean_loss))[0]
    squares = [jnp.sum(grad_in * grad_in) for grad_in in gradients]
    global_norm = jnp.sqrt(squares[0] + squares[1] + squares[2] + squares[3] + squares[4] + squares[5])
    factor = jnp.minimum(1.0, MAX_NORM / global_norm)
    firsts = (patch_first, attn_first, mlp_first, pos_first, head_first, norm_first)
    seconds = (patch_second, attn_second, mlp_second, pos_second, head_second, norm_second)
    results = [adam_update(masters[number], firsts[number], seconds[number], gradients[number], factor, STEP_RATES[number]) for number in range(6)]
    return (loss_sum, global_norm, results[0][0], results[1][0], results[2][0], results[3][0], results[4][0], results[5][0], results[0][1], results[1][1], results[2][1], results[3][1], results[4][1], results[5][1], results[0][2], results[1][2], results[2][2], results[3][2], results[4][2], results[5][2])
```

```python
import jax
import jax.numpy as jnp
from jax import lax
from jax.experimental import pallas as pl
from jax.experimental.pallas import tpu as pltpu
from jax.sharding import PartitionSpec as P

D = 384
C = 1000
PATCH_DIM = 768
NPATCH = 196
L = 3
TOK = 198
IMG = 3
ROWS = 208
ALL = IMG * ROWS
BLOCKS = 4

LN_EPS = 1e-06
TEMPER = 3.0
MAX_NORM = 0.02
BETA_ONE = 0.9
BETA_TWO = 0.999
STEP_RATES = (0.05, 0.05, 0.05, 0.4, 0.12, 0.5)
DECAY = 0.05
ADAM_EPS = 1e-08
ADAM_STEP = 10.0
LOWEST = -1e30

BF16 = jnp.bfloat16
F32 = jnp.float32
VMEM = pl.BlockSpec(memory_space=pltpu.VMEM)
SMEM = pl.BlockSpec(memory_space=pltpu.SMEM)
HBM = pl.BlockSpec(memory_space=pl.ANY)


def nn(left, right):
    return jnp.dot(left, right, preferred_element_type=F32)


def nt(left, right):
    return lax.dot_general(left, right, (((1,), (1,)), ((), ())), preferred_element_type=F32)


def tn(left, right):
    return lax.dot_general(left, right, (((0,), (0,)), ((), ())), preferred_element_type=F32)


def unit_norm(inputs):
    centred = inputs - jnp.mean(inputs, axis=-1, keepdims=True)
    inverse = lax.rsqrt(jnp.mean(centred * centred, axis=-1, keepdims=True) + LN_EPS)
    return centred * inverse, inverse


def norm_backward(grad_out, inputs, gain):
    normed, inverse = unit_norm(inputs)
    grad_gain = jnp.sum(grad_out * normed, axis=0, keepdims=True)
    grad_shift = jnp.sum(grad_out, axis=0, keepdims=True)
    scaled = grad_out * gain
    grad_in = inverse * (
        scaled
        - jnp.mean(scaled, axis=-1, keepdims=True)
        - normed * jnp.mean(scaled * normed, axis=-1, keepdims=True)
    )
    return grad_in, grad_gain, grad_shift


def head_lanes(shape, head):
    lane = lax.broadcasted_iota(jnp.int32, shape, len(shape) - 1)
    return lane < 64 if head == 0 else lane >= 64


def attend(qkv, out, image, pair):
    rows = slice(image * ROWS, (image + 1) * ROWS)
    lanes = 128 * pair
    queries = qkv[rows, lanes : lanes + 128] * BF16(0.125)
    keys = qkv[rows, D + lanes : D + lanes + 128]
    values = qkv[rows, 2 * D + lanes : 2 * D + lanes + 128]
    key_lane = lax.broadcasted_iota(jnp.int32, (1, ROWS), 1)
    parts = []
    for head in range(2):
        scores = nt(jnp.where(head_lanes((ROWS, 128), head), queries, BF16(0)), keys)
        scores = jnp.where(key_lane < TOK, scores, LOWEST)
        weights = jnp.exp(scores - jnp.max(scores, axis=-1, keepdims=True))
        inverse = 1.0 / jnp.sum(weights, axis=-1, keepdims=True)
        parts.append(nn(weights.astype(BF16), values) * inverse)
    out[rows, lanes : lanes + 128] = jnp.where(
        head_lanes((ROWS, 128), 0), parts[0], parts[1]
    ).astype(BF16)


def attend_backward(qkv, grad_out, grad_qkv, image, pair):
    rows = slice(image * ROWS, (image + 1) * ROWS)
    lanes = 128 * pair
    queries = qkv[rows, lanes : lanes + 128] * BF16(0.125)
    keys = qkv[rows, D + lanes : D + lanes + 128]
    values = qkv[rows, 2 * D + lanes : 2 * D + lanes + 128]
    grad = grad_out[rows, lanes : lanes + 128]
    key_row = lax.broadcasted_iota(jnp.int32, (ROWS, 1), 0)
    grad_q, grad_k, grad_v = [], [], []
    for head in range(2):
        own = head_lanes((ROWS, 128), head)
        scores = nt(jnp.where(own, keys, BF16(0)), queries)
        scores = jnp.where(key_row < TOK, scores, LOWEST)
        probs = jnp.exp(scores - jnp.max(scores, axis=0, keepdims=True))
        probs = probs * (1.0 / jnp.sum(probs, axis=0, keepdims=True))
        grad_probs = nt(jnp.where(own, values, BF16(0)), grad)
        total = jnp.sum(probs * grad_probs, axis=0, keepdims=True)
        grad_scores = (probs * (grad_probs - total)).astype(BF16)
        grad_v.append(nn(probs.astype(BF16), grad))
        grad_k.append(nn(grad_scores, queries))
        grad_q.append(tn(grad_scores, keys))
    first = head_lanes((ROWS, 128), 0)
    grad_qkv[rows, lanes : lanes + 128] = (
        jnp.where(first, grad_q[0], grad_q[1]) * 0.125
    ).astype(BF16)
    grad_qkv[rows, D + lanes : D + lanes + 128] = jnp.where(first, grad_k[0], grad_k[1]).astype(
        BF16
    )
    grad_qkv[rows, 2 * D + lanes : 2 * D + lanes + 128] = jnp.where(
        first, grad_v[0], grad_v[1]
    ).astype(BF16)


def mix_images(partners, mix, patches, mixed):
    for image in range(IMG):
        total = None
        for other in range(IMG):
            share = jnp.where(partners[image] == other, 1.0 - mix[image], 0.0)
            if image == other:
                share = share + mix[image]
            term = share * patches[other].astype(F32)
            total = term if total is None else total + term
        padding = jnp.zeros((ROWS - NPATCH, PATCH_DIM), F32)
        mixed[image * ROWS : (image + 1) * ROWS, :] = jnp.concatenate(
            [total, padding], axis=0
        ).astype(BF16)


def head_and_loss(
    image_count, stream, norms, partners, mix, labels, teacher, head, loss, feature, dlogits, dtop, dnorm
):
    picked = [
        stream[image * ROWS + NPATCH + kind : image * ROWS + NPATCH + kind + 1, :]
        for kind in range(2)
        for image in range(IMG)
    ]
    top = jnp.concatenate(picked + [jnp.zeros((2, D), F32)], axis=0)
    gain = norms[4 * L : 4 * L + 1, :]
    normed, _ = unit_norm(top)
    features = (normed * gain + norms[4 * L + 1 : 4 * L + 2, :]).astype(BF16)
    weights = head[...].astype(BF16)
    row = lax.broadcasted_iota(jnp.int32, (8, 2 * C), 0)
    lane = lax.broadcasted_iota(jnp.int32, (8, 2 * C), 1)
    is_class = row < IMG
    low_lane = jnp.where(is_class, 0, C)
    high_lane = jnp.where(is_class, C, jnp.where(row < 2 * IMG, 2 * C, 0))
    used = (lane >= low_lane) & (lane < high_lane)

    def log_softmax(values):
        values = jnp.where(used, values, LOWEST)
        shifted = values - jnp.max(values, axis=-1, keepdims=True)
        return shifted - jnp.log(jnp.sum(jnp.exp(shifted), axis=-1, keepdims=True))

    taught = jnp.concatenate([jnp.zeros((IMG, C), F32), teacher[...]], axis=1)
    taught = jnp.concatenate(
        [jnp.zeros((IMG, 2 * C), F32), taught, jnp.zeros((8 - 2 * IMG, 2 * C), F32)], axis=0
    )
    logits = nn(features, weights)
    student_log = log_softmax(jnp.where(is_class, logits, logits / TEMPER))
    teacher_log = log_softmax(taught / TEMPER)
    teacher_prob = jnp.exp(teacher_log)
    target = jnp.zeros((8, 2 * C), F32)
    for image in range(IMG):
        partner_label = labels[IMG - 1]
        for other in range(IMG - 1):
            partner_label = jnp.where(partners[image] == other, labels[other], partner_label)
        ours = jnp.where(lane == labels[image], mix[image], 0.0) + jnp.where(
            lane == partner_label, 1.0 - mix[image], 0.0
        )
        target = target + jnp.where(row == image, ours, 0.0)
    terms = jnp.where(
        is_class,
        -0.5 * target * student_log,
        0.5 * TEMPER * TEMPER * teacher_prob * (teacher_log - student_log),
    )
    terms = jnp.where(used, terms, 0.0)
    loss[...] = jnp.broadcast_to(jnp.sum(terms, axis=(0, 1), keepdims=True), (8, 128))
    wanted = jnp.where(is_class, target, teacher_prob)
    scale = jnp.where(is_class, 0.5 / image_count, 0.5 * TEMPER / image_count)
    grad_logits = (scale * jnp.where(used, jnp.exp(student_log) - wanted, 0.0)).astype(BF16)
    feature[...] = features.astype(F32)
    dlogits[...] = grad_logits.astype(F32)
    grad_top, grad_gain, grad_shift = norm_backward(nt(grad_logits, weights), top, gain)
    dtop[...] = grad_top
    dnorm[...] = jnp.concatenate([grad_gain, grad_shift, jnp.zeros((6, D), F32)], axis=0)


def forward_kernel(
    image_count,
    partners, mix, labels, patches, teacher, pos, head, norms, patch_w, attn_w, mlp_w,
    mixed_h, x_h, a_h, qkv_h, o_h, x1_h, a2_h, z_h, slope_h, loss, feature, dlogits, dtop, dnorm,
    mixed, x, a, qkv, o, x1, a2, z, slope, y, sems,
):
    mix_images(partners, mix, patches, mixed)
    embedded = nn(mixed[...], patch_w[...])
    for image in range(IMG):
        rows = slice(image * ROWS, (image + 1) * ROWS)
        x[rows, :] = embedded[rows] + pos[...]
    mixed_copy = pltpu.make_async_copy(mixed, mixed_h, sems.at[8])
    mixed_copy.start()

    def layer(depth, carry):
        norm = [norms[pl.ds(4 * depth + n, 1), :] for n in range(4)]
        a[...] = (unit_norm(x[...])[0] * norm[0] + norm[1]).astype(BF16)
        attn = attn_w.at[depth]
        for n in range(3):
            qkv[:, D * n : D * n + D] = nt(a[...], attn[2 * n : 2 * n + 2].reshape(D, D)).astype(BF16)
        for image in range(IMG):
            for pair in range(3):
                attend(qkv, o, image, pair)
        x1[...] = x[...] + nt(o[...], attn[6:8].reshape(D, D))
        a2[...] = (unit_norm(x1[...])[0] * norm[2] + norm[3]).astype(BF16)
        y[...] = x1[...]

        def block(m, carry):
            hidden = nn(a2[...], mlp_w[depth, 0, m].reshape(D, D))
            phi = 0.5 * (1.0 + lax.erf(hidden * 2.0**-0.5))
            low = (hidden * phi).astype(BF16)
            z[m] = low
            slope[m] = (phi + hidden * (jnp.exp(-0.5 * hidden * hidden) * 0.3989422804014327)).astype(BF16)
            y[...] += nt(low, mlp_w[depth, 1, m].reshape(D, D))
            return carry

        lax.fori_loop(0, BLOCKS, block, 0)
        saved = [(x, x_h), (a, a_h), (qkv, qkv_h), (o, o_h), (x1, x1_h), (a2, a2_h), (z, z_h), (slope, slope_h)]
        copies = [
            pltpu.make_async_copy(source, target.at[depth], sems.at[n])
            for n, (source, target) in enumerate(saved)
        ]
        for copy in copies:
            copy.start()
        for copy in copies:
            copy.wait()
        x[...] = y[...]
        return carry

    lax.fori_loop(0, L, layer, 0)
    mixed_copy.wait()
    head_and_loss(
        image_count, x, norms, partners, mix, labels, teacher, head, loss, feature, dlogits, dtop, dnorm
    )


SAVED = (
    ((ALL, PATCH_DIM), BF16),
    ((L, ALL, D), F32),
    ((L, ALL, D), BF16),
    ((L, ALL, 3 * D), BF16),
    ((L, ALL, D), BF16),
    ((L, ALL, D), F32),
    ((L, ALL, D), BF16),
    ((L, BLOCKS, ALL, D), BF16),
    ((L, BLOCKS, ALL, D), BF16),
)


def forward(image_count, *operands):
    small = (((8, 128), F32), ((8, D), F32), ((8, 2 * C), F32), ((8, D), F32), ((8, D), F32))
    scratch = [(SAVED[0])] + [(shape[1:], kind) for shape, kind in SAVED[1:]] + [((ALL, D), F32)]
    return pl.pallas_call(
        lambda *refs: forward_kernel(image_count, *refs),
        out_shape=[jax.ShapeDtypeStruct(*entry) for entry in SAVED + small],
        in_specs=[SMEM] * 3 + [VMEM] * 8,
        out_specs=[HBM] * len(SAVED) + [VMEM] * len(small),
        scratch_shapes=[pltpu.VMEM(*entry) for entry in scratch] + [pltpu.SemaphoreType.DMA((9,))],
        compiler_params=pltpu.CompilerParams(vmem_limit_bytes=60 * 2**20),
        name="forward",
    )(*operands)


def backward_kernel(
    dtop, norms, mixed, attn_w, mlp_w, x_h, a_h, qkv_h, o_h, x1_h, a2_h, z_h, slope_h,
    grad_patch, grad_attn, grad_mlp, grad_norm, grad_pos,
    dx, dy, low, dout, dqkv, x, a, qkv, o, x1, a2, z, slope, sems,
):
    saved = [(x_h, x), (a_h, a), (qkv_h, qkv), (o_h, o), (x1_h, x1), (a2_h, a2), (z_h, z), (slope_h, slope)]

    def fetch(depth, slot):
        return [
            pltpu.make_async_copy(source.at[depth], target.at[slot], sems.at[slot, n])
            for n, (source, target) in enumerate(saved)
        ]

    for copy in fetch(L - 1, 0):
        copy.start()
    dx[...] = jnp.zeros((ALL, D), F32)
    for kind in range(2):
        for image in range(IMG):
            row = image * ROWS + NPATCH + kind
            dx[row : row + 1, :] = dtop[kind * IMG + image : kind * IMG + image + 1, :]
    grad_norm[...] = jnp.zeros((16, D), F32)

    def layer(step, carry):
        depth = L - 1 - step
        slot = lax.rem(step, 2)
        for copy in fetch(depth, slot):
            copy.wait()

        @pl.when(step < L - 1)
        def _():
            for copy in fetch(depth - 1, 1 - slot):
                copy.start()

        low[...] = dx[...].astype(BF16)
        dy[...] = jnp.zeros((ALL, D), F32)

        def block(m, carry):
            grad_gelu = nn(low[...], mlp_w[depth, 1, m].reshape(D, D))
            grad_hidden = (grad_gelu * slope[slot, m].astype(F32)).astype(BF16)
            grad_mlp[depth, 0, m] = tn(a2[slot], grad_hidden).astype(BF16)
            grad_mlp[depth, 1, m] = tn(low[...], z[slot, m]).astype(BF16)
            dy[...] += nt(grad_hidden, mlp_w[depth, 0, m].reshape(D, D))
            return carry

        lax.fori_loop(0, BLOCKS, block, 0)
        grad_in, gain, shift = norm_backward(dy[...], x1[slot], norms[pl.ds(4 * depth + 2, 1), :])
        grad_norm[pl.ds(4 * depth + 2, 1), :] = gain
        grad_norm[pl.ds(4 * depth + 3, 1), :] = shift
        dx[...] += grad_in
        low[...] = dx[...].astype(BF16)
        attn = attn_w.at[depth]
        grad_attn[depth, 3 * D :] = tn(low[...], o[slot]).astype(BF16)
        dout[...] = nn(low[...], attn[6:8].reshape(D, D)).astype(BF16)
        for image in range(IMG):
            for pair in range(3):
                attend_backward(qkv.at[slot], dout, dqkv, image, pair)
        total = None
        for n in range(3):
            part = dqkv[:, D * n : D * n + D]
            grad_attn[depth, D * n : D * n + D] = tn(part, a[slot]).astype(BF16)
            term = nn(part, attn[2 * n : 2 * n + 2].reshape(D, D))
            total = term if total is None else total + term
        grad_in, gain, shift = norm_backward(total, x[slot], norms[pl.ds(4 * depth, 1), :])
        grad_norm[pl.ds(4 * depth, 1), :] = gain
        grad_norm[pl.ds(4 * depth + 1, 1), :] = shift
        dx[...] += grad_in
        return carry

    lax.fori_loop(0, L, layer, 0)
    grad_pos[...] = dx[0:ROWS] + dx[ROWS : 2 * ROWS] + dx[2 * ROWS :]
    grad_patch[...] = tn(mixed[...], dx[...].astype(BF16)).astype(BF16)


def backward(*operands):
    outs = (
        ((PATCH_DIM, D), BF16),
        ((L, 4 * D, D), BF16),
        ((L, 2, BLOCKS, D, D), BF16),
        ((16, D), F32),
        ((ROWS, D), F32),
    )
    scratch = [((ALL, D), F32), ((ALL, D), F32), ((ALL, D), BF16), ((ALL, D), BF16), ((ALL, 3 * D), BF16)]
    scratch += [((2,) + shape[1:], kind) for shape, kind in SAVED[1:]]
    return pl.pallas_call(
        backward_kernel,
        out_shape=[jax.ShapeDtypeStruct(*entry) for entry in outs],
        in_specs=[VMEM] * 5 + [HBM] * 8,
        out_specs=[VMEM] * len(outs),
        scratch_shapes=[pltpu.VMEM(*entry) for entry in scratch] + [pltpu.SemaphoreType.DMA((2, 8))],
        compiler_params=pltpu.CompilerParams(vmem_limit_bytes=62 * 2**20),
        name="backward",
    )(*operands)


def adam_update(weight, first_moment, second, grad_in, factor, step_rate):
    clipped = grad_in * factor
    first_moment = BETA_ONE * first_moment + (1.0 - BETA_ONE) * clipped
    second = BETA_TWO * second + (1.0 - BETA_TWO) * clipped * clipped
    adam_move = (
        first_moment
        / (1.0 - BETA_ONE**ADAM_STEP)
        / (jnp.sqrt(second / (1.0 - BETA_TWO**ADAM_STEP)) + ADAM_EPS)
    )
    return (weight - step_rate * (adam_move + DECAY * weight), first_moment, second)


def per_device(
    patches, partners, mix_weight, labels, teacher_logits,
    patch_weight, attn_weight, mlp_weight, positions, head_weight, norm_params,
    patch_first, attn_first, mlp_first, pos_first, head_first, norm_first,
    patch_second, attn_second, mlp_second, pos_second, head_second, norm_second,
):
    axes = ("dp", "mp")
    image_count = patches.shape[0] * lax.axis_size("dp") * lax.axis_size("mp")
    attn_t = jnp.swapaxes(attn_weight.astype(BF16), 1, 2)
    patch_low = lax.all_gather(patch_weight.astype(BF16), axes, axis=0, tiled=True)
    attn_low = lax.all_gather(attn_t, axes, axis=1, tiled=True)
    mlp_low = lax.all_gather(mlp_weight.astype(BF16), "dp", axis=2, tiled=True)
    mlp_low = lax.all_gather(mlp_low, "mp", axis=2, tiled=False)
    positions_last = jnp.concatenate(
        [positions[2:], positions[:2], jnp.zeros((ROWS - TOK, D), F32)], axis=0
    )
    attn_low = attn_low.reshape(L, 8, 4, 48, D)
    mlp_low = mlp_low.reshape(L, 2, BLOCKS, 8, 48, D)
    results = forward(
        image_count, partners, mix_weight, labels, patches, teacher_logits, positions_last,
        head_weight, norm_params, patch_low, attn_low, mlp_low,
    )
    saved, (loss, feature, dlogits, dtop, dnorm) = results[: len(SAVED)], results[len(SAVED) :]
    features = lax.all_gather(feature.astype(BF16), axes, axis=0, tiled=True)
    all_dlogits = lax.all_gather(dlogits.astype(BF16), axes, axis=0, tiled=True)
    head_sum = tn(features, all_dlogits)
    grad_patch, grad_attn, grad_mlp, grad_norm, grad_pos = backward(
        dtop, norm_params, saved[0], attn_low, mlp_low, *saved[1:]
    )
    patch_share = lax.psum_scatter(grad_patch.astype(F32), axes, scatter_dimension=0, tiled=True)
    attn_share = lax.psum_scatter(grad_attn.astype(F32), axes, scatter_dimension=1, tiled=True)
    mlp_share = lax.psum_scatter(grad_mlp.astype(F32), "mp", scatter_dimension=2, tiled=True)
    mlp_share = lax.psum_scatter(mlp_share, "dp", scatter_dimension=3, tiled=True)
    attn_share = jnp.swapaxes(attn_share, 1, 2)
    mlp_share = mlp_share.reshape(mlp_weight.shape)
    grad_norms = jnp.concatenate([grad_norm[: 4 * L], dnorm[:2]], axis=0)
    pos_sum, norm_sum, loss_sum = lax.psum(
        (jnp.concatenate([grad_pos[NPATCH:TOK], grad_pos[:NPATCH]], axis=0), grad_norms, loss[0, 0]), axes
    )
    own_squares = (
        jnp.sum(patch_share * patch_share)
        + jnp.sum(attn_share * attn_share)
        + jnp.sum(mlp_share * mlp_share)
    )
    shared = jnp.sum(pos_sum * pos_sum) + jnp.sum(head_sum * head_sum) + jnp.sum(norm_sum * norm_sum)
    global_norm = jnp.sqrt(lax.psum(own_squares, axes) + shared)
    factor = jnp.minimum(1.0, MAX_NORM / global_norm)
    weights = (patch_weight, attn_weight, mlp_weight, positions, head_weight, norm_params)
    firsts = (patch_first, attn_first, mlp_first, pos_first, head_first, norm_first)
    seconds = (patch_second, attn_second, mlp_second, pos_second, head_second, norm_second)
    grads = (patch_share, attn_share, mlp_share, pos_sum, head_sum, norm_sum)
    updated = [
        adam_update(weights[n], firsts[n], seconds[n], grads[n], factor, STEP_RATES[n]) for n in range(6)
    ]
    return (loss_sum, global_norm, *(entry[kind] for kind in range(3) for entry in updated))


def solution(mesh):
    images = (P(("dp", "mp"), None, None), P(("dp", "mp")), P(("dp", "mp")), P(("dp", "mp")), P(("dp", "mp"), None))
    weights = (P(("dp", "mp"), None), P(None, None, ("dp", "mp")), P(None, None, "dp", "mp"), P(), P(), P())
    return jax.shard_map(
        per_device,
        mesh=mesh,
        in_specs=images + weights * 3,
        out_specs=(P(), P()) + weights * 3,
        check_vma=False,
    )
```

```python
import jax
import jax.numpy as jnp
from jax import lax
from jax.experimental import pallas as pl
from jax.experimental.pallas import tpu as pltpu
from jax.sharding import PartitionSpec as P

D = 384
C = 1000
PATCH_DIM = 768
NPATCH = 196
L = 3
TOK = 198
IMG = 3
ROWS = 208
ALL = IMG * ROWS
BLOCKS = 4

Z = 4
Y = 2
X = 2
CORES = 2
EVERY = slice(0, 2)
PIECES = 11

LN_EPS = 1e-06
TEMPER = 3.0
MAX_NORM = 0.02
BETA_ONE = 0.9
BETA_TWO = 0.999
STEP_RATES = (0.05, 0.05, 0.05, 0.4, 0.12, 0.5)
DECAY = 0.05
ADAM_EPS = 1e-08
ADAM_STEP = 10.0
LOWEST = -1e30

BF16 = jnp.bfloat16
F32 = jnp.float32
VMEM = pl.BlockSpec(memory_space=pltpu.VMEM)
SMEM = pl.BlockSpec(memory_space=pltpu.SMEM)
HBM = pl.BlockSpec(memory_space=pl.ANY)
MESH = pl.DeviceIdType.MESH


def nn(left, right):
    return jnp.dot(left, right, preferred_element_type=F32)


def nt(left, right):
    return lax.dot_general(left, right, (((1,), (1,)), ((), ())), preferred_element_type=F32)


def tn(left, right):
    return lax.dot_general(left, right, (((0,), (0,)), ((), ())), preferred_element_type=F32)


def unit_norm(inputs):
    centred = inputs - jnp.mean(inputs, axis=-1, keepdims=True)
    inverse = lax.rsqrt(jnp.mean(centred * centred, axis=-1, keepdims=True) + LN_EPS)
    return centred * inverse, inverse


def norm_backward(grad_out, inputs, gain):
    normed, inverse = unit_norm(inputs)
    grad_gain = jnp.sum(grad_out * normed, axis=0, keepdims=True)
    grad_shift = jnp.sum(grad_out, axis=0, keepdims=True)
    scaled = grad_out * gain
    grad_in = inverse * (
        scaled
        - jnp.mean(scaled, axis=-1, keepdims=True)
        - normed * jnp.mean(scaled * normed, axis=-1, keepdims=True)
    )
    return grad_in, grad_gain, grad_shift


class Place:
    def __init__(self):
        dp, mp = lax.axis_index("dp"), lax.axis_index("mp")
        self.z, self.y = dp // Y, dp % Y
        self.x, self.core = mp // CORES, mp % CORES

    def at(self, dz=0, dy=0, dx=0, dcore=0):
        z = lax.rem(self.z + dz, Z)
        y = 1 - self.y if dy else self.y
        x = 1 - self.x if dx else self.x
        core = 1 - self.core if dcore else self.core
        return {"dp": z * Y + y, "mp": x * CORES + core}

    def partners(self):
        column = [self.at(dz=step) for step in range(1, Z)]
        return column + [self.at(dx=1), self.at(dy=1), self.at(dcore=1), self.at(dy=1, dx=1)]


def greet(partners):
    barrier = pltpu.get_barrier_semaphore()
    for partner in partners:
        pl.semaphore_signal(barrier, inc=1, device_id=partner, device_id_type=MESH)
    pl.semaphore_wait(barrier, len(partners))


class Gather:
    def __init__(self, place, pieces, planes, send_sems, recv_sems):
        self.place, self.pieces, self.planes = place, pieces, planes
        self.send_sems, self.recv_sems = send_sems, recv_sems
        self.started = []
        self.done = set()

    def copy(self, piece, n, region, target):
        view = self.pieces[piece](*region)
        return pltpu.make_async_remote_copy(
            src_ref=view,
            dst_ref=view,
            send_sem=self.send_sems.at[piece, n],
            recv_sem=self.recv_sems.at[piece, n],
            device_id=target,
            device_id_type=MESH,
        )

    def send(self, piece, n, region, **offset):
        copy = self.copy(piece, n, region, self.place.at(**offset))
        copy.start()
        self.started.append(copy)

    def recv(self, piece, n, region):
        self.copy(piece, n, region, self.place.at(dcore=1)).wait_recv()

    def step(self, piece, stage):
        if (piece, stage) in self.done:
            return
        self.done.add((piece, stage))
        z, y, x, core = self.place.z, self.place.y, self.place.x, self.place.core
        far_y, far_x, sibling = 1 - y, 1 - x, 1 - core
        column, low, high = slice(0, Z), slice(0, Z // 2), slice(Z // 2, Z)
        if piece in self.planes:
            if stage == 1:
                self.send(piece, 3, (z, y, x, core), dx=1)
                self.send(piece, 4, (z, y, x, core), dy=1)
                self.send(piece, 6, (z, y, x, core), dy=1, dx=1)
            if stage == 2:
                self.recv(piece, 3, (z, y, far_x, core))
                self.recv(piece, 4, (z, far_y, x, core))
                self.recv(piece, 6, (z, far_y, far_x, core))
                for hop in range(1, Z):
                    self.send(piece, hop - 1, (z, EVERY, EVERY, core), dz=hop)
            if stage == 4:
                for hop in range(1, Z):
                    self.recv(piece, hop - 1, (lax.rem(z + Z - hop, Z), EVERY, EVERY, core))
                self.send(piece, 5, (column, EVERY, EVERY, core), dcore=1)
            if stage == 5:
                self.recv(piece, 5, (column, EVERY, EVERY, sibling))
            return
        if stage == 1:
            for hop in range(1, Z):
                self.send(piece, hop - 1, (z, y, x, core), dz=hop)
        if stage == 2:
            for hop in range(1, Z):
                self.recv(piece, hop - 1, (lax.rem(z + Z - hop, Z), y, x, core))
            self.send(piece, 3, (column, y, x, core), dx=1)
            self.send(piece, 4, (column, y, x, core), dy=1)
            self.send(piece, 5, (column, y, x, core), dcore=1)
        if stage == 3:
            self.recv(piece, 3, (column, y, far_x, core))
            self.send(piece, 6, (low, y, far_x, core), dy=1)
            self.send(piece, 8, (column, y, far_x, core), dcore=1)
            self.recv(piece, 4, (column, far_y, x, core))
            self.send(piece, 7, (high, far_y, x, core), dx=1)
            self.send(piece, 9, (column, far_y, x, core), dcore=1)
        if stage == 4:
            self.recv(piece, 6, (low, far_y, far_x, core))
            self.recv(piece, 7, (high, far_y, far_x, core))
            self.send(piece, 10, (column, far_y, far_x, core), dcore=1)
        if stage == 5:
            self.recv(piece, 5, (column, y, x, sibling))
            self.recv(piece, 8, (column, y, far_x, sibling))
            self.recv(piece, 9, (column, far_y, x, sibling))
            self.recv(piece, 10, (column, far_y, far_x, sibling))

    def finish(self):
        for copy in self.started:
            copy.wait_send()


def head_lanes(shape, head):
    lane = lax.broadcasted_iota(jnp.int32, shape, len(shape) - 1)
    return lane < 64 if head == 0 else lane >= 64


def attend(qkv, out, image, pair):
    rows = slice(image * ROWS, (image + 1) * ROWS)
    lanes = 128 * pair
    queries = qkv[rows, lanes : lanes + 128] * BF16(0.125)
    keys = qkv[rows, D + lanes : D + lanes + 128]
    values = qkv[rows, 2 * D + lanes : 2 * D + lanes + 128]
    key_lane = lax.broadcasted_iota(jnp.int32, (1, ROWS), 1)
    parts = []
    for head in range(2):
        scores = nt(jnp.where(head_lanes((ROWS, 128), head), queries, BF16(0)), keys)
        scores = jnp.where(key_lane < TOK, scores, LOWEST)
        weights = jnp.exp(scores - jnp.max(scores, axis=-1, keepdims=True))
        inverse = 1.0 / jnp.sum(weights, axis=-1, keepdims=True)
        parts.append(nn(weights.astype(BF16), values) * inverse)
    out[rows, lanes : lanes + 128] = jnp.where(
        head_lanes((ROWS, 128), 0), parts[0], parts[1]
    ).astype(BF16)


def attend_backward(qkv, grad_out, grad_qkv, image, pair):
    rows = slice(image * ROWS, (image + 1) * ROWS)
    lanes = 128 * pair
    queries = qkv[rows, lanes : lanes + 128] * BF16(0.125)
    keys = qkv[rows, D + lanes : D + lanes + 128]
    values = qkv[rows, 2 * D + lanes : 2 * D + lanes + 128]
    grad = grad_out[rows, lanes : lanes + 128]
    key_row = lax.broadcasted_iota(jnp.int32, (ROWS, 1), 0)
    grad_q, grad_k, grad_v = [], [], []
    for head in range(2):
        own = head_lanes((ROWS, 128), head)
        scores = nt(jnp.where(own, keys, BF16(0)), queries)
        scores = jnp.where(key_row < TOK, scores, LOWEST)
        probs = jnp.exp(scores - jnp.max(scores, axis=0, keepdims=True))
        probs = probs * (1.0 / jnp.sum(probs, axis=0, keepdims=True))
        grad_probs = nt(jnp.where(own, values, BF16(0)), grad)
        total = jnp.sum(probs * grad_probs, axis=0, keepdims=True)
        grad_scores = (probs * (grad_probs - total)).astype(BF16)
        grad_v.append(nn(probs.astype(BF16), grad))
        grad_k.append(nn(grad_scores, queries))
        grad_q.append(tn(grad_scores, keys))
    first = head_lanes((ROWS, 128), 0)
    grad_qkv[rows, lanes : lanes + 128] = (
        jnp.where(first, grad_q[0], grad_q[1]) * 0.125
    ).astype(BF16)
    grad_qkv[rows, D + lanes : D + lanes + 128] = jnp.where(first, grad_k[0], grad_k[1]).astype(
        BF16
    )
    grad_qkv[rows, 2 * D + lanes : 2 * D + lanes + 128] = jnp.where(
        first, grad_v[0], grad_v[1]
    ).astype(BF16)


def mix_images(partners, mix, patches, mixed):
    for image in range(IMG):
        total = None
        for other in range(IMG):
            share = jnp.where(partners[image] == other, 1.0 - mix[image], 0.0)
            if image == other:
                share = share + mix[image]
            term = share * patches[other].astype(F32)
            total = term if total is None else total + term
        padding = jnp.zeros((ROWS - NPATCH, PATCH_DIM), F32)
        mixed[image * ROWS : (image + 1) * ROWS, :] = jnp.concatenate(
            [total, padding], axis=0
        ).astype(BF16)


def head_and_loss(
    image_count, stream, norms, partners, mix, labels, teacher, head, loss, feature, dlogits, dtop, dnorm
):
    picked = [
        stream[image * ROWS + NPATCH + kind : image * ROWS + NPATCH + kind + 1, :]
        for kind in range(2)
        for image in range(IMG)
    ]
    top = jnp.concatenate(picked + [jnp.zeros((2, D), F32)], axis=0)
    gain = norms[4 * L : 4 * L + 1, :]
    normed, _ = unit_norm(top)
    features = (normed * gain + norms[4 * L + 1 : 4 * L + 2, :]).astype(BF16)
    weights = head[...].astype(BF16)
    row = lax.broadcasted_iota(jnp.int32, (8, 2 * C), 0)
    lane = lax.broadcasted_iota(jnp.int32, (8, 2 * C), 1)
    is_class = row < IMG
    low_lane = jnp.where(is_class, 0, C)
    high_lane = jnp.where(is_class, C, jnp.where(row < 2 * IMG, 2 * C, 0))
    used = (lane >= low_lane) & (lane < high_lane)

    def log_softmax(values):
        values = jnp.where(used, values, LOWEST)
        shifted = values - jnp.max(values, axis=-1, keepdims=True)
        return shifted - jnp.log(jnp.sum(jnp.exp(shifted), axis=-1, keepdims=True))

    taught = jnp.concatenate([jnp.zeros((IMG, C), F32), teacher[...]], axis=1)
    taught = jnp.concatenate(
        [jnp.zeros((IMG, 2 * C), F32), taught, jnp.zeros((8 - 2 * IMG, 2 * C), F32)], axis=0
    )
    logits = nt(features, weights)
    student_log = log_softmax(jnp.where(is_class, logits, logits / TEMPER))
    teacher_log = log_softmax(taught / TEMPER)
    teacher_prob = jnp.exp(teacher_log)
    target = jnp.zeros((8, 2 * C), F32)
    for image in range(IMG):
        partner_label = labels[IMG - 1]
        for other in range(IMG - 1):
            partner_label = jnp.where(partners[image] == other, labels[other], partner_label)
        ours = jnp.where(lane == labels[image], mix[image], 0.0) + jnp.where(
            lane == partner_label, 1.0 - mix[image], 0.0
        )
        target = target + jnp.where(row == image, ours, 0.0)
    terms = jnp.where(
        is_class,
        -0.5 * target * student_log,
        0.5 * TEMPER * TEMPER * teacher_prob * (teacher_log - student_log),
    )
    terms = jnp.where(used, terms, 0.0)
    loss[...] = jnp.broadcast_to(jnp.sum(terms, axis=(0, 1), keepdims=True), (8, 128))
    wanted = jnp.where(is_class, target, teacher_prob)
    scale = jnp.where(is_class, 0.5 / image_count, 0.5 * TEMPER / image_count)
    grad_logits = (scale * jnp.where(used, jnp.exp(student_log) - wanted, 0.0)).astype(BF16)
    feature[...] = features.astype(F32)
    dlogits[...] = grad_logits.astype(F32)
    grad_top, grad_gain, grad_shift = norm_backward(nn(grad_logits, weights), top, gain)
    dtop[...] = grad_top
    dnorm[...] = jnp.concatenate([grad_gain, grad_shift, jnp.zeros((6, D), F32)], axis=0)


ATTN_SHAPE = (L, Z, Y, X, CORES, 48, D)
MLP_SHAPE = (L, 2, X, CORES, Z, Y, 48, D)
PATCH_SHAPE = (Z, Y, X, CORES, 32, D)
N_PIECES = 1 + 3 * L
PLANES = (1 + 3 * (L - 1),)
QUEUE = tuple(n for n in range(N_PIECES) if n not in PLANES)


def gather_views(patch_w, attn_w, mlp_w):
    def attn(depth):
        return lambda z, y, x, core: attn_w.at[depth, z, y, x, core]

    def mlp(depth, part):
        return lambda z, y, x, core: mlp_w.at[depth, part, x, core, z, y]

    views = [lambda z, y, x, core: patch_w.at[z, y, x, core]]
    for depth in range(L):
        views += [attn(depth), mlp(depth, 0), mlp(depth, 1)]
    return views


def forward_kernel(image_count, sharded, *refs):
    (
        partners, mix, labels, patches_h, teacher, pos, head_h, norms, patch_in, attn_in, mlp_in,
        mixed_h, x_h, a_h, qkv_h, o_h, x1_h, a2_h, z_h, slope_h, attn_h, mlp_h,
        loss, feature, dlogits, dtop, dnorm,
        mixed, x, a, qkv, o, x1, a2, z, slope, attn_w, mlp_w,
        patches, head, stream, patch_w, in_sems, out_sems, *rest,
    ) = refs
    outgoing = []

    def keep(source, target):
        copy = pltpu.make_async_copy(source, target, out_sems.at[len(outgoing)])
        copy.start()
        outgoing.append(copy)

    if sharded:
        patch_all, patch_s, attn_s, mlp_s, send_sems, recv_sems = rest
        loads = [(attn_in, attn_s), (mlp_in, mlp_s), (patch_in, patch_s)]
    else:
        loads = [(attn_in, attn_w), (mlp_in, mlp_w), (patch_in, patch_w)]
    loads += [(patches_h, patches), (head_h, head)]
    loads = [
        pltpu.make_async_copy(source, target, in_sems.at[n]) for n, (source, target) in enumerate(loads)
    ]
    for copy in loads:
        copy.start()

    if sharded:
        place = Place()
        gather = Gather(place, gather_views(patch_all, attn_w, mlp_w), PLANES, send_sems, recv_sems)
        mine = (place.z, place.y, place.x, place.core)
        loads[2].wait()
        patch_all[mine] = jnp.concatenate([patch_s[...], jnp.zeros((8, D), F32)], axis=0).astype(BF16)
        loads[0].wait()
        for depth in range(L):
            attn_w[(depth,) + mine] = attn_s[depth].astype(BF16)
        loads[1].wait()
        for depth in range(L):
            for part in range(2):
                mlp_w[depth, part, place.x, place.core, place.z, place.y] = mlp_s[depth, part].astype(BF16)
        greet(place.partners())
        for piece in PLANES + QUEUE:
            gather.step(piece, 1)

    def ahead(n, stage):
        if sharded and n < len(QUEUE):
            gather.step(QUEUE[n], stage)

    def need(piece):
        if not sharded:
            return
        if piece in PLANES:
            for stage in (4, 5):
                gather.step(piece, stage)
            return
        n = QUEUE.index(piece)
        ahead(n + 1, 2)
        ahead(n, 3)
        ahead(n + 2, 2)
        ahead(n + 1, 3)
        ahead(n, 4)
        ahead(n, 5)

    def between(piece):
        if not sharded:
            return
        later = [n for n in range(len(QUEUE)) if QUEUE[n] > piece]
        if later:
            ahead(later[0] + 2, 2)
            ahead(later[0] + 1, 3)

    if sharded:
        ahead(0, 2)
        for piece in PLANES:
            gather.step(piece, 2)
        ahead(1, 2)
        ahead(0, 3)
    else:
        for n in range(3):
            loads[n].wait()
    loads[3].wait()
    mix_images(partners, mix, patches, mixed)
    keep(mixed, mixed_h)
    need(0)
    if sharded:
        for n in range(Z * Y * X):
            block = patch_all[n // 4, n // 2 % 2, n % 2].astype(F32)
            patch_w[48 * n : 48 * n + 48, :] = jnp.concatenate([block[0, :24], block[1, :24]], axis=0).astype(BF16)
    embedded = nn(mixed[...], patch_w[...])
    added = jnp.concatenate([pos[2:TOK, :], pos[0:2, :], jnp.zeros((ROWS - TOK, D), F32)], axis=0)
    for image in range(IMG):
        rows = slice(image * ROWS, (image + 1) * ROWS)
        x[0, rows, :] = embedded[rows] + added
    for depth in range(L):
        norm = [norms[4 * depth + n : 4 * depth + n + 1, :] for n in range(4)]
        first = 1 + 3 * depth
        keep(x.at[depth], x_h.at[depth])
        a[depth] = (unit_norm(x[depth])[0] * norm[0] + norm[1]).astype(BF16)
        keep(a.at[depth], a_h.at[depth])
        need(first)
        for n in range(3):
            qkv[depth, :, D * n : D * n + D] = nt(a[depth], attn_w[depth, n].reshape(D, D)).astype(BF16)
        keep(qkv.at[depth], qkv_h.at[depth])
        keep(attn_w.at[depth], attn_h.at[depth])
        for image in range(IMG):
            for pair in range(3):
                attend(qkv.at[depth], o.at[depth], image, pair)
            if image == 1:
                between(first)
        keep(o.at[depth], o_h.at[depth])
        x1[depth] = x[depth] + nt(o[depth], attn_w[depth, 3].reshape(D, D))
        keep(x1.at[depth], x1_h.at[depth])
        a2[depth] = (unit_norm(x1[depth])[0] * norm[2] + norm[3]).astype(BF16)
        keep(a2.at[depth], a2_h.at[depth])
        need(first + 1)

        def widen(m, carry):
            hidden = nn(a2[depth], mlp_w[depth, 0, m // 2, lax.rem(m, 2)].reshape(D, D))
            phi = 0.5 * (1.0 + lax.erf(hidden * 2.0**-0.5))
            z[depth, m] = (hidden * phi).astype(BF16)
            density = jnp.exp(-0.5 * hidden * hidden) * 0.3989422804014327
            slope[depth, m] = (phi + hidden * density).astype(BF16)
            return carry

        lax.fori_loop(0, BLOCKS, widen, 0)
        keep(z.at[depth], z_h.at[depth])
        keep(slope.at[depth], slope_h.at[depth])
        need(first + 2)
        keep(mlp_w.at[depth], mlp_h.at[depth])
        total = x1[depth]
        for m in range(BLOCKS):
            total = total + nt(z[depth, m], mlp_w[depth, 1, m // 2, m % 2].reshape(D, D))
        if depth + 1 < L:
            x[depth + 1] = total
        else:
            stream[...] = total
    loads[4].wait()
    head_and_loss(
        image_count, stream, norms, partners, mix, labels, teacher, head, loss, feature, dlogits, dtop, dnorm
    )
    for copy in outgoing:
        copy.wait()
    if sharded:
        gather.finish()


SAVED = (
    ((ALL, PATCH_DIM), BF16),
    ((L, ALL, D), F32),
    ((L, ALL, D), BF16),
    ((L, ALL, 3 * D), BF16),
    ((L, ALL, D), BF16),
    ((L, ALL, D), F32),
    ((L, ALL, D), BF16),
    ((L, BLOCKS, ALL, D), BF16),
    ((L, BLOCKS, ALL, D), BF16),
    (ATTN_SHAPE, BF16),
    (MLP_SHAPE, BF16),
)
SMALL = (((8, 128), F32), ((8, D), F32), ((8, 2 * C), F32), ((8, D), F32), ((8, D), F32))


def forward(image_count, sharded, *operands):
    scratch = SAVED + (
        ((IMG, NPATCH, PATCH_DIM), BF16),
        ((2 * C, D), F32),
        ((ALL, D), F32),
        ((PATCH_DIM, D), BF16),
    )
    scratch = [pltpu.VMEM(*entry) for entry in scratch]
    scratch += [pltpu.SemaphoreType.DMA((5,)), pltpu.SemaphoreType.DMA((1 + 10 * L,))]
    if sharded:
        scratch += [
            pltpu.VMEM(PATCH_SHAPE, BF16),
            pltpu.VMEM((PATCH_DIM // (Z * Y * X * CORES), D), F32),
            pltpu.VMEM((L, 48, D), F32),
            pltpu.VMEM((L, 2, 48, D), F32),
            pltpu.SemaphoreType.DMA((N_PIECES, PIECES)),
            pltpu.SemaphoreType.DMA((N_PIECES, PIECES)),
        ]
    params = dict(collective_id=0, has_side_effects=True) if sharded else {}
    return pl.pallas_call(
        lambda *refs: forward_kernel(image_count, sharded, *refs),
        out_shape=[jax.ShapeDtypeStruct(*entry) for entry in SAVED + SMALL],
        in_specs=[SMEM] * 3 + [HBM, VMEM, VMEM, HBM, VMEM] + [HBM] * 3,
        out_specs=[HBM] * len(SAVED) + [VMEM] * len(SMALL),
        scratch_shapes=scratch,
        compiler_params=pltpu.CompilerParams(vmem_limit_bytes=62 * 2**20, **params),
        name="forward",
    )(*operands)


def backward_kernel(
    dtop, norms, mixed, attn_w, mlp_w, x_h, a_h, qkv_h, o_h, x1_h, a2_h, z_h, slope_h,
    grad_patch, grad_attn, grad_mlp, grad_norm, grad_pos,
    dx, dy, low, dout, dqkv, x, a, qkv, o, x1, a2, z, slope, sems,
):
    saved = [(x_h, x), (a_h, a), (qkv_h, qkv), (o_h, o), (x1_h, x1), (a2_h, a2), (z_h, z), (slope_h, slope)]

    def fetch(depth, slot):
        return [
            pltpu.make_async_copy(source.at[depth], target.at[slot], sems.at[slot, n])
            for n, (source, target) in enumerate(saved)
        ]

    for copy in fetch(L - 1, 0):
        copy.start()
    dx[...] = jnp.zeros((ALL, D), F32)
    for kind in range(2):
        for image in range(IMG):
            row = image * ROWS + NPATCH + kind
            dx[row : row + 1, :] = dtop[kind * IMG + image : kind * IMG + image + 1, :]
    grad_norm[...] = jnp.zeros((16, D), F32)

    def layer(step, carry):
        depth = L - 1 - step
        slot = lax.rem(step, 2)
        for copy in fetch(depth, slot):
            copy.wait()

        @pl.when(step < L - 1)
        def _():
            for copy in fetch(depth - 1, 1 - slot):
                copy.start()

        low[...] = dx[...].astype(BF16)
        dy[...] = jnp.zeros((ALL, D), F32)

        def block(m, carry):
            grad_gelu = nn(low[...], mlp_w[depth, 1, m // 2, lax.rem(m, 2)].reshape(D, D))
            grad_hidden = (grad_gelu * slope[slot, m].astype(F32)).astype(BF16)
            grad_mlp[depth, 0, m] = tn(a2[slot], grad_hidden).astype(BF16)
            grad_mlp[depth, 1, m] = tn(low[...], z[slot, m]).astype(BF16)
            dy[...] += nt(grad_hidden, mlp_w[depth, 0, m // 2, lax.rem(m, 2)].reshape(D, D))
            return carry

        lax.fori_loop(0, BLOCKS, block, 0)
        grad_in, gain, shift = norm_backward(dy[...], x1[slot], norms[pl.ds(4 * depth + 2, 1), :])
        grad_norm[pl.ds(4 * depth + 2, 1), :] = gain
        grad_norm[pl.ds(4 * depth + 3, 1), :] = shift
        dx[...] += grad_in
        low[...] = dx[...].astype(BF16)
        attn = attn_w.at[depth]
        grad_attn[depth, 3 * D :] = tn(low[...], o[slot]).astype(BF16)
        dout[...] = nn(low[...], attn[3].reshape(D, D)).astype(BF16)
        for image in range(IMG):
            for pair in range(3):
                attend_backward(qkv.at[slot], dout, dqkv, image, pair)
        total = None
        for n in range(3):
            part = dqkv[:, D * n : D * n + D]
            grad_attn[depth, D * n : D * n + D] = tn(part, a[slot]).astype(BF16)
            term = nn(part, attn[n].reshape(D, D))
            total = term if total is None else total + term
        grad_in, gain, shift = norm_backward(total, x[slot], norms[pl.ds(4 * depth, 1), :])
        grad_norm[pl.ds(4 * depth, 1), :] = gain
        grad_norm[pl.ds(4 * depth + 1, 1), :] = shift
        dx[...] += grad_in
        return carry

    lax.fori_loop(0, L, layer, 0)
    grad_pos[...] = dx[0:ROWS] + dx[ROWS : 2 * ROWS] + dx[2 * ROWS :]
    grad_patch[...] = tn(mixed[...], dx[...].astype(BF16)).astype(BF16)


def backward(*operands):
    outs = (
        ((PATCH_DIM, D), BF16),
        ((L, 4 * D, D), BF16),
        ((L, 2, BLOCKS, D, D), BF16),
        ((16, D), F32),
        ((ROWS, D), F32),
    )
    scratch = [((ALL, D), F32), ((ALL, D), F32), ((ALL, D), BF16), ((ALL, D), BF16), ((ALL, 3 * D), BF16)]
    scratch += [((2,) + shape[1:], kind) for shape, kind in SAVED[1:9]]
    return pl.pallas_call(
        backward_kernel,
        out_shape=[jax.ShapeDtypeStruct(*entry) for entry in outs],
        in_specs=[VMEM] * 5 + [HBM] * 8,
        out_specs=[VMEM] * len(outs),
        scratch_shapes=[pltpu.VMEM(*entry) for entry in scratch] + [pltpu.SemaphoreType.DMA((2, 8))],
        compiler_params=pltpu.CompilerParams(vmem_limit_bytes=62 * 2**20),
        name="backward",
    )(*operands)


def adam_update(weight, first_moment, second, grad_in, factor, step_rate):
    clipped = grad_in * factor
    first_moment = BETA_ONE * first_moment + (1.0 - BETA_ONE) * clipped
    second = BETA_TWO * second + (1.0 - BETA_TWO) * clipped * clipped
    adam_move = (
        first_moment
        / (1.0 - BETA_ONE**ADAM_STEP)
        / (jnp.sqrt(second / (1.0 - BETA_TWO**ADAM_STEP)) + ADAM_EPS)
    )
    return (weight - step_rate * (adam_move + DECAY * weight), first_moment, second)


def per_device(
    patches, partners, mix_weight, labels, teacher_logits,
    patch_weight, attn_weight, mlp_weight, positions, head_weight, norm_params,
    patch_first, attn_first, mlp_first, pos_first, head_first, norm_first,
    patch_second, attn_second, mlp_second, pos_second, head_second, norm_second,
):
    axes = ("dp", "mp")
    image_count = patches.shape[0] * lax.axis_size("dp") * lax.axis_size("mp")
    sharded = (lax.axis_size("dp"), lax.axis_size("mp")) == (Z * Y, X * CORES)
    attn_t = jnp.swapaxes(attn_weight, 1, 2)
    if sharded:
        weights_in = (patch_weight, attn_t, mlp_weight)
    else:
        patch_low = lax.all_gather(patch_weight.astype(BF16), axes, axis=0, tiled=True)
        attn_low = lax.all_gather(attn_t.astype(BF16), axes, axis=1, tiled=True)
        mlp_low = lax.all_gather(mlp_weight.astype(BF16), "dp", axis=2, tiled=True)
        mlp_low = lax.all_gather(mlp_low, "mp", axis=2, tiled=False)
        weights_in = (patch_low, attn_low.reshape(ATTN_SHAPE), mlp_low.reshape(MLP_SHAPE))
    results = forward(
        image_count, sharded, partners, mix_weight, labels, patches, teacher_logits, positions,
        head_weight.T, norm_params, *weights_in,
    )
    saved, (loss, feature, dlogits, dtop, dnorm) = results[: len(SAVED)], results[len(SAVED) :]
    features = lax.all_gather(feature.astype(BF16), axes, axis=0, tiled=True)
    all_dlogits = lax.all_gather(dlogits.astype(BF16), axes, axis=0, tiled=True)
    head_sum = tn(all_dlogits, features).T
    grad_patch, grad_attn, grad_mlp, grad_norm, grad_pos = backward(
        dtop, norm_params, saved[0], *saved[9:], *saved[1:9]
    )
    patch_share = lax.psum_scatter(grad_patch.astype(F32), axes, scatter_dimension=0, tiled=True)
    attn_share = lax.psum_scatter(grad_attn.astype(F32), axes, scatter_dimension=1, tiled=True)
    mlp_share = lax.psum_scatter(grad_mlp.astype(F32), "mp", scatter_dimension=2, tiled=True)
    mlp_share = lax.psum_scatter(mlp_share, "dp", scatter_dimension=3, tiled=True)
    attn_share = jnp.swapaxes(attn_share, 1, 2)
    mlp_share = mlp_share.reshape(mlp_weight.shape)
    grad_norms = jnp.concatenate([grad_norm[: 4 * L], dnorm[:2]], axis=0)
    pos_sum, norm_sum, loss_sum = lax.psum(
        (jnp.concatenate([grad_pos[NPATCH:TOK], grad_pos[:NPATCH]], axis=0), grad_norms, loss[0, 0]), axes
    )
    own_squares = (
        jnp.sum(patch_share * patch_share)
        + jnp.sum(attn_share * attn_share)
        + jnp.sum(mlp_share * mlp_share)
    )
    shared = jnp.sum(pos_sum * pos_sum) + jnp.sum(head_sum * head_sum) + jnp.sum(norm_sum * norm_sum)
    global_norm = jnp.sqrt(lax.psum(own_squares, axes) + shared)
    factor = jnp.minimum(1.0, MAX_NORM / global_norm)
    weights = (patch_weight, attn_weight, mlp_weight, positions, head_weight, norm_params)
    firsts = (patch_first, attn_first, mlp_first, pos_first, head_first, norm_first)
    seconds = (patch_second, attn_second, mlp_second, pos_second, head_second, norm_second)
    grads = (patch_share, attn_share, mlp_share, pos_sum, head_sum, norm_sum)
    updated = [
        adam_update(weights[n], firsts[n], seconds[n], grads[n], factor, STEP_RATES[n]) for n in range(6)
    ]
    return (loss_sum, global_norm, *(entry[kind] for kind in range(3) for entry in updated))


def solution(mesh):
    images = (P(("dp", "mp"), None, None), P(("dp", "mp")), P(("dp", "mp")), P(("dp", "mp")), P(("dp", "mp"), None))
    weights = (P(("dp", "mp"), None), P(None, None, ("dp", "mp")), P(None, None, "dp", "mp"), P(), P(), P())
    return jax.shard_map(
        per_device,
        mesh=mesh,
        in_specs=images + weights * 3,
        out_specs=(P(), P()) + weights * 3,
        check_vma=False,
    )
```

```python
import jax
import jax.numpy as jnp
from jax import lax
from jax.experimental import pallas as pl
from jax.experimental.pallas import tpu as pltpu
from jax.sharding import PartitionSpec as P

D = 384
C = 1000
PATCH_DIM = 768
NPATCH = 196
L = 3
TOK = 198
IMG = 3
ROWS = 208
ALL = IMG * ROWS
BLOCKS = 4

Z = 4
Y = 2
X = 2
CORES = 2
EVERY = slice(0, 2)
PIECES = 11

LN_EPS = 1e-06
TEMPER = 3.0
MAX_NORM = 0.02
BETA_ONE = 0.9
BETA_TWO = 0.999
STEP_RATES = (0.05, 0.05, 0.05, 0.4, 0.12, 0.5)
DECAY = 0.05
ADAM_EPS = 1e-08
ADAM_STEP = 10.0
LOWEST = -1e30

BF16 = jnp.bfloat16
F32 = jnp.float32
VMEM = pl.BlockSpec(memory_space=pltpu.VMEM)
SMEM = pl.BlockSpec(memory_space=pltpu.SMEM)
HBM = pl.BlockSpec(memory_space=pl.ANY)
MESH = pl.DeviceIdType.MESH


def nn(left, right):
    return jnp.dot(left, right, preferred_element_type=F32)


def nt(left, right):
    return lax.dot_general(left, right, (((1,), (1,)), ((), ())), preferred_element_type=F32)


def tn(left, right):
    return lax.dot_general(left, right, (((0,), (0,)), ((), ())), preferred_element_type=F32)


def unit_norm(inputs):
    centred = inputs - jnp.mean(inputs, axis=-1, keepdims=True)
    inverse = lax.rsqrt(jnp.mean(centred * centred, axis=-1, keepdims=True) + LN_EPS)
    return centred * inverse, inverse


def norm_backward(grad_out, inputs, gain):
    normed, inverse = unit_norm(inputs)
    grad_gain = jnp.sum(grad_out * normed, axis=0, keepdims=True)
    grad_shift = jnp.sum(grad_out, axis=0, keepdims=True)
    scaled = grad_out * gain
    grad_in = inverse * (
        scaled
        - jnp.mean(scaled, axis=-1, keepdims=True)
        - normed * jnp.mean(scaled * normed, axis=-1, keepdims=True)
    )
    return grad_in, grad_gain, grad_shift


class Place:
    def __init__(self):
        dp, mp = lax.axis_index("dp"), lax.axis_index("mp")
        self.z, self.y = dp // Y, dp % Y
        self.x, self.core = mp // CORES, mp % CORES

    def at(self, dz=0, dy=0, dx=0, dcore=0):
        z = lax.rem(self.z + dz, Z)
        y = 1 - self.y if dy else self.y
        x = 1 - self.x if dx else self.x
        core = 1 - self.core if dcore else self.core
        return {"dp": z * Y + y, "mp": x * CORES + core}

    def partners(self):
        column = [self.at(dz=step) for step in range(1, Z)]
        return column + [self.at(dx=1), self.at(dy=1), self.at(dcore=1), self.at(dy=1, dx=1)]


def greet(partners):
    barrier = pltpu.get_barrier_semaphore()
    for partner in partners:
        pl.semaphore_signal(barrier, inc=1, device_id=partner, device_id_type=MESH)
    pl.semaphore_wait(barrier, len(partners))


class Gather:
    def __init__(self, place, pieces, planes, send_sems, recv_sems):
        self.place, self.pieces, self.planes = place, pieces, planes
        self.send_sems, self.recv_sems = send_sems, recv_sems
        self.started = []
        self.done = set()

    def copy(self, piece, n, region, target):
        view = self.pieces[piece](*region)
        return pltpu.make_async_remote_copy(
            src_ref=view,
            dst_ref=view,
            send_sem=self.send_sems.at[piece, n],
            recv_sem=self.recv_sems.at[piece, n],
            device_id=target,
            device_id_type=MESH,
        )

    def send(self, piece, n, region, **offset):
        copy = self.copy(piece, n, region, self.place.at(**offset))
        copy.start()
        self.started.append(copy)

    def recv(self, piece, n, region):
        self.copy(piece, n, region, self.place.at(dcore=1)).wait_recv()

    def step(self, piece, stage):
        if (piece, stage) in self.done:
            return
        self.done.add((piece, stage))
        z, y, x, core = self.place.z, self.place.y, self.place.x, self.place.core
        far_y, far_x, sibling = 1 - y, 1 - x, 1 - core
        column, low, high = slice(0, Z), slice(0, Z // 2), slice(Z // 2, Z)
        if piece in self.planes:
            if stage == 1:
                self.send(piece, 3, (z, y, x, core), dx=1)
                self.send(piece, 4, (z, y, x, core), dy=1)
                self.send(piece, 6, (z, y, x, core), dy=1, dx=1)
            if stage == 2:
                self.recv(piece, 3, (z, y, far_x, core))
                self.recv(piece, 4, (z, far_y, x, core))
                self.recv(piece, 6, (z, far_y, far_x, core))
                for hop in range(1, Z):
                    self.send(piece, hop - 1, (z, EVERY, EVERY, core), dz=hop)
            if stage == 4:
                for hop in range(1, Z):
                    self.recv(piece, hop - 1, (lax.rem(z + Z - hop, Z), EVERY, EVERY, core))
                self.send(piece, 5, (column, EVERY, EVERY, core), dcore=1)
            if stage == 5:
                self.recv(piece, 5, (column, EVERY, EVERY, sibling))
            return
        if stage == 1:
            for hop in range(1, Z):
                self.send(piece, hop - 1, (z, y, x, core), dz=hop)
        if stage == 2:
            for hop in range(1, Z):
                self.recv(piece, hop - 1, (lax.rem(z + Z - hop, Z), y, x, core))
            self.send(piece, 3, (column, y, x, core), dx=1)
            self.send(piece, 4, (column, y, x, core), dy=1)
            self.send(piece, 5, (column, y, x, core), dcore=1)
        if stage == 3:
            self.recv(piece, 3, (column, y, far_x, core))
            self.send(piece, 6, (low, y, far_x, core), dy=1)
            self.send(piece, 8, (column, y, far_x, core), dcore=1)
            self.recv(piece, 4, (column, far_y, x, core))
            self.send(piece, 7, (high, far_y, x, core), dx=1)
            self.send(piece, 9, (column, far_y, x, core), dcore=1)
        if stage == 4:
            self.recv(piece, 6, (low, far_y, far_x, core))
            self.recv(piece, 7, (high, far_y, far_x, core))
            self.send(piece, 10, (column, far_y, far_x, core), dcore=1)
        if stage == 5:
            self.recv(piece, 5, (column, y, x, sibling))
            self.recv(piece, 8, (column, y, far_x, sibling))
            self.recv(piece, 9, (column, far_y, x, sibling))
            self.recv(piece, 10, (column, far_y, far_x, sibling))

    def finish(self):
        for copy in self.started:
            copy.wait_send()


def add_into(target, *terms):
    def body(n, carry):
        total = target[n].astype(F32)
        for term in terms:
            total = total + term[n].astype(F32)
        target[n] = total.astype(target.dtype)
        return carry

    lax.fori_loop(0, target.shape[0], body, 0)


class Scatter:
    def __init__(self, place, pieces, send_sems, recv_sems):
        self.place, self.pieces = place, pieces
        self.send_sems, self.recv_sems = send_sems, recv_sems
        self.started = []

    def copy(self, piece, n, source, target, **offset):
        return pltpu.make_async_remote_copy(
            src_ref=source,
            dst_ref=target,
            send_sem=self.send_sems.at[piece, n],
            recv_sem=self.recv_sems.at[piece, n],
            device_id=self.place.at(**offset),
            device_id_type=MESH,
        )

    def send(self, piece, n, source, target, **offset):
        copy = self.copy(piece, n, source, target, **offset)
        copy.start()
        self.started.append(copy)

    def recv(self, piece, n, target):
        self.copy(piece, n, target, target, dcore=1).wait_recv()
        return target

    def step(self, piece, stage):
        z, y, x, core = self.place.z, self.place.y, self.place.x, self.place.core
        far_y, far_x, sibling = 1 - y, 1 - x, 1 - core
        column, low, high = slice(0, Z), slice(0, Z // 2), slice(Z // 2, Z)
        part = self.pieces[piece]
        grad = part["grad"]
        if stage == 1:
            self.send(piece, 0, grad(column, EVERY, EVERY, sibling), part["half"], dcore=1)
        if stage == 2:
            add_into(grad(column, EVERY, EVERY, core), self.recv(piece, 0, part["half"]))
            self.send(piece, 1, grad(low, far_y, far_x, core), part["corner"](0), dy=1)
            self.send(piece, 2, grad(high, far_y, far_x, core), part["corner"](1), dx=1)
        if stage == 3:
            add_into(grad(low, y, far_x, core), self.recv(piece, 1, part["corner"](0)))
            self.send(piece, 3, grad(column, y, far_x, core), part["side"](0), dx=1)
            add_into(grad(high, far_y, x, core), self.recv(piece, 2, part["corner"](1)))
            self.send(piece, 4, grad(column, far_y, x, core), part["side"](1), dy=1)
        if stage == 4:
            sides = [self.recv(piece, 3 + n, part["side"](n)) for n in range(2)]
            add_into(grad(column, y, x, core), *sides)
            for hop in range(1, Z):
                self.send(
                    piece, 4 + hop, grad(lax.rem(z + hop, Z), y, x, core), part["hop"](hop - 1), dz=hop
                )
        if stage == 5:
            total = grad(z, y, x, core)[...].astype(F32)
            for hop in range(1, Z):
                total = total + self.recv(piece, 4 + hop, part["hop"](hop - 1))[...].astype(F32)
            part["share"](total)

    def finish(self):
        for copy in self.started:
            copy.wait_send()


def round_rows(source, target):
    def body(n, carry):
        rows = pl.ds(n * ROWS, ROWS)
        target[rows, :] = source[rows, :].astype(target.dtype)
        return carry

    lax.fori_loop(0, IMG, body, 0)


def head_lanes(shape, head):
    lane = lax.broadcasted_iota(jnp.int32, shape, len(shape) - 1)
    return lane < 64 if head == 0 else lane >= 64


def attend(qkv, out, image, pair):
    rows = slice(image * ROWS, (image + 1) * ROWS)
    lanes = 128 * pair
    queries = qkv[rows, lanes : lanes + 128] * BF16(0.125)
    keys = qkv[rows, D + lanes : D + lanes + 128]
    values = qkv[rows, 2 * D + lanes : 2 * D + lanes + 128]
    key_lane = lax.broadcasted_iota(jnp.int32, (1, ROWS), 1)
    parts = []
    for head in range(2):
        scores = nt(jnp.where(head_lanes((ROWS, 128), head), queries, BF16(0)), keys)
        scores = jnp.where(key_lane < TOK, scores, LOWEST)
        weights = jnp.exp(scores - jnp.max(scores, axis=-1, keepdims=True))
        inverse = 1.0 / jnp.sum(weights, axis=-1, keepdims=True)
        parts.append(nn(weights.astype(BF16), values) * inverse)
    out[rows, lanes : lanes + 128] = jnp.where(
        head_lanes((ROWS, 128), 0), parts[0], parts[1]
    ).astype(BF16)


def attend_backward(qkv, grad_out, grad_qkv, image, pair):
    rows = slice(image * ROWS, (image + 1) * ROWS)
    lanes = 128 * pair
    queries = qkv[rows, lanes : lanes + 128] * BF16(0.125)
    keys = qkv[rows, D + lanes : D + lanes + 128]
    values = qkv[rows, 2 * D + lanes : 2 * D + lanes + 128]
    grad = grad_out[rows, lanes : lanes + 128]
    key_row = lax.broadcasted_iota(jnp.int32, (ROWS, 1), 0)
    grad_q, grad_k, grad_v = [], [], []
    for head in range(2):
        own = head_lanes((ROWS, 128), head)
        scores = nt(jnp.where(own, keys, BF16(0)), queries)
        scores = jnp.where(key_row < TOK, scores, LOWEST)
        probs = jnp.exp(scores - jnp.max(scores, axis=0, keepdims=True))
        probs = probs * (1.0 / jnp.sum(probs, axis=0, keepdims=True))
        grad_probs = nt(jnp.where(own, values, BF16(0)), grad)
        total = jnp.sum(probs * grad_probs, axis=0, keepdims=True)
        grad_scores = (probs * (grad_probs - total)).astype(BF16)
        grad_v.append(nn(probs.astype(BF16), grad))
        grad_k.append(nn(grad_scores, queries))
        grad_q.append(tn(grad_scores, keys))
    first = head_lanes((ROWS, 128), 0)
    grad_qkv[rows, lanes : lanes + 128] = (
        jnp.where(first, grad_q[0], grad_q[1]) * 0.125
    ).astype(BF16)
    grad_qkv[rows, D + lanes : D + lanes + 128] = jnp.where(first, grad_k[0], grad_k[1]).astype(
        BF16
    )
    grad_qkv[rows, 2 * D + lanes : 2 * D + lanes + 128] = jnp.where(
        first, grad_v[0], grad_v[1]
    ).astype(BF16)


def mix_images(partners, mix, patches, mixed):
    for image in range(IMG):
        total = None
        for other in range(IMG):
            share = jnp.where(partners[image] == other, 1.0 - mix[image], 0.0)
            if image == other:
                share = share + mix[image]
            term = share * patches[other].astype(F32)
            total = term if total is None else total + term
        padding = jnp.zeros((ROWS - NPATCH, PATCH_DIM), F32)
        mixed[image * ROWS : (image + 1) * ROWS, :] = jnp.concatenate(
            [total, padding], axis=0
        ).astype(BF16)


def head_and_loss(
    image_count, stream, norms, partners, mix, labels, teacher, head, loss, feature, dlogits, dtop, dnorm
):
    picked = [
        stream[image * ROWS + NPATCH + kind : image * ROWS + NPATCH + kind + 1, :]
        for kind in range(2)
        for image in range(IMG)
    ]
    top = jnp.concatenate(picked + [jnp.zeros((2, D), F32)], axis=0)
    gain = norms[4 * L : 4 * L + 1, :]
    normed, _ = unit_norm(top)
    features = (normed * gain + norms[4 * L + 1 : 4 * L + 2, :]).astype(BF16)
    weights = head[...].astype(BF16)
    row = lax.broadcasted_iota(jnp.int32, (8, 2 * C), 0)
    lane = lax.broadcasted_iota(jnp.int32, (8, 2 * C), 1)
    is_class = row < IMG
    low_lane = jnp.where(is_class, 0, C)
    high_lane = jnp.where(is_class, C, jnp.where(row < 2 * IMG, 2 * C, 0))
    used = (lane >= low_lane) & (lane < high_lane)

    def log_softmax(values):
        values = jnp.where(used, values, LOWEST)
        shifted = values - jnp.max(values, axis=-1, keepdims=True)
        return shifted - jnp.log(jnp.sum(jnp.exp(shifted), axis=-1, keepdims=True))

    taught = jnp.concatenate([jnp.zeros((IMG, C), F32), teacher[...]], axis=1)
    taught = jnp.concatenate(
        [jnp.zeros((IMG, 2 * C), F32), taught, jnp.zeros((8 - 2 * IMG, 2 * C), F32)], axis=0
    )
    logits = nt(features, weights)
    student_log = log_softmax(jnp.where(is_class, logits, logits / TEMPER))
    teacher_log = log_softmax(taught / TEMPER)
    teacher_prob = jnp.exp(teacher_log)
    target = jnp.zeros((8, 2 * C), F32)
    for image in range(IMG):
        partner_label = labels[IMG - 1]
        for other in range(IMG - 1):
            partner_label = jnp.where(partners[image] == other, labels[other], partner_label)
        ours = jnp.where(lane == labels[image], mix[image], 0.0) + jnp.where(
            lane == partner_label, 1.0 - mix[image], 0.0
        )
        target = target + jnp.where(row == image, ours, 0.0)
    terms = jnp.where(
        is_class,
        -0.5 * target * student_log,
        0.5 * TEMPER * TEMPER * teacher_prob * (teacher_log - student_log),
    )
    terms = jnp.where(used, terms, 0.0)
    loss[...] = jnp.broadcast_to(jnp.sum(terms, axis=(0, 1), keepdims=True), (8, 128))
    wanted = jnp.where(is_class, target, teacher_prob)
    scale = jnp.where(is_class, 0.5 / image_count, 0.5 * TEMPER / image_count)
    grad_logits = (scale * jnp.where(used, jnp.exp(student_log) - wanted, 0.0)).astype(BF16)
    feature[...] = features.astype(F32)
    dlogits[...] = grad_logits.astype(F32)
    grad_top, grad_gain, grad_shift = norm_backward(nn(grad_logits, weights), top, gain)
    dtop[...] = grad_top
    dnorm[...] = jnp.concatenate([grad_gain, grad_shift, jnp.zeros((6, D), F32)], axis=0)


ATTN_SHAPE = (L, Z, Y, X, CORES, 48, D)
MLP_SHAPE = (L, 2, X, CORES, Z, Y, 48, D)
PATCH_SHAPE = (Z, Y, X, CORES, 32, D)
N_PIECES = 1 + 3 * L
PLANES = (1 + 3 * (L - 1),)
QUEUE = tuple(n for n in range(N_PIECES) if n not in PLANES)


def gather_views(patch_w, attn_w, mlp_w):
    def attn(depth):
        return lambda z, y, x, core: attn_w.at[depth, z, y, x, core]

    def mlp(depth, part):
        return lambda z, y, x, core: mlp_w.at[depth, part, x, core, z, y]

    views = [lambda z, y, x, core: patch_w.at[z, y, x, core]]
    for depth in range(L):
        views += [attn(depth), mlp(depth, 0), mlp(depth, 1)]
    return views


def forward_kernel(image_count, sharded, *refs):
    (
        partners, mix, labels, patches_h, teacher, pos, head_h, norms, patch_in, attn_in, mlp_in,
        mixed_h, x_h, a_h, qkv_h, o_h, x1_h, a2_h, z_h, slope_h, attn_h, mlp_h,
        loss, feature, dlogits, dtop, dnorm,
        mixed, x, a, qkv, o, x1, a2, z, slope, attn_w, mlp_w,
        patches, head, stream, patch_w, in_sems, out_sems, *rest,
    ) = refs
    outgoing = []

    def keep(source, target):
        copy = pltpu.make_async_copy(source, target, out_sems.at[len(outgoing)])
        copy.start()
        outgoing.append(copy)

    if sharded:
        patch_all, patch_s, attn_s, mlp_s, send_sems, recv_sems = rest
        loads = [(attn_in, attn_s), (mlp_in, mlp_s), (patch_in, patch_s)]
    else:
        loads = [(attn_in, attn_w), (mlp_in, mlp_w), (patch_in, patch_w)]
    loads += [(patches_h, patches), (head_h, head)]
    loads = [
        pltpu.make_async_copy(source, target, in_sems.at[n]) for n, (source, target) in enumerate(loads)
    ]
    for copy in loads:
        copy.start()

    if sharded:
        place = Place()
        gather = Gather(place, gather_views(patch_all, attn_w, mlp_w), PLANES, send_sems, recv_sems)
        mine = (place.z, place.y, place.x, place.core)
        loads[2].wait()
        patch_all[mine] = jnp.concatenate([patch_s[...], jnp.zeros((8, D), F32)], axis=0).astype(BF16)
        loads[0].wait()
        for depth in range(L):
            attn_w[(depth,) + mine] = attn_s[depth].astype(BF16)
        loads[1].wait()
        for depth in range(L):
            for part in range(2):
                mlp_w[depth, part, place.x, place.core, place.z, place.y] = mlp_s[depth, part].astype(BF16)
        greet(place.partners())
        for piece in PLANES + QUEUE:
            gather.step(piece, 1)

    def ahead(n, stage):
        if sharded and n < len(QUEUE):
            gather.step(QUEUE[n], stage)

    def need(piece):
        if not sharded:
            return
        if piece in PLANES:
            for stage in (4, 5):
                gather.step(piece, stage)
            return
        n = QUEUE.index(piece)
        ahead(n + 1, 2)
        ahead(n, 3)
        ahead(n + 2, 2)
        ahead(n + 1, 3)
        ahead(n, 4)
        ahead(n, 5)

    def between(piece):
        if not sharded:
            return
        later = [n for n in range(len(QUEUE)) if QUEUE[n] > piece]
        if later:
            ahead(later[0] + 2, 2)
            ahead(later[0] + 1, 3)

    if sharded:
        ahead(0, 2)
        for piece in PLANES:
            gather.step(piece, 2)
        ahead(1, 2)
        ahead(0, 3)
    else:
        for n in range(3):
            loads[n].wait()
    loads[3].wait()
    mix_images(partners, mix, patches, mixed)
    keep(mixed, mixed_h)
    need(0)
    if sharded:
        for n in range(Z * Y * X):
            block = patch_all[n // 4, n // 2 % 2, n % 2].astype(F32)
            patch_w[48 * n : 48 * n + 48, :] = jnp.concatenate([block[0, :24], block[1, :24]], axis=0).astype(BF16)
    embedded = nn(mixed[...], patch_w[...])
    added = jnp.concatenate([pos[2:TOK, :], pos[0:2, :], jnp.zeros((ROWS - TOK, D), F32)], axis=0)
    for image in range(IMG):
        rows = slice(image * ROWS, (image + 1) * ROWS)
        x[0, rows, :] = embedded[rows] + added
    for depth in range(L):
        norm = [norms[4 * depth + n : 4 * depth + n + 1, :] for n in range(4)]
        first = 1 + 3 * depth
        keep(x.at[depth], x_h.at[depth])
        a[depth] = (unit_norm(x[depth])[0] * norm[0] + norm[1]).astype(BF16)
        keep(a.at[depth], a_h.at[depth])
        need(first)
        for n in range(3):
            qkv[depth, :, D * n : D * n + D] = nt(a[depth], attn_w[depth, n].reshape(D, D)).astype(BF16)
        keep(qkv.at[depth], qkv_h.at[depth])
        keep(attn_w.at[depth], attn_h.at[depth])
        for image in range(IMG):
            for pair in range(3):
                attend(qkv.at[depth], o.at[depth], image, pair)
            if image == 1:
                between(first)
        keep(o.at[depth], o_h.at[depth])
        x1[depth] = x[depth] + nt(o[depth], attn_w[depth, 3].reshape(D, D))
        keep(x1.at[depth], x1_h.at[depth])
        a2[depth] = (unit_norm(x1[depth])[0] * norm[2] + norm[3]).astype(BF16)
        keep(a2.at[depth], a2_h.at[depth])
        need(first + 1)

        def widen(m, carry):
            hidden = nn(a2[depth], mlp_w[depth, 0, m // 2, lax.rem(m, 2)].reshape(D, D))
            phi = 0.5 * (1.0 + lax.erf(hidden * 2.0**-0.5))
            z[depth, m] = (hidden * phi).astype(BF16)
            density = jnp.exp(-0.5 * hidden * hidden) * 0.3989422804014327
            slope[depth, m] = (phi + hidden * density).astype(BF16)
            return carry

        lax.fori_loop(0, BLOCKS, widen, 0)
        keep(z.at[depth], z_h.at[depth])
        keep(slope.at[depth], slope_h.at[depth])
        need(first + 2)
        keep(mlp_w.at[depth], mlp_h.at[depth])
        total = x1[depth]
        for m in range(BLOCKS):
            total = total + nt(z[depth, m], mlp_w[depth, 1, m // 2, m % 2].reshape(D, D))
        if depth + 1 < L:
            x[depth + 1] = total
        else:
            stream[...] = total
    loads[4].wait()
    head_and_loss(
        image_count, stream, norms, partners, mix, labels, teacher, head, loss, feature, dlogits, dtop, dnorm
    )
    for copy in outgoing:
        copy.wait()
    if sharded:
        gather.finish()


SAVED = (
    ((ALL, PATCH_DIM), BF16),
    ((L, ALL, D), F32),
    ((L, ALL, D), BF16),
    ((L, ALL, 3 * D), BF16),
    ((L, ALL, D), BF16),
    ((L, ALL, D), F32),
    ((L, ALL, D), BF16),
    ((L, BLOCKS, ALL, D), BF16),
    ((L, BLOCKS, ALL, D), BF16),
    (ATTN_SHAPE, BF16),
    (MLP_SHAPE, BF16),
)
SMALL = (((8, 128), F32), ((8, D), F32), ((8, 2 * C), F32), ((8, D), F32), ((8, D), F32))


def forward(image_count, sharded, *operands):
    scratch = SAVED + (
        ((IMG, NPATCH, PATCH_DIM), BF16),
        ((2 * C, D), F32),
        ((ALL, D), F32),
        ((PATCH_DIM, D), BF16),
    )
    scratch = [pltpu.VMEM(*entry) for entry in scratch]
    scratch += [pltpu.SemaphoreType.DMA((5,)), pltpu.SemaphoreType.DMA((1 + 10 * L,))]
    if sharded:
        scratch += [
            pltpu.VMEM(PATCH_SHAPE, BF16),
            pltpu.VMEM((PATCH_DIM // (Z * Y * X * CORES), D), F32),
            pltpu.VMEM((L, 48, D), F32),
            pltpu.VMEM((L, 2, 48, D), F32),
            pltpu.SemaphoreType.DMA((N_PIECES, PIECES)),
            pltpu.SemaphoreType.DMA((N_PIECES, PIECES)),
        ]
    params = dict(collective_id=0, has_side_effects=True) if sharded else {}
    return pl.pallas_call(
        lambda *refs: forward_kernel(image_count, sharded, *refs),
        out_shape=[jax.ShapeDtypeStruct(*entry) for entry in SAVED + SMALL],
        in_specs=[SMEM] * 3 + [HBM, VMEM, VMEM, HBM, VMEM] + [HBM] * 3,
        out_specs=[HBM] * len(SAVED) + [VMEM] * len(SMALL),
        scratch_shapes=scratch,
        compiler_params=pltpu.CompilerParams(vmem_limit_bytes=62 * 2**20, **params),
        name="forward",
    )(*operands)


SMALL_SHAPE = (Z, Y, X, CORES, 8, D)
N_GRADS = 2 * L + 2
PATCH_PIECE = 2 * L
SMALL_PIECE = 2 * L + 1
MLP_DUE = (3, 5, 7, 10, 14)
ATTN_DUE = (8, 10, 12, 14, 17)
LAST_DUE = (20, 21, 22, 23, 24)
HEAD_DUE = (0, 1, 2, 3, 4)


def scatter_pieces(grads, halves, corners, sides, hops, shares):
    patch, attn, mlp, small = range(4)

    def flat(kind):
        return dict(
            grad=lambda z, y, x, core: grads[kind].at[z, y, x, core],
            half=halves[kind],
            corner=lambda n: corners[kind].at[n],
            side=lambda n: sides[kind].at[n],
            hop=lambda n: hops[kind].at[n],
            share=shares[kind],
        )

    def layered(kind, depth, grad):
        return dict(
            grad=grad,
            half=halves[kind].at[depth],
            corner=lambda n: corners[kind].at[depth, n],
            side=lambda n: sides[kind].at[depth, n],
            hop=lambda n: hops[kind].at[depth, n],
            share=lambda total: shares[kind](depth, total),
        )

    pieces = []
    for depth in reversed(range(L)):
        pieces.append(
            layered(mlp, depth, lambda z, y, x, core, depth=depth: grads[mlp].at[depth, :, x, core, z, y])
        )
        pieces.append(layered(attn, depth, lambda z, y, x, core, depth=depth: grads[attn].at[depth, z, y, x, core]))
    return pieces + [flat(patch), flat(small)]


def scatter_scratch():
    cases = (((), (), 32, BF16), ((L,), (), 48, BF16), ((L,), (2,), 48, BF16), ((), (), 8, F32))
    halves = [
        pltpu.VMEM((Z, Y, X, 32, D), BF16),
        pltpu.VMEM((L, Z, Y, X, 48, D), BF16),
        pltpu.VMEM((L, 2, X, Z, Y, 48, D), BF16),
        pltpu.VMEM((Z, Y, X, 8, D), F32),
    ]
    corners = [pltpu.VMEM(lead + (2,) + parts + (Z // 2, rows, D), kind) for lead, parts, rows, kind in cases]
    sides = [pltpu.VMEM(lead + (2,) + parts + (Z, rows, D), kind) for lead, parts, rows, kind in cases]
    hops = [pltpu.VMEM(lead + (Z - 1,) + parts + (rows, D), kind) for lead, parts, rows, kind in cases]
    return halves + corners + sides + hops


def backward_kernel(sharded, *refs):
    dtop, norms, mixed_h, *refs = refs
    held, refs = refs[:10], refs[10:]
    if sharded:
        loss, feature, dlogits, dnorm, *refs = refs
        patch_share, attn_share, mlp_share, head_sum, pos_sum, norm_sum, stats, *refs = refs
    else:
        grad_patch, grad_attn, grad_mlp, grad_norm, grad_pos, *refs = refs
    dx, dy, low, dout, dqkv, mixed, *refs = refs
    kept, sems, refs = refs[:10], refs[10], refs[11:]
    x, a, qkv, o, x1, a2, z, slope, attn_w, mlp_w = kept
    names = ("x", "a", "qkv", "o", "x1", "a2", "z", "slope", "attn", "mlp")

    def fetch(depth, *wanted):
        if depth < 0:
            return
        for name in wanted:
            n = names.index(name)
            pltpu.make_async_copy(held[n].at[depth], kept[n], sems.at[n]).start()

    def arrive(depth, *wanted):
        for name in wanted:
            n = names.index(name)
            pltpu.make_async_copy(held[n].at[depth], kept[n], sems.at[n]).wait()

    fetch(L - 1, "mlp", "slope", "a2", "z", "x1", "o", "attn", "qkv", "a", "x")
    mixed_copy = pltpu.make_async_copy(mixed_h, mixed, sems.at[len(names)])
    mixed_copy.start()
    due = {}
    if sharded:
        grad_patch, grad_attn, grad_mlp, grad_small, grad_norm, all_features, all_dlogits, packed, gathered, squares, *refs = refs
        buffers, refs = refs[:16], refs[16:]
        send_sems, recv_sems, head_send, head_recv, last_send, last_recv = refs
        place = Place()
        mine = (place.z, place.y, place.x, place.core)

        def count(total):
            flat = total.reshape(-1, D)
            squares[0:1, :] += jnp.sum(flat * flat, axis=0, keepdims=True)

        def share_patch(total):
            patch_share[...] = total[: patch_share.shape[0]]
            count(total)

        def share_attn(depth, total):
            attn_share[depth] = total
            count(total)

        def share_mlp(depth, total):
            mlp_share[depth] = total
            count(total)

        def share_small(total):
            gathered[mine + (slice(None), slice(0, D))] = total

        scatter = Scatter(
            place,
            scatter_pieces(
                (grad_patch, grad_attn, grad_mlp, grad_small),
                *(buffers[4 * n : 4 * n + 4] for n in range(4)),
                (share_patch, share_attn, share_mlp, share_small),
            ),
            send_sems,
            recv_sems,
        )
        heads = Gather(
            place,
            [
                lambda z, y, x, core: all_features.at[z, y, x, core],
                lambda z, y, x, core: all_dlogits.at[z, y, x, core],
            ],
            (), head_send, head_recv,
        )
        for turn in range(L):
            for stage in range(5):
                due.setdefault(10 * turn + MLP_DUE[stage], []).append((scatter, 2 * turn, stage + 1))
                due.setdefault(10 * turn + ATTN_DUE[stage], []).append((scatter, 2 * turn + 1, stage + 1))
        for stage in range(5):
            for piece in (PATCH_PIECE, SMALL_PIECE):
                due.setdefault(10 * (L - 1) + LAST_DUE[stage] - 10, []).append((scatter, piece, stage + 1))
            for piece in (1, 0):
                due.setdefault(HEAD_DUE[stage] - 1, []).append((heads, piece, stage + 1))
        squares[...] = jnp.zeros_like(squares)
        all_features[mine] = feature[...]
        all_dlogits[mine] = dlogits[...]
        greet(place.partners())

    def point(now):
        for who, piece, stage in due.pop(now, ()):
            who.step(piece, stage)

    point(-1)
    dx[...] = jnp.zeros((ALL, D), F32)
    for kind in range(2):
        for image in range(IMG):
            row = image * ROWS + NPATCH + kind
            dx[row : row + 1, :] = dtop[kind * IMG + image : kind * IMG + image + 1, :]
    grad_norm[...] = jnp.zeros((16, D), F32)
    for turn in range(L):
        depth = L - 1 - turn
        start = 10 * turn
        round_rows(dx, low)
        arrive(depth, "mlp", "slope", "a2", "z")
        total = None
        for m in range(BLOCKS):
            at = (m // 2, m % 2)
            grad_gelu = nn(low[...], mlp_w[(1,) + at].reshape(D, D))
            grad_hidden = (grad_gelu * slope[m].astype(F32)).astype(BF16)
            grad_mlp[(depth, 0) + at] = tn(a2[...], grad_hidden).astype(BF16).reshape(Z, Y, 48, D)
            grad_mlp[(depth, 1) + at] = tn(low[...], z[m]).astype(BF16).reshape(Z, Y, 48, D)
            term = nt(grad_hidden, mlp_w[(0,) + at].reshape(D, D))
            dy[...] = term if m == 0 else dy[...] + term
            point(start + m)
        fetch(depth - 1, "mlp", "slope", "a2", "z")
        arrive(depth, "x1", "o", "attn")
        grad_in, gain, shift = norm_backward(dy[...], x1[...], norms[4 * depth + 2 : 4 * depth + 3, :])
        grad_norm[4 * depth + 2 : 4 * depth + 3, :] = gain
        grad_norm[4 * depth + 3 : 4 * depth + 4, :] = shift
        dx[...] += grad_in
        round_rows(dx, low)
        point(start + 4)
        grad_attn[depth, 3] = tn(low[...], o[...]).astype(BF16).reshape(Y, X, CORES, 48, D)
        dout[...] = nn(low[...], attn_w[3].reshape(D, D)).astype(BF16)
        fetch(depth - 1, "x1", "o")
        arrive(depth, "qkv")
        for image in range(IMG):
            for pair in range(3):
                attend_backward(qkv, dout, dqkv, image, pair)
            point(start + 5 + image)
        fetch(depth - 1, "qkv")
        arrive(depth, "a", "x")
        for n in range(3):
            part = dqkv[:, D * n : D * n + D]
            grad_attn[depth, n] = tn(part, a[...]).astype(BF16).reshape(Y, X, CORES, 48, D)
        point(start + 8)
        total = None
        for n in range(3):
            term = nn(dqkv[:, D * n : D * n + D], attn_w[n].reshape(D, D))
            total = term if total is None else total + term
        fetch(depth - 1, "attn", "a")
        grad_in, gain, shift = norm_backward(total, x[...], norms[4 * depth : 4 * depth + 1, :])
        grad_norm[4 * depth : 4 * depth + 1, :] = gain
        grad_norm[4 * depth + 1 : 4 * depth + 2, :] = shift
        dx[...] += grad_in
        fetch(depth - 1, "x")
        point(start + 9)
    total = dx[0:ROWS] + dx[ROWS : 2 * ROWS] + dx[2 * ROWS :]
    round_rows(dx, low)
    mixed_copy.wait()
    patch = tn(mixed[...], low[...])
    rows = PATCH_DIM // (Z * Y * X * CORES)
    for n in range(Z * Y * X * CORES):
        block = jnp.concatenate([patch[rows * n : rows * n + rows], jnp.zeros((32 - rows, D), F32)], axis=0)
        grad_patch[n // 8, n // 4 % 2, n // 2 % 2, n % 2] = block.astype(BF16)
    if not sharded:
        grad_pos[...] = total
        return
    small = [total[8 * n : 8 * n + 8] for n in range(ROWS // 8)]
    small += [grad_norm[0:8, :], jnp.concatenate([grad_norm[8:12, :], dnorm[0:2, :], jnp.zeros((2, D), F32)], axis=0)]
    small.append(jnp.concatenate([loss[...], jnp.zeros((8, D - 128), F32)], axis=1))
    for n in range(Z * Y * X * CORES):
        grad_small[n // 8, n // 4 % 2, n // 2 % 2, n % 2] = small[n] if n < len(small) else jnp.zeros((8, D), F32)
    left = sorted(due)
    for now in left[:2]:
        point(now)
    features = all_features[...].reshape(-1, D).astype(BF16)
    per_plane = packed.shape[0] // Z

    def pack(n, carry):
        packed[pl.ds(n * per_plane, per_plane), :] = all_dlogits[n].reshape(per_plane, -1).astype(BF16)
        return carry

    lax.fori_loop(0, Z, pack, 0)
    for n in range(0, 2 * C, 512):
        lanes = slice(n, min(n + 512, 2 * C))
        part = tn(packed[:, lanes], features)
        head_sum[lanes, :] = part
        squares[1:2, :] += jnp.sum(part * part, axis=0, keepdims=True)
    for now in left[2:]:
        point(now)
    own = jnp.sum(squares[0:1, :], axis=(0, 1), keepdims=True)
    gathered[mine + (slice(None), slice(D, D + 128))] = jnp.broadcast_to(own, (8, 128))
    last = Gather(place, [lambda z, y, x, core: gathered.at[z, y, x, core]], (), last_send, last_recv)
    for stage in range(1, 6):
        last.step(0, stage)
    blocks = [gathered[n // 8, n // 4 % 2, n // 2 % 2, n % 2] for n in range(Z * Y * X * CORES)]
    pos = jnp.concatenate([block[:, :D] for block in blocks[: ROWS // 8]], axis=0)
    norm = jnp.concatenate([block[:, :D] for block in blocks[ROWS // 8 : ROWS // 8 + 2]], axis=0)
    pos_sum[...] = jnp.concatenate([pos[NPATCH:TOK], pos[:NPATCH]], axis=0)
    norm_sum[...] = norm[: 4 * L + 2]
    total = blocks[0][:, D:]
    for block in blocks[1:]:
        total = total + block[:, D:]
    rest = jnp.sum(pos * pos, axis=0, keepdims=True) + jnp.sum(norm * norm, axis=0, keepdims=True) + squares[1:2, :]
    total = total[0:1, :] + jnp.sum(rest, axis=(0, 1), keepdims=True)
    norm_all = jnp.sqrt(total)
    stats[...] = jnp.concatenate(
        [blocks[ROWS // 8 + 2][0:1, :128], norm_all, jnp.minimum(1.0, MAX_NORM / norm_all), jnp.zeros((5, 128), F32)],
        axis=0,
    )
    scatter.finish()
    heads.finish()
    last.finish()


def backward(sharded, *operands):
    full = ((PATCH_SHAPE, BF16), (ATTN_SHAPE, BF16), (MLP_SHAPE, BF16))
    if sharded:
        outs = (
            ((PATCH_DIM // (Z * Y * X * CORES), D), F32),
            ((L, 48, D), F32),
            ((L, 2, 48, D), F32),
            ((2 * C, D), F32),
            ((TOK, D), F32),
            ((4 * L + 2, D), F32),
            ((8, 128), F32),
        )
    else:
        outs = full + (((16, D), F32), ((ROWS, D), F32))
    scratch = [((ALL, D), F32), ((ALL, D), F32), ((ALL, D), BF16), ((ALL, D), BF16), ((ALL, 3 * D), BF16), SAVED[0]]
    scratch = [pltpu.VMEM(*entry) for entry in scratch]
    scratch += [pltpu.VMEM(shape[1:], kind) for shape, kind in SAVED[1:]]
    scratch += [pltpu.SemaphoreType.DMA((11,))]
    if sharded:
        scratch += [pltpu.VMEM(*entry) for entry in full]
        scratch += [
            pltpu.VMEM(SMALL_SHAPE, F32),
            pltpu.VMEM((16, D), F32),
            pltpu.VMEM(SMALL_SHAPE, F32),
            pltpu.VMEM((Z, Y, X, CORES, 8, 2 * C), F32),
            pltpu.VMEM((Z * Y * X * CORES * 8, 2 * C), BF16),
            pltpu.VMEM((Z, Y, X, CORES, 8, D + 128), F32),
            pltpu.VMEM((8, D), F32),
        ]
        scratch += scatter_scratch()
        scratch += [pltpu.SemaphoreType.DMA((N_GRADS, 8))] * 2
        scratch += [pltpu.SemaphoreType.DMA((2, PIECES))] * 2 + [pltpu.SemaphoreType.DMA((1, PIECES))] * 2
    params = dict(collective_id=1, has_side_effects=True) if sharded else {}
    return pl.pallas_call(
        lambda *refs: backward_kernel(sharded, *refs),
        out_shape=[jax.ShapeDtypeStruct(*entry) for entry in outs],
        in_specs=[VMEM] * 2 + [HBM] * 11 + [VMEM] * (4 if sharded else 0),
        out_specs=[VMEM] * len(outs),
        scratch_shapes=scratch,
        compiler_params=pltpu.CompilerParams(vmem_limit_bytes=63 * 2**20, **params),
        name="backward",
    )(*operands)


def adam_update(weight, first_moment, second, grad_in, factor, step_rate):
    clipped = grad_in * factor
    first_moment = BETA_ONE * first_moment + (1.0 - BETA_ONE) * clipped
    second = BETA_TWO * second + (1.0 - BETA_TWO) * clipped * clipped
    adam_move = (
        first_moment
        / (1.0 - BETA_ONE**ADAM_STEP)
        / (jnp.sqrt(second / (1.0 - BETA_TWO**ADAM_STEP)) + ADAM_EPS)
    )
    return (weight - step_rate * (adam_move + DECAY * weight), first_moment, second)


def per_device(
    patches, partners, mix_weight, labels, teacher_logits,
    patch_weight, attn_weight, mlp_weight, positions, head_weight, norm_params,
    patch_first, attn_first, mlp_first, pos_first, head_first, norm_first,
    patch_second, attn_second, mlp_second, pos_second, head_second, norm_second,
):
    axes = ("dp", "mp")
    image_count = patches.shape[0] * lax.axis_size("dp") * lax.axis_size("mp")
    sharded = (lax.axis_size("dp"), lax.axis_size("mp")) == (Z * Y, X * CORES)
    attn_t = jnp.swapaxes(attn_weight, 1, 2)
    if sharded:
        weights_in = (patch_weight, attn_t, mlp_weight)
    else:
        patch_low = lax.all_gather(patch_weight.astype(BF16), axes, axis=0, tiled=True)
        attn_low = lax.all_gather(attn_t.astype(BF16), axes, axis=1, tiled=True)
        mlp_low = lax.all_gather(mlp_weight.astype(BF16), "dp", axis=2, tiled=True)
        mlp_low = lax.all_gather(mlp_low, "mp", axis=2, tiled=False)
        weights_in = (patch_low, attn_low.reshape(ATTN_SHAPE), mlp_low.reshape(MLP_SHAPE))
    results = forward(
        image_count, sharded, partners, mix_weight, labels, patches, teacher_logits, positions,
        head_weight.T, norm_params, *weights_in,
    )
    saved, (loss, feature, dlogits, dtop, dnorm) = results[: len(SAVED)], results[len(SAVED) :]
    operands = (dtop, norm_params, *saved)
    if sharded:
        patch_share, attn_share, mlp_share, head_sum, pos_sum, norm_sum, stats = backward(
            True, *operands, loss, feature, dlogits, dnorm
        )
        loss_sum, global_norm, factor = stats[0, 0], stats[1, 0], stats[2, 0]
        mlp_share = mlp_share.reshape(mlp_weight.shape)
    else:
        grad_patch, grad_attn, grad_mlp, grad_norm, grad_pos = backward(False, *operands)
        rows = PATCH_DIM // (Z * Y * X * CORES)
        grad_patch = grad_patch.reshape(-1, 32, D)[:, :rows].reshape(PATCH_DIM, D).astype(F32)
        patch_share = lax.psum_scatter(grad_patch, axes, scatter_dimension=0, tiled=True)
        grad_attn = grad_attn.reshape(L, 4 * D, D).astype(F32)
        attn_share = lax.psum_scatter(grad_attn, axes, scatter_dimension=1, tiled=True)
        grad_mlp = grad_mlp.reshape(L, 2, BLOCKS, D, D).astype(F32)
        mlp_share = lax.psum_scatter(grad_mlp, "mp", scatter_dimension=2, tiled=True)
        mlp_share = lax.psum_scatter(mlp_share, "dp", scatter_dimension=3, tiled=True)
        mlp_share = mlp_share.reshape(mlp_weight.shape)
        features = lax.all_gather(feature.astype(BF16), axes, axis=0, tiled=True)
        all_dlogits = lax.all_gather(dlogits.astype(BF16), axes, axis=0, tiled=True)
        head_sum = tn(all_dlogits, features)
        grad_norms = jnp.concatenate([grad_norm[: 4 * L], dnorm[:2]], axis=0)
        grad_pos = jnp.concatenate([grad_pos[NPATCH:TOK], grad_pos[:NPATCH]], axis=0)
        pos_sum, norm_sum, loss_sum = lax.psum((grad_pos, grad_norms, loss[0, 0]), axes)
        own_squares = sum(jnp.sum(share * share) for share in (patch_share, attn_share, mlp_share))
        shared = sum(jnp.sum(total * total) for total in (pos_sum, head_sum, norm_sum))
        global_norm = jnp.sqrt(lax.psum(own_squares, axes) + shared)
        factor = jnp.minimum(1.0, MAX_NORM / global_norm)
    attn_share = jnp.swapaxes(attn_share, 1, 2)
    head_sum = head_sum.T
    weights = (patch_weight, attn_weight, mlp_weight, positions, head_weight, norm_params)
    firsts = (patch_first, attn_first, mlp_first, pos_first, head_first, norm_first)
    seconds = (patch_second, attn_second, mlp_second, pos_second, head_second, norm_second)
    grads = (patch_share, attn_share, mlp_share, pos_sum, head_sum, norm_sum)
    updated = [
        adam_update(weights[n], firsts[n], seconds[n], grads[n], factor, STEP_RATES[n]) for n in range(6)
    ]
    return (loss_sum, global_norm, *(entry[kind] for kind in range(3) for entry in updated))


def solution(mesh):
    images = (P(("dp", "mp"), None, None), P(("dp", "mp")), P(("dp", "mp")), P(("dp", "mp")), P(("dp", "mp"), None))
    weights = (P(("dp", "mp"), None), P(None, None, ("dp", "mp")), P(None, None, "dp", "mp"), P(), P(), P())
    return jax.shard_map(
        per_device,
        mesh=mesh,
        in_specs=images + weights * 3,
        out_specs=(P(), P()) + weights * 3,
        check_vma=False,
    )
```

```python
import jax
import jax.numpy as jnp
from jax import lax
from jax.experimental import pallas as pl
from jax.experimental.pallas import tpu as pltpu
from jax.sharding import PartitionSpec as P

D = 384
C = 1000
PATCH_DIM = 768
NPATCH = 196
L = 3
TOK = 198
IMG = 3
ROWS = 208
ALL = IMG * ROWS
BLOCKS = 4

Z = 4
Y = 2
X = 2
CORES = 2
EVERY = slice(0, 2)
PIECES = 11

LN_EPS = 1e-06
TEMPER = 3.0
MAX_NORM = 0.02
BETA_ONE = 0.9
BETA_TWO = 0.999
STEP_RATES = (0.05, 0.05, 0.05, 0.4, 0.12, 0.5)
DECAY = 0.05
ADAM_EPS = 1e-08
ADAM_STEP = 10.0
LOWEST = -1e30

BF16 = jnp.bfloat16
F32 = jnp.float32
VMEM = pl.BlockSpec(memory_space=pltpu.VMEM)
SMEM = pl.BlockSpec(memory_space=pltpu.SMEM)
HBM = pl.BlockSpec(memory_space=pl.ANY)
MESH = pl.DeviceIdType.MESH


def nn(left, right):
    return jnp.dot(left, right, preferred_element_type=F32)


def nt(left, right):
    return lax.dot_general(left, right, (((1,), (1,)), ((), ())), preferred_element_type=F32)


def tn(left, right):
    return lax.dot_general(left, right, (((0,), (0,)), ((), ())), preferred_element_type=F32)


def unit_norm(inputs):
    centred = inputs - jnp.mean(inputs, axis=-1, keepdims=True)
    inverse = lax.rsqrt(jnp.mean(centred * centred, axis=-1, keepdims=True) + LN_EPS)
    return centred * inverse, inverse


def norm_backward(grad_out, inputs, gain):
    normed, inverse = unit_norm(inputs)
    grad_gain = jnp.sum(grad_out * normed, axis=0, keepdims=True)
    grad_shift = jnp.sum(grad_out, axis=0, keepdims=True)
    scaled = grad_out * gain
    grad_in = inverse * (
        scaled
        - jnp.mean(scaled, axis=-1, keepdims=True)
        - normed * jnp.mean(scaled * normed, axis=-1, keepdims=True)
    )
    return grad_in, grad_gain, grad_shift


class Place:
    def __init__(self):
        dp, mp = lax.axis_index("dp"), lax.axis_index("mp")
        self.z, self.y = dp // Y, dp % Y
        self.x, self.core = mp // CORES, mp % CORES

    def at(self, dz=0, dy=0, dx=0, dcore=0):
        z = lax.rem(self.z + dz, Z)
        y = 1 - self.y if dy else self.y
        x = 1 - self.x if dx else self.x
        core = 1 - self.core if dcore else self.core
        return {"dp": z * Y + y, "mp": x * CORES + core}

    def partners(self):
        column = [self.at(dz=step) for step in range(1, Z)]
        return column + [self.at(dx=1), self.at(dy=1), self.at(dcore=1), self.at(dy=1, dx=1)]


def greet(partners):
    barrier = pltpu.get_barrier_semaphore()
    for partner in partners:
        pl.semaphore_signal(barrier, inc=1, device_id=partner, device_id_type=MESH)
    pl.semaphore_wait(barrier, len(partners))


class Gather:
    def __init__(self, place, pieces, send_sems, recv_sems, planes=(), direct=False):
        self.place, self.pieces, self.planes, self.direct = place, pieces, planes, direct
        self.send_sems, self.recv_sems = send_sems, recv_sems
        self.started = []
        self.done = set()

    def copy(self, piece, n, region, target):
        view = self.pieces[piece](*region)
        return pltpu.make_async_remote_copy(
            src_ref=view,
            dst_ref=view,
            send_sem=self.send_sems.at[piece, n],
            recv_sem=self.recv_sems.at[piece, n],
            device_id=target,
            device_id_type=MESH,
        )

    def send(self, piece, n, region, **offset):
        copy = self.copy(piece, n, region, self.place.at(**offset))
        copy.start()
        self.started.append(copy)

    def recv(self, piece, n, region):
        self.copy(piece, n, region, self.place.at(dcore=1)).wait_recv()

    def step(self, piece, stage):
        if (piece, stage) in self.done:
            return
        self.done.add((piece, stage))
        z, y, x, core = self.place.z, self.place.y, self.place.x, self.place.core
        far_y, far_x, sibling = 1 - y, 1 - x, 1 - core
        column, low, high = slice(0, Z), slice(0, Z // 2), slice(Z // 2, Z)
        if piece in self.planes:
            if stage == 1:
                self.send(piece, 3, (z, y, x, core), dx=1)
                self.send(piece, 4, (z, y, x, core), dy=1)
                self.send(piece, 6, (z, y, x, core), dy=1, dx=1)
            if stage == 2:
                self.recv(piece, 3, (z, y, far_x, core))
                self.recv(piece, 4, (z, far_y, x, core))
                self.recv(piece, 6, (z, far_y, far_x, core))
                for hop in range(1, Z):
                    self.send(piece, hop - 1, (z, EVERY, EVERY, core), dz=hop)
            if stage == 4:
                for hop in range(1, Z):
                    self.recv(piece, hop - 1, (lax.rem(z + Z - hop, Z), EVERY, EVERY, core))
                self.send(piece, 5, (column, EVERY, EVERY, core), dcore=1)
            if stage == 5:
                self.recv(piece, 5, (column, EVERY, EVERY, sibling))
            return
        if stage == 1:
            for hop in range(1, Z):
                self.send(piece, hop - 1, (z, y, x, core), dz=hop)
        if self.direct:
            if stage == 2:
                for hop in range(1, Z):
                    self.recv(piece, hop - 1, (lax.rem(z + Z - hop, Z), y, x, core))
                self.send(piece, 3, (column, y, x, core), dx=1)
                self.send(piece, 4, (column, y, x, core), dy=1)
                self.send(piece, 6, (column, y, x, core), dy=1, dx=1)
            if stage == 4:
                self.recv(piece, 3, (column, y, far_x, core))
                self.recv(piece, 4, (column, far_y, x, core))
                self.recv(piece, 6, (column, far_y, far_x, core))
                self.send(piece, 5, (column, EVERY, EVERY, core), dcore=1)
            if stage == 5:
                self.recv(piece, 5, (column, EVERY, EVERY, sibling))
            return
        if stage == 2:
            for hop in range(1, Z):
                self.recv(piece, hop - 1, (lax.rem(z + Z - hop, Z), y, x, core))
            self.send(piece, 3, (column, y, x, core), dx=1)
            self.send(piece, 4, (column, y, x, core), dy=1)
            self.send(piece, 5, (column, y, x, core), dcore=1)
        if stage == 3:
            self.recv(piece, 3, (column, y, far_x, core))
            self.send(piece, 6, (low, y, far_x, core), dy=1)
            self.send(piece, 8, (column, y, far_x, core), dcore=1)
            self.recv(piece, 4, (column, far_y, x, core))
            self.send(piece, 7, (high, far_y, x, core), dx=1)
            self.send(piece, 9, (column, far_y, x, core), dcore=1)
        if stage == 4:
            self.recv(piece, 6, (low, far_y, far_x, core))
            self.recv(piece, 7, (high, far_y, far_x, core))
            self.send(piece, 10, (column, far_y, far_x, core), dcore=1)
        if stage == 5:
            self.recv(piece, 5, (column, y, x, sibling))
            self.recv(piece, 8, (column, y, far_x, sibling))
            self.recv(piece, 9, (column, far_y, x, sibling))
            self.recv(piece, 10, (column, far_y, far_x, sibling))

    def finish(self):
        for copy in self.started:
            copy.wait_send()


def add_into(target, *terms):
    def body(n, carry):
        total = target[n].astype(F32)
        for term in terms:
            total = total + term[n].astype(F32)
        target[n] = total.astype(target.dtype)
        return carry

    lax.fori_loop(0, target.shape[0], body, 0)


class Scatter:
    def __init__(self, place, pieces, send_sems, recv_sems):
        self.place, self.pieces = place, pieces
        self.send_sems, self.recv_sems = send_sems, recv_sems
        self.started = []

    def copy(self, piece, n, source, target, **offset):
        return pltpu.make_async_remote_copy(
            src_ref=source,
            dst_ref=target,
            send_sem=self.send_sems.at[piece, n],
            recv_sem=self.recv_sems.at[piece, n],
            device_id=self.place.at(**offset),
            device_id_type=MESH,
        )

    def send(self, piece, n, source, target, **offset):
        copy = self.copy(piece, n, source, target, **offset)
        copy.start()
        self.started.append(copy)

    def recv(self, piece, n, target):
        self.copy(piece, n, target, target, dcore=1).wait_recv()
        return target

    def step(self, piece, stage):
        z, y, x, core = self.place.z, self.place.y, self.place.x, self.place.core
        far_y, far_x, sibling = 1 - y, 1 - x, 1 - core
        column, low, high = slice(0, Z), slice(0, Z // 2), slice(Z // 2, Z)
        part = self.pieces[piece]
        grad = part["grad"]
        if stage == 1:
            self.send(piece, 0, grad(column, EVERY, EVERY, sibling), part["half"], dcore=1)
        if stage == 2:
            add_into(grad(column, EVERY, EVERY, core), self.recv(piece, 0, part["half"]))
            if part["direct"]:
                self.send(piece, 1, grad(column, far_y, far_x, core), part["corner"], dy=1, dx=1)
                self.send(piece, 3, grad(column, y, far_x, core), part["side"](0), dx=1)
                self.send(piece, 4, grad(column, far_y, x, core), part["side"](1), dy=1)
                return
            self.send(piece, 1, grad(low, far_y, far_x, core), part["corner"](0), dy=1)
            self.send(piece, 2, grad(high, far_y, far_x, core), part["corner"](1), dx=1)
        if stage == 3 and not part["direct"]:
            add_into(grad(low, y, far_x, core), self.recv(piece, 1, part["corner"](0)))
            self.send(piece, 3, grad(column, y, far_x, core), part["side"](0), dx=1)
            add_into(grad(high, far_y, x, core), self.recv(piece, 2, part["corner"](1)))
            self.send(piece, 4, grad(column, far_y, x, core), part["side"](1), dy=1)
        if stage == 4:
            sides = [self.recv(piece, 3 + n, part["side"](n)) for n in range(2)]
            if part["direct"]:
                sides.append(self.recv(piece, 1, part["corner"]))
            add_into(grad(column, y, x, core), *sides)
            for hop in range(1, Z):
                self.send(
                    piece, 4 + hop, grad(lax.rem(z + hop, Z), y, x, core), part["hop"](hop - 1), dz=hop
                )
        if stage == 5:
            total = grad(z, y, x, core)[...].astype(F32)
            for hop in range(1, Z):
                total = total + self.recv(piece, 4 + hop, part["hop"](hop - 1))[...].astype(F32)
            part["share"](total)

    def finish(self):
        for copy in self.started:
            copy.wait_send()


def round_rows(source, target):
    def body(n, carry):
        rows = pl.ds(n * ROWS, ROWS)
        target[rows, :] = source[rows, :].astype(target.dtype)
        return carry

    lax.fori_loop(0, IMG, body, 0)


def head_lanes(shape, head):
    lane = lax.broadcasted_iota(jnp.int32, shape, len(shape) - 1)
    return lane < 64 if head == 0 else lane >= 64


def attend(qkv, out, image, pair):
    rows = slice(image * ROWS, (image + 1) * ROWS)
    lanes = 128 * pair
    queries = qkv[rows, lanes : lanes + 128] * BF16(0.125)
    keys = qkv[rows, D + lanes : D + lanes + 128]
    values = qkv[rows, 2 * D + lanes : 2 * D + lanes + 128]
    key_lane = lax.broadcasted_iota(jnp.int32, (1, ROWS), 1)
    parts = []
    for head in range(2):
        scores = nt(jnp.where(head_lanes((ROWS, 128), head), queries, BF16(0)), keys)
        scores = jnp.where(key_lane < TOK, scores, LOWEST)
        weights = jnp.exp(scores - jnp.max(scores, axis=-1, keepdims=True))
        inverse = 1.0 / jnp.sum(weights, axis=-1, keepdims=True)
        parts.append(nn(weights.astype(BF16), values) * inverse)
    out[rows, lanes : lanes + 128] = jnp.where(
        head_lanes((ROWS, 128), 0), parts[0], parts[1]
    ).astype(BF16)


def attend_backward(qkv, grad_out, grad_qkv, image, pair):
    rows = slice(image * ROWS, (image + 1) * ROWS)
    lanes = 128 * pair
    queries = qkv[rows, lanes : lanes + 128] * BF16(0.125)
    keys = qkv[rows, D + lanes : D + lanes + 128]
    values = qkv[rows, 2 * D + lanes : 2 * D + lanes + 128]
    grad = grad_out[rows, lanes : lanes + 128]
    key_row = lax.broadcasted_iota(jnp.int32, (ROWS, 1), 0)
    grad_q, grad_k, grad_v = [], [], []
    for head in range(2):
        own = head_lanes((ROWS, 128), head)
        scores = nt(jnp.where(own, keys, BF16(0)), queries)
        scores = jnp.where(key_row < TOK, scores, LOWEST)
        probs = jnp.exp(scores - jnp.max(scores, axis=0, keepdims=True))
        probs = probs * (1.0 / jnp.sum(probs, axis=0, keepdims=True))
        grad_probs = nt(jnp.where(own, values, BF16(0)), grad)
        total = jnp.sum(probs * grad_probs, axis=0, keepdims=True)
        grad_scores = (probs * (grad_probs - total)).astype(BF16)
        grad_v.append(nn(probs.astype(BF16), grad))
        grad_k.append(nn(grad_scores, queries))
        grad_q.append(tn(grad_scores, keys))
    first = head_lanes((ROWS, 128), 0)
    grad_qkv[rows, lanes : lanes + 128] = (
        jnp.where(first, grad_q[0], grad_q[1]) * 0.125
    ).astype(BF16)
    grad_qkv[rows, D + lanes : D + lanes + 128] = jnp.where(first, grad_k[0], grad_k[1]).astype(
        BF16
    )
    grad_qkv[rows, 2 * D + lanes : 2 * D + lanes + 128] = jnp.where(
        first, grad_v[0], grad_v[1]
    ).astype(BF16)


def mix_images(partners, mix, patches, mixed):
    for image in range(IMG):
        total = None
        for other in range(IMG):
            share = jnp.where(partners[image] == other, 1.0 - mix[image], 0.0)
            if image == other:
                share = share + mix[image]
            term = share * patches[other].astype(F32)
            total = term if total is None else total + term
        padding = jnp.zeros((ROWS - NPATCH, PATCH_DIM), F32)
        mixed[image * ROWS : (image + 1) * ROWS, :] = jnp.concatenate(
            [total, padding], axis=0
        ).astype(BF16)


def head_and_loss(
    image_count, stream, norms, partners, mix, labels, teacher, head, loss, feature, dlogits, dtop, dnorm
):
    picked = [
        stream[image * ROWS + NPATCH + kind : image * ROWS + NPATCH + kind + 1, :]
        for kind in range(2)
        for image in range(IMG)
    ]
    top = jnp.concatenate(picked + [jnp.zeros((2, D), F32)], axis=0)
    gain = norms[4 * L : 4 * L + 1, :]
    normed, _ = unit_norm(top)
    features = (normed * gain + norms[4 * L + 1 : 4 * L + 2, :]).astype(BF16)
    weights = head[...].astype(BF16)
    row = lax.broadcasted_iota(jnp.int32, (8, 2 * C), 0)
    lane = lax.broadcasted_iota(jnp.int32, (8, 2 * C), 1)
    is_class = row < IMG
    low_lane = jnp.where(is_class, 0, C)
    high_lane = jnp.where(is_class, C, jnp.where(row < 2 * IMG, 2 * C, 0))
    used = (lane >= low_lane) & (lane < high_lane)

    def log_softmax(values):
        values = jnp.where(used, values, LOWEST)
        shifted = values - jnp.max(values, axis=-1, keepdims=True)
        return shifted - jnp.log(jnp.sum(jnp.exp(shifted), axis=-1, keepdims=True))

    taught = jnp.concatenate([jnp.zeros((IMG, C), F32), teacher[...]], axis=1)
    taught = jnp.concatenate(
        [jnp.zeros((IMG, 2 * C), F32), taught, jnp.zeros((8 - 2 * IMG, 2 * C), F32)], axis=0
    )
    logits = nt(features, weights)
    student_log = log_softmax(jnp.where(is_class, logits, logits / TEMPER))
    teacher_log = log_softmax(taught / TEMPER)
    teacher_prob = jnp.exp(teacher_log)
    target = jnp.zeros((8, 2 * C), F32)
    for image in range(IMG):
        partner_label = labels[IMG - 1]
        for other in range(IMG - 1):
            partner_label = jnp.where(partners[image] == other, labels[other], partner_label)
        ours = jnp.where(lane == labels[image], mix[image], 0.0) + jnp.where(
            lane == partner_label, 1.0 - mix[image], 0.0
        )
        target = target + jnp.where(row == image, ours, 0.0)
    terms = jnp.where(
        is_class,
        -0.5 * target * student_log,
        0.5 * TEMPER * TEMPER * teacher_prob * (teacher_log - student_log),
    )
    terms = jnp.where(used, terms, 0.0)
    loss[...] = jnp.broadcast_to(jnp.sum(terms, axis=(0, 1), keepdims=True), (8, 128))
    wanted = jnp.where(is_class, target, teacher_prob)
    scale = jnp.where(is_class, 0.5 / image_count, 0.5 * TEMPER / image_count)
    grad_logits = (scale * jnp.where(used, jnp.exp(student_log) - wanted, 0.0)).astype(BF16)
    feature[...] = features.astype(F32)
    dlogits[...] = grad_logits.astype(F32)
    grad_top, grad_gain, grad_shift = norm_backward(nn(grad_logits, weights), top, gain)
    dtop[...] = grad_top
    dnorm[...] = jnp.concatenate([grad_gain, grad_shift, jnp.zeros((6, D), F32)], axis=0)


ATTN_SHAPE = (L, Z, Y, X, CORES, 48, D)
MLP_SHAPE = (L, 2, X, CORES, Z, Y, 48, D)
PATCH_SHAPE = (Z, Y, X, CORES, 32, D)
N_PIECES = 1 + 3 * L
PLANES = (1 + 3 * (L - 1),)
QUEUE = tuple(n for n in range(N_PIECES) if n not in PLANES)


def gather_views(patch_w, attn_w, mlp_w):
    def attn(depth):
        return lambda z, y, x, core: attn_w.at[depth, z, y, x, core]

    def mlp(depth, part):
        return lambda z, y, x, core: mlp_w.at[depth, part, x, core, z, y]

    views = [lambda z, y, x, core: patch_w.at[z, y, x, core]]
    for depth in range(L):
        views += [attn(depth), mlp(depth, 0), mlp(depth, 1)]
    return views


def forward_kernel(image_count, sharded, *refs):
    (
        partners, mix, labels, patches_h, teacher, pos, head_h, norms, patch_in, attn_in, mlp_in,
        mixed_h, x_h, a_h, qkv_h, o_h, x1_h, a2_h, z_h, slope_h, attn_h, mlp_h,
        loss, feature, dlogits, dtop, dnorm,
        mixed, x, a, qkv, o, x1, a2, z, slope, attn_w, mlp_w,
        patches, head, stream, patch_w, in_sems, out_sems, *rest,
    ) = refs
    outgoing = []

    def keep(source, target):
        copy = pltpu.make_async_copy(source, target, out_sems.at[len(outgoing)])
        copy.start()
        outgoing.append(copy)

    if sharded:
        patch_all, patch_s, attn_s, mlp_s, send_sems, recv_sems = rest
        loads = [(attn_in, attn_s), (mlp_in, mlp_s), (patch_in, patch_s)]
    else:
        loads = [(attn_in, attn_w), (mlp_in, mlp_w), (patch_in, patch_w)]
    loads += [(patches_h, patches), (head_h, head)]
    loads = [
        pltpu.make_async_copy(source, target, in_sems.at[n]) for n, (source, target) in enumerate(loads)
    ]
    for copy in loads:
        copy.start()

    if sharded:
        place = Place()
        gather = Gather(place, gather_views(patch_all, attn_w, mlp_w), send_sems, recv_sems, planes=PLANES)
        mine = (place.z, place.y, place.x, place.core)
        loads[2].wait()
        patch_all[mine] = jnp.concatenate([patch_s[...], jnp.zeros((8, D), F32)], axis=0).astype(BF16)
        loads[0].wait()
        for depth in range(L):
            attn_w[(depth,) + mine] = attn_s[depth].astype(BF16)
        loads[1].wait()
        for depth in range(L):
            for part in range(2):
                mlp_w[depth, part, place.x, place.core, place.z, place.y] = mlp_s[depth, part].astype(BF16)
        greet(place.partners())
        for piece in PLANES + QUEUE:
            gather.step(piece, 1)

    def ahead(n, stage):
        if sharded and n < len(QUEUE):
            gather.step(QUEUE[n], stage)

    def need(piece):
        if not sharded:
            return
        if piece in PLANES:
            for stage in (4, 5):
                gather.step(piece, stage)
            return
        n = QUEUE.index(piece)
        ahead(n + 1, 2)
        ahead(n, 3)
        ahead(n + 2, 2)
        ahead(n + 1, 3)
        ahead(n, 4)
        ahead(n, 5)

    def between(piece):
        if not sharded:
            return
        later = [n for n in range(len(QUEUE)) if QUEUE[n] > piece]
        if later:
            ahead(later[0] + 2, 2)
            ahead(later[0] + 1, 3)

    if sharded:
        ahead(0, 2)
        for piece in PLANES:
            gather.step(piece, 2)
        ahead(1, 2)
        ahead(0, 3)
    else:
        for n in range(3):
            loads[n].wait()
    loads[3].wait()
    mix_images(partners, mix, patches, mixed)
    keep(mixed, mixed_h)
    need(0)
    if sharded:
        for n in range(Z * Y * X):
            block = patch_all[n // 4, n // 2 % 2, n % 2].astype(F32)
            patch_w[48 * n : 48 * n + 48, :] = jnp.concatenate([block[0, :24], block[1, :24]], axis=0).astype(BF16)
    embedded = nn(mixed[...], patch_w[...])
    added = jnp.concatenate([pos[2:TOK, :], pos[0:2, :], jnp.zeros((ROWS - TOK, D), F32)], axis=0)
    for image in range(IMG):
        rows = slice(image * ROWS, (image + 1) * ROWS)
        x[0, rows, :] = embedded[rows] + added
    for depth in range(L):
        norm = [norms[4 * depth + n : 4 * depth + n + 1, :] for n in range(4)]
        first = 1 + 3 * depth
        keep(x.at[depth], x_h.at[depth])
        a[depth] = (unit_norm(x[depth])[0] * norm[0] + norm[1]).astype(BF16)
        keep(a.at[depth], a_h.at[depth])
        need(first)
        for n in range(3):
            qkv[depth, :, D * n : D * n + D] = nt(a[depth], attn_w[depth, n].reshape(D, D)).astype(BF16)
        keep(qkv.at[depth], qkv_h.at[depth])
        keep(attn_w.at[depth], attn_h.at[depth])
        for image in range(IMG):
            for pair in range(3):
                attend(qkv.at[depth], o.at[depth], image, pair)
            if image == 1:
                between(first)
        keep(o.at[depth], o_h.at[depth])
        x1[depth] = x[depth] + nt(o[depth], attn_w[depth, 3].reshape(D, D))
        keep(x1.at[depth], x1_h.at[depth])
        a2[depth] = (unit_norm(x1[depth])[0] * norm[2] + norm[3]).astype(BF16)
        keep(a2.at[depth], a2_h.at[depth])
        need(first + 1)

        def widen(m, carry):
            hidden = nn(a2[depth], mlp_w[depth, 0, m // 2, lax.rem(m, 2)].reshape(D, D))
            phi = 0.5 * (1.0 + lax.erf(hidden * 2.0**-0.5))
            z[depth, m] = (hidden * phi).astype(BF16)
            density = jnp.exp(-0.5 * hidden * hidden) * 0.3989422804014327
            slope[depth, m] = (phi + hidden * density).astype(BF16)
            return carry

        lax.fori_loop(0, BLOCKS, widen, 0)
        keep(z.at[depth], z_h.at[depth])
        keep(slope.at[depth], slope_h.at[depth])
        need(first + 2)
        keep(mlp_w.at[depth], mlp_h.at[depth])
        total = x1[depth]
        for m in range(BLOCKS):
            total = total + nt(z[depth, m], mlp_w[depth, 1, m // 2, m % 2].reshape(D, D))
        if depth + 1 < L:
            x[depth + 1] = total
        else:
            stream[...] = total
    loads[4].wait()
    head_and_loss(
        image_count, stream, norms, partners, mix, labels, teacher, head, loss, feature, dlogits, dtop, dnorm
    )
    for copy in outgoing:
        copy.wait()
    if sharded:
        gather.finish()


SAVED = (
    ((ALL, PATCH_DIM), BF16),
    ((L, ALL, D), F32),
    ((L, ALL, D), BF16),
    ((L, ALL, 3 * D), BF16),
    ((L, ALL, D), BF16),
    ((L, ALL, D), F32),
    ((L, ALL, D), BF16),
    ((L, BLOCKS, ALL, D), BF16),
    ((L, BLOCKS, ALL, D), BF16),
    (ATTN_SHAPE, BF16),
    (MLP_SHAPE, BF16),
)
SMALL = (((8, 128), F32), ((8, D), F32), ((8, 2 * C), F32), ((8, D), F32), ((8, D), F32))


def forward(image_count, sharded, *operands):
    scratch = SAVED + (
        ((IMG, NPATCH, PATCH_DIM), BF16),
        ((2 * C, D), F32),
        ((ALL, D), F32),
        ((PATCH_DIM, D), BF16),
    )
    scratch = [pltpu.VMEM(*entry) for entry in scratch]
    scratch += [pltpu.SemaphoreType.DMA((5,)), pltpu.SemaphoreType.DMA((1 + 10 * L,))]
    if sharded:
        scratch += [
            pltpu.VMEM(PATCH_SHAPE, BF16),
            pltpu.VMEM((PATCH_DIM // (Z * Y * X * CORES), D), F32),
            pltpu.VMEM((L, 48, D), F32),
            pltpu.VMEM((L, 2, 48, D), F32),
            pltpu.SemaphoreType.DMA((N_PIECES, PIECES)),
            pltpu.SemaphoreType.DMA((N_PIECES, PIECES)),
        ]
    params = dict(collective_id=0, has_side_effects=True) if sharded else {}
    return pl.pallas_call(
        lambda *refs: forward_kernel(image_count, sharded, *refs),
        out_shape=[jax.ShapeDtypeStruct(*entry) for entry in SAVED + SMALL],
        in_specs=[SMEM] * 3 + [HBM, VMEM, VMEM, HBM, VMEM] + [HBM] * 3,
        out_specs=[HBM] * len(SAVED) + [VMEM] * len(SMALL),
        scratch_shapes=scratch,
        compiler_params=pltpu.CompilerParams(vmem_limit_bytes=62 * 2**20, **params),
        name="forward",
    )(*operands)


SMALL_SHAPE = (Z, Y, X, CORES, 8, D)
HEAD_LANES = 1280
HEAD_AT = 2048
N_GRADS = 2 * L + 2
PATCH_PIECE = 2 * L
SMALL_PIECE = 2 * L + 1
MLP_DUE = (3, 6, 10, 16, 20)
ATTN_DUE = (8, 10, 12, 17, 21)
MLP_DUE_LAST = (3, 5, 8, 13, 16)
ATTN_DUE_LAST = (8, 9, 11, 14, 17)
LAST_DUE = (10, 11, 12, 13, 14)
HEAD_DUE = (-1, 2, 4, 6, 9)


def scatter_pieces(grads, halves, corners, sides, hops, shares):
    patch, attn, mlp, small = range(4)

    def flat(kind):
        return dict(
            grad=lambda z, y, x, core: grads[kind].at[z, y, x, core],
            direct=True,
            half=halves[kind],
            corner=corners[kind],
            side=lambda n: sides[kind].at[n],
            hop=lambda n: hops[kind].at[n],
            share=shares[kind],
        )

    def layered(kind, depth, grad):
        return dict(
            direct=False,
            grad=grad,
            half=halves[kind].at[depth],
            corner=lambda n: corners[kind].at[depth, n],
            side=lambda n: sides[kind].at[depth, n],
            hop=lambda n: hops[kind].at[depth, n],
            share=lambda total: shares[kind](depth, total),
        )

    pieces = []
    for depth in reversed(range(L)):
        pieces.append(
            layered(mlp, depth, lambda z, y, x, core, depth=depth: grads[mlp].at[depth, :, x, core, z, y])
        )
        pieces.append(layered(attn, depth, lambda z, y, x, core, depth=depth: grads[attn].at[depth, z, y, x, core]))
    return pieces + [flat(patch), flat(small)]


def scatter_scratch():
    cases = (((), (), 32, BF16), ((L,), (), 48, BF16), ((L,), (2,), 48, BF16), ((), (), 8, F32))
    halves = [
        pltpu.VMEM((Z, Y, X, 32, D), BF16),
        pltpu.VMEM((L, Z, Y, X, 48, D), BF16),
        pltpu.VMEM((L, 2, X, Z, Y, 48, D), BF16),
        pltpu.VMEM((Z, Y, X, 8, D), F32),
    ]
    corners = [
        pltpu.VMEM(lead + (2,) + parts + (Z // 2, rows, D) if lead else (Z, rows, D), kind)
        for lead, parts, rows, kind in cases
    ]
    sides = [pltpu.VMEM(lead + (2,) + parts + (Z, rows, D), kind) for lead, parts, rows, kind in cases]
    hops = [pltpu.VMEM(lead + (Z - 1,) + parts + (rows, D), kind) for lead, parts, rows, kind in cases]
    return halves + corners + sides + hops


def backward_kernel(sharded, *refs):
    dtop, norms, mixed_h, *refs = refs
    held, refs = refs[:10], refs[10:]
    if sharded:
        loss, feature, dlogits, dnorm, *refs = refs
        patch_share, attn_share, mlp_share, head_out, pos_sum, norm_sum, stats, *refs = refs
    else:
        grad_patch, grad_attn, grad_mlp, grad_norm, grad_pos, *refs = refs
    dx, dy, low, dout, dqkv, mixed, *refs = refs
    kept, sems, refs = refs[:10], refs[10], refs[11:]
    x, a, qkv, o, x1, a2, z, slope, attn_w, mlp_w = kept
    names = ("x", "a", "qkv", "o", "x1", "a2", "z", "slope", "attn", "mlp")

    def fetch(depth, *wanted):
        if depth < 0:
            return
        for name in wanted:
            n = names.index(name)
            pltpu.make_async_copy(held[n].at[depth], kept[n], sems.at[n]).start()

    def arrive(depth, *wanted):
        for name in wanted:
            n = names.index(name)
            pltpu.make_async_copy(held[n].at[depth], kept[n], sems.at[n]).wait()

    fetch(L - 1, "mlp", "slope", "a2", "z", "x1", "o", "attn", "qkv", "a", "x")
    mixed_copy = pltpu.make_async_copy(mixed_h, mixed, sems.at[len(names)])
    mixed_copy.start()
    due = {}
    if sharded:
        grad_patch, grad_attn, grad_mlp, grad_small, grad_norm, heads_all, head_rows, head_sum, gathered, squares, *refs = refs
        buffers, refs = refs[:16], refs[16:]
        send_sems, recv_sems, head_send, head_recv, last_send, last_recv = refs
        place = Place()
        mine = (place.z, place.y, place.x, place.core)

        def count(total):
            flat = total.reshape(-1, D)
            squares[0:1, :] += jnp.sum(flat * flat, axis=0, keepdims=True)

        def share_patch(total):
            patch_share[...] = total[: patch_share.shape[0]]
            count(total)

        def share_attn(depth, total):
            attn_share[depth] = total
            count(total)

        def share_mlp(depth, total):
            mlp_share[depth] = total
            count(total)

        def share_small(total):
            gathered[mine + (slice(None), slice(0, D))] = total

        scatter = Scatter(
            place,
            scatter_pieces(
                (grad_patch, grad_attn, grad_mlp, grad_small),
                *(buffers[4 * n : 4 * n + 4] for n in range(4)),
                (share_patch, share_attn, share_mlp, share_small),
            ),
            send_sems,
            recv_sems,
        )
        heads = Gather(
            place,
            [lambda z, y, x, core: heads_all.at[z, y, x, core]],
            head_send,
            head_recv,
        )
        plan = [(HEAD_DUE, 0, heads, 0)]
        for turn in range(L):
            final = turn == L - 1
            plan.append((ATTN_DUE_LAST if final else ATTN_DUE, turn, scatter, 2 * turn + 1))
            plan.append((MLP_DUE_LAST if final else MLP_DUE, turn, scatter, 2 * turn))
        plan += [(LAST_DUE, L - 1, scatter, piece) for piece in (PATCH_PIECE, SMALL_PIECE)]
        for times, turn, who, piece in plan:
            for stage in range(5):
                due.setdefault(10 * turn + times[stage], []).append((who, piece, stage + 1))
        squares[...] = jnp.zeros_like(squares)
        packed = [dlogits[:, HEAD_LANES:], jnp.zeros((8, HEAD_AT - 2 * C), F32), feature[...]]
        packed = jnp.concatenate(packed + [jnp.zeros((8, 2 * HEAD_LANES - HEAD_AT - D), F32)], axis=1)
        heads_all[mine] = jnp.concatenate([dlogits[:, :HEAD_LANES], packed], axis=0).astype(BF16)
        greet(place.partners())

    def point(now):
        for who, piece, stage in due.pop(now, ()):
            who.step(piece, stage)

    point(-1)
    dx[...] = jnp.zeros((ALL, D), F32)
    for kind in range(2):
        for image in range(IMG):
            row = image * ROWS + NPATCH + kind
            dx[row : row + 1, :] = dtop[kind * IMG + image : kind * IMG + image + 1, :]
    grad_norm[...] = jnp.zeros((16, D), F32)
    for turn in range(L):
        depth = L - 1 - turn
        start = 10 * turn
        round_rows(dx, low)
        arrive(depth, "mlp", "slope", "a2", "z")
        total = None
        for m in range(BLOCKS):
            at = (m // 2, m % 2)
            grad_gelu = nn(low[...], mlp_w[(1,) + at].reshape(D, D))
            grad_hidden = (grad_gelu * slope[m].astype(F32)).astype(BF16)
            grad_mlp[(depth, 0) + at] = tn(a2[...], grad_hidden).astype(BF16).reshape(Z, Y, 48, D)
            grad_mlp[(depth, 1) + at] = tn(low[...], z[m]).astype(BF16).reshape(Z, Y, 48, D)
            term = nt(grad_hidden, mlp_w[(0,) + at].reshape(D, D))
            dy[...] = term if m == 0 else dy[...] + term
            point(start + m)
        fetch(depth - 1, "mlp", "slope", "a2", "z")
        arrive(depth, "x1", "o", "attn")
        grad_in, gain, shift = norm_backward(dy[...], x1[...], norms[4 * depth + 2 : 4 * depth + 3, :])
        grad_norm[4 * depth + 2 : 4 * depth + 3, :] = gain
        grad_norm[4 * depth + 3 : 4 * depth + 4, :] = shift
        dx[...] += grad_in
        round_rows(dx, low)
        point(start + 4)
        grad_attn[depth, 3] = tn(low[...], o[...]).astype(BF16).reshape(Y, X, CORES, 48, D)
        dout[...] = nn(low[...], attn_w[3].reshape(D, D)).astype(BF16)
        fetch(depth - 1, "x1", "o")
        arrive(depth, "qkv")
        for image in range(IMG):
            for pair in range(3):
                attend_backward(qkv, dout, dqkv, image, pair)
            point(start + 5 + image)
        fetch(depth - 1, "qkv")
        arrive(depth, "a", "x")
        for n in range(3):
            part = dqkv[:, D * n : D * n + D]
            grad_attn[depth, n] = tn(part, a[...]).astype(BF16).reshape(Y, X, CORES, 48, D)
        point(start + 8)
        total = None
        for n in range(3):
            term = nn(dqkv[:, D * n : D * n + D], attn_w[n].reshape(D, D))
            total = term if total is None else total + term
        fetch(depth - 1, "attn", "a")
        grad_in, gain, shift = norm_backward(total, x[...], norms[4 * depth : 4 * depth + 1, :])
        grad_norm[4 * depth : 4 * depth + 1, :] = gain
        grad_norm[4 * depth + 1 : 4 * depth + 2, :] = shift
        dx[...] += grad_in
        fetch(depth - 1, "x")
        point(start + 9)
    total = dx[0:ROWS] + dx[ROWS : 2 * ROWS] + dx[2 * ROWS :]
    round_rows(dx, low)
    mixed_copy.wait()
    patch = tn(mixed[...], low[...])
    rows = PATCH_DIM // (Z * Y * X * CORES)
    for n in range(Z * Y * X * CORES):
        block = jnp.concatenate([patch[rows * n : rows * n + rows], jnp.zeros((32 - rows, D), F32)], axis=0)
        grad_patch[n // 8, n // 4 % 2, n // 2 % 2, n % 2] = block.astype(BF16)
    if not sharded:
        grad_pos[...] = total
        return
    small = [total[8 * n : 8 * n + 8] for n in range(ROWS // 8)]
    small += [grad_norm[0:8, :], jnp.concatenate([grad_norm[8:12, :], dnorm[0:2, :], jnp.zeros((2, D), F32)], axis=0)]
    small.append(jnp.concatenate([loss[...], jnp.zeros((8, D - 128), F32)], axis=1))
    for n in range(Z * Y * X * CORES):
        grad_small[n // 8, n // 4 % 2, n // 2 % 2, n % 2] = small[n] if n < len(small) else jnp.zeros((8, D), F32)
    left = sorted(due)
    for now in left[:2]:
        point(now)
    per_plane = head_rows.shape[0] // Z

    def unpack(n, carry):
        plane = heads_all[n].astype(F32).reshape(Y * X * CORES, 16, HEAD_LANES)
        for part in range(2):
            block = plane[:, 8 * part : 8 * part + 8].reshape(per_plane, HEAD_LANES)
            lanes = slice(part * HEAD_LANES, (part + 1) * HEAD_LANES)
            head_rows[pl.ds(n * per_plane, per_plane), lanes] = block.astype(BF16)
        return carry

    lax.fori_loop(0, Z, unpack, 0)
    features = head_rows[:, HEAD_AT : HEAD_AT + D]
    for n in range(0, 2 * C, 512):
        lanes = slice(n, min(n + 512, 2 * C))
        part = tn(head_rows[:, lanes], features)
        head_sum[lanes, :] = part
        squares[1:2, :] += jnp.sum(part * part, axis=0, keepdims=True)
    head_copy = pltpu.make_async_copy(head_sum, head_out, sems.at[len(names)])
    head_copy.start()
    for now in left[2:]:
        point(now)
    own = jnp.sum(squares[0:1, :], axis=(0, 1), keepdims=True)
    gathered[mine + (slice(None), slice(D, D + 128))] = jnp.broadcast_to(own, (8, 128))
    last = Gather(
        place, [lambda z, y, x, core: gathered.at[z, y, x, core]], last_send, last_recv, direct=True
    )
    for stage in range(1, 6):
        last.step(0, stage)
    blocks = [gathered[n // 8, n // 4 % 2, n // 2 % 2, n % 2] for n in range(Z * Y * X * CORES)]
    pos = jnp.concatenate([block[:, :D] for block in blocks[: ROWS // 8]], axis=0)
    norm = jnp.concatenate([block[:, :D] for block in blocks[ROWS // 8 : ROWS // 8 + 2]], axis=0)
    pos_sum[...] = jnp.concatenate([pos[NPATCH:TOK], pos[:NPATCH]], axis=0)
    norm_sum[...] = norm[: 4 * L + 2]
    total = blocks[0][:, D:]
    for block in blocks[1:]:
        total = total + block[:, D:]
    rest = jnp.sum(pos * pos, axis=0, keepdims=True) + jnp.sum(norm * norm, axis=0, keepdims=True) + squares[1:2, :]
    total = total[0:1, :] + jnp.sum(rest, axis=(0, 1), keepdims=True)
    norm_all = jnp.sqrt(total)
    stats[...] = jnp.concatenate(
        [blocks[ROWS // 8 + 2][0:1, :128], norm_all, jnp.minimum(1.0, MAX_NORM / norm_all), jnp.zeros((5, 128), F32)],
        axis=0,
    )
    head_copy.wait()
    scatter.finish()
    heads.finish()
    last.finish()


def backward(sharded, *operands):
    full = ((PATCH_SHAPE, BF16), (ATTN_SHAPE, BF16), (MLP_SHAPE, BF16))
    if sharded:
        outs = (
            ((PATCH_DIM // (Z * Y * X * CORES), D), F32),
            ((L, 48, D), F32),
            ((L, 2, 48, D), F32),
            ((2 * C, D), F32),
            ((TOK, D), F32),
            ((4 * L + 2, D), F32),
            ((8, 128), F32),
        )
    else:
        outs = full + (((16, D), F32), ((ROWS, D), F32))
    scratch = [((ALL, D), F32), ((ALL, D), F32), ((ALL, D), BF16), ((ALL, D), BF16), ((ALL, 3 * D), BF16), SAVED[0]]
    scratch = [pltpu.VMEM(*entry) for entry in scratch]
    scratch += [pltpu.VMEM(shape[1:], kind) for shape, kind in SAVED[1:]]
    scratch += [pltpu.SemaphoreType.DMA((11,))]
    if sharded:
        scratch += [pltpu.VMEM(*entry) for entry in full]
        scratch += [
            pltpu.VMEM(SMALL_SHAPE, F32),
            pltpu.VMEM((16, D), F32),
            pltpu.VMEM((Z, Y, X, CORES, 16, HEAD_LANES), BF16),
            pltpu.VMEM((Z * Y * X * CORES * 8, 2 * HEAD_LANES), BF16),
            pltpu.VMEM((2 * C, D), F32),
            pltpu.VMEM((Z, Y, X, CORES, 8, D + 128), F32),
            pltpu.VMEM((8, D), F32),
        ]
        scratch += scatter_scratch()
        scratch += [pltpu.SemaphoreType.DMA((N_GRADS, 8))] * 2
        scratch += [pltpu.SemaphoreType.DMA((1, PIECES))] * 4
    params = dict(collective_id=1, has_side_effects=True) if sharded else {}
    return pl.pallas_call(
        lambda *refs: backward_kernel(sharded, *refs),
        out_shape=[jax.ShapeDtypeStruct(*entry) for entry in outs],
        in_specs=[VMEM] * 2 + [HBM] * 11 + [VMEM] * (4 if sharded else 0),
        out_specs=[HBM if entry == ((2 * C, D), F32) else VMEM for entry in outs],
        scratch_shapes=scratch,
        compiler_params=pltpu.CompilerParams(vmem_limit_bytes=63 * 2**20, **params),
        name="backward",
    )(*operands)


def adam_kernel(*refs):
    stats_h, refs = refs[0], refs[1:]
    count = len(STEP_RATES)
    grads, weights, firsts, seconds = (refs[n * count : (n + 1) * count] for n in range(4))
    outs, refs = refs[4 * count : 7 * count], refs[7 * count :]
    stats, buffers, (stats_sem, in_sems, out_sems) = refs[0], refs[1 : 1 + 4 * count], refs[1 + 4 * count :]
    stats_copy = pltpu.make_async_copy(stats_h, stats, stats_sem.at[0])
    stats_copy.start()
    chunks = []
    for n in ADAM_ORDER:
        rows = grads[n].shape[0]
        step = HEAD_ROWS if rows > HEAD_ROWS else rows
        chunks += [(n, pl.ds(first, step)) for first in range(0, rows, step)]
    loads = []
    for at, (n, rows) in enumerate(chunks):
        sources = (weights[n], firsts[n], seconds[n], grads[n])
        loads.append(
            [
                pltpu.make_async_copy(source.at[rows], buffers[4 * n + k].at[rows], in_sems.at[at, k])
                for k, source in enumerate(sources)
            ]
        )
        for copy in loads[-1]:
            copy.start()
    stats_copy.wait()
    factor = stats[2:3, 0:1]
    stores = []
    for at, (n, rows) in enumerate(chunks):
        for copy in loads[at]:
            copy.wait()
        weight, first, second, grad = (buffers[4 * n + k].at[rows] for k in range(4))
        old = weight[...]
        clipped = grad[...] * factor.reshape((1,) * old.ndim)
        new_first = BETA_ONE * first[...] + (1.0 - BETA_ONE) * clipped
        new_second = BETA_TWO * second[...] + (1.0 - BETA_TWO) * clipped * clipped
        root = jnp.sqrt(new_second * (1.0 / (1.0 - BETA_TWO**ADAM_STEP))) + ADAM_EPS
        move = new_first * (1.0 / (1.0 - BETA_ONE**ADAM_STEP)) / root
        weight[...] = old - STEP_RATES[n] * (move + DECAY * old)
        first[...] = new_first
        second[...] = new_second
        for k in range(3):
            copy = pltpu.make_async_copy(
                buffers[4 * n + k].at[rows], outs[k * count + n].at[rows], out_sems.at[at, k]
            )
            copy.start()
            stores.append(copy)
    for copy in stores:
        copy.wait()


HEAD_ROWS = 400
ADAM_ORDER = (4, 2, 1, 3, 0, 5)


def adam(stats, grads, weights, firsts, seconds):
    shapes = [weight.shape for weight in weights]
    chunk_count = len(shapes) - 1 + 2 * C // HEAD_ROWS
    return pl.pallas_call(
        adam_kernel,
        out_shape=[jax.ShapeDtypeStruct(shape, F32) for shape in shapes] * 3,
        in_specs=[HBM] * (1 + 4 * len(shapes)),
        out_specs=[HBM] * (3 * len(shapes)),
        scratch_shapes=[pltpu.VMEM((8, 128), F32)]
        + [pltpu.VMEM(shape, F32) for shape in shapes for _ in range(4)]
        + [pltpu.SemaphoreType.DMA((1,))]
        + [pltpu.SemaphoreType.DMA((chunk_count, 4)), pltpu.SemaphoreType.DMA((chunk_count, 3))],
        compiler_params=pltpu.CompilerParams(vmem_limit_bytes=63 * 2**20),
        name="adam",
    )(stats, *grads, *weights, *firsts, *seconds)


def per_device(
    patches, partners, mix_weight, labels, teacher_logits,
    patch_weight, attn_weight, mlp_weight, positions, head_weight, norm_params,
    patch_first, attn_first, mlp_first, pos_first, head_first, norm_first,
    patch_second, attn_second, mlp_second, pos_second, head_second, norm_second,
):
    axes = ("dp", "mp")
    image_count = patches.shape[0] * lax.axis_size("dp") * lax.axis_size("mp")
    sharded = (lax.axis_size("dp"), lax.axis_size("mp")) == (Z * Y, X * CORES)
    attn_t = jnp.swapaxes(attn_weight, 1, 2)
    if sharded:
        weights_in = (patch_weight, attn_t, mlp_weight)
    else:
        patch_low = lax.all_gather(patch_weight.astype(BF16), axes, axis=0, tiled=True)
        attn_low = lax.all_gather(attn_t.astype(BF16), axes, axis=1, tiled=True)
        mlp_low = lax.all_gather(mlp_weight.astype(BF16), "dp", axis=2, tiled=True)
        mlp_low = lax.all_gather(mlp_low, "mp", axis=2, tiled=False)
        weights_in = (patch_low, attn_low.reshape(ATTN_SHAPE), mlp_low.reshape(MLP_SHAPE))
    results = forward(
        image_count, sharded, partners, mix_weight, labels, patches, teacher_logits, positions,
        head_weight.T, norm_params, *weights_in,
    )
    saved, (loss, feature, dlogits, dtop, dnorm) = results[: len(SAVED)], results[len(SAVED) :]
    operands = (dtop, norm_params, *saved)
    if sharded:
        patch_share, attn_share, mlp_share, head_sum, pos_sum, norm_sum, stats = backward(
            True, *operands, loss, feature, dlogits, dnorm
        )
        loss_sum, global_norm = stats[0, 0], stats[1, 0]
        mlp_share = mlp_share.reshape(mlp_weight.shape)
    else:
        grad_patch, grad_attn, grad_mlp, grad_norm, grad_pos = backward(False, *operands)
        rows = PATCH_DIM // (Z * Y * X * CORES)
        grad_patch = grad_patch.reshape(-1, 32, D)[:, :rows].reshape(PATCH_DIM, D).astype(F32)
        patch_share = lax.psum_scatter(grad_patch, axes, scatter_dimension=0, tiled=True)
        grad_attn = grad_attn.reshape(L, 4 * D, D).astype(F32)
        attn_share = lax.psum_scatter(grad_attn, axes, scatter_dimension=1, tiled=True)
        grad_mlp = grad_mlp.reshape(L, 2, BLOCKS, D, D).astype(F32)
        mlp_share = lax.psum_scatter(grad_mlp, "mp", scatter_dimension=2, tiled=True)
        mlp_share = lax.psum_scatter(mlp_share, "dp", scatter_dimension=3, tiled=True)
        mlp_share = mlp_share.reshape(mlp_weight.shape)
        features = lax.all_gather(feature.astype(BF16), axes, axis=0, tiled=True)
        all_dlogits = lax.all_gather(dlogits.astype(BF16), axes, axis=0, tiled=True)
        head_sum = tn(all_dlogits, features)
        grad_norms = jnp.concatenate([grad_norm[: 4 * L], dnorm[:2]], axis=0)
        grad_pos = jnp.concatenate([grad_pos[NPATCH:TOK], grad_pos[:NPATCH]], axis=0)
        pos_sum, norm_sum, loss_sum = lax.psum((grad_pos, grad_norms, loss[0, 0]), axes)
        own_squares = sum(jnp.sum(share * share) for share in (patch_share, attn_share, mlp_share))
        shared = sum(jnp.sum(total * total) for total in (pos_sum, head_sum, norm_sum))
        global_norm = jnp.sqrt(lax.psum(own_squares, axes) + shared)
        stats = jnp.full((8, 128), jnp.minimum(1.0, MAX_NORM / global_norm))
    weights = (patch_weight, attn_weight, mlp_weight, positions, head_weight, norm_params)
    firsts = (patch_first, attn_first, mlp_first, pos_first, head_first, norm_first)
    seconds = (patch_second, attn_second, mlp_second, pos_second, head_second, norm_second)

    def turned(arrays):
        return (arrays[0], jnp.swapaxes(arrays[1], 1, 2), arrays[2], arrays[3], arrays[4].T, arrays[5])

    grads = (patch_share, attn_share, mlp_share, pos_sum, head_sum, norm_sum)
    updated = adam(stats, grads, turned(weights), turned(firsts), turned(seconds))
    return (loss_sum, global_norm, *(out for n in range(3) for out in turned(updated[6 * n : 6 * n + 6])))


def solution(mesh):
    images = (P(("dp", "mp"), None, None), P(("dp", "mp")), P(("dp", "mp")), P(("dp", "mp")), P(("dp", "mp"), None))
    weights = (P(("dp", "mp"), None), P(None, None, ("dp", "mp")), P(None, None, "dp", "mp"), P(), P(), P())
    return jax.shard_map(
        per_device,
        mesh=mesh,
        in_specs=images + weights * 3,
        out_specs=(P(), P()) + weights * 3,
        check_vma=False,
    )
```

```python
import jax
import jax.numpy as jnp
from jax import lax
from jax.experimental import pallas as pl
from jax.experimental.pallas import tpu as pltpu
from jax.sharding import PartitionSpec as P

D = 384
C = 1000
PATCH_DIM = 768
NPATCH = 196
L = 3
TOK = 198
IMG = 3
ROWS = 208
ALL = IMG * ROWS
BLOCKS = 4

Z = 4
Y = 2
X = 2
CORES = 2
EVERY = slice(0, 2)
PIECES = 11

LN_EPS = 1e-06
TEMPER = 3.0
MAX_NORM = 0.02
BETA_ONE = 0.9
BETA_TWO = 0.999
STEP_RATES = (0.05, 0.05, 0.05, 0.4, 0.12, 0.5)
DECAY = 0.05
ADAM_EPS = 1e-08
ADAM_STEP = 10.0
LOWEST = -1e30

BF16 = jnp.bfloat16
F32 = jnp.float32
VMEM = pl.BlockSpec(memory_space=pltpu.VMEM)
SMEM = pl.BlockSpec(memory_space=pltpu.SMEM)
HBM = pl.BlockSpec(memory_space=pl.ANY)
MESH = pl.DeviceIdType.MESH


def nn(left, right):
    return jnp.dot(left, right, preferred_element_type=F32)


def nt(left, right):
    return lax.dot_general(left, right, (((1,), (1,)), ((), ())), preferred_element_type=F32)


def tn(left, right):
    return lax.dot_general(left, right, (((0,), (0,)), ((), ())), preferred_element_type=F32)


def unit_norm(inputs):
    centred = inputs - jnp.mean(inputs, axis=-1, keepdims=True)
    inverse = lax.rsqrt(jnp.mean(centred * centred, axis=-1, keepdims=True) + LN_EPS)
    return centred * inverse, inverse


def norm_backward(grad_out, inputs, gain):
    normed, inverse = unit_norm(inputs)
    grad_gain = jnp.sum(grad_out * normed, axis=0, keepdims=True)
    grad_shift = jnp.sum(grad_out, axis=0, keepdims=True)
    scaled = grad_out * gain
    grad_in = inverse * (
        scaled
        - jnp.mean(scaled, axis=-1, keepdims=True)
        - normed * jnp.mean(scaled * normed, axis=-1, keepdims=True)
    )
    return grad_in, grad_gain, grad_shift


class Place:
    def __init__(self):
        dp, mp = lax.axis_index("dp"), lax.axis_index("mp")
        self.z, self.y = dp // Y, dp % Y
        self.x, self.core = mp // CORES, mp % CORES

    def at(self, dz=0, dy=0, dx=0, dcore=0):
        z = lax.rem(self.z + dz, Z)
        y = 1 - self.y if dy else self.y
        x = 1 - self.x if dx else self.x
        core = 1 - self.core if dcore else self.core
        return {"dp": z * Y + y, "mp": x * CORES + core}

    def partners(self):
        column = [self.at(dz=step) for step in range(1, Z)]
        return column + [self.at(dx=1), self.at(dy=1), self.at(dcore=1), self.at(dy=1, dx=1)]


def greet(partners):
    for partner in partners:
        pl.semaphore_signal(pltpu.get_barrier_semaphore(), inc=1, device_id=partner, device_id_type=MESH)


def await_greetings(partners):
    pl.semaphore_wait(pltpu.get_barrier_semaphore(), len(partners))


class Gather:
    def __init__(self, place, pieces, send_sems, recv_sems, planes=(), direct=False):
        self.place, self.pieces, self.planes, self.direct = place, pieces, planes, direct
        self.send_sems, self.recv_sems = send_sems, recv_sems
        self.started = []
        self.done = set()

    def copy(self, piece, n, region, target):
        view = self.pieces[piece](*region)
        return pltpu.make_async_remote_copy(
            src_ref=view,
            dst_ref=view,
            send_sem=self.send_sems.at[piece, n],
            recv_sem=self.recv_sems.at[piece, n],
            device_id=target,
            device_id_type=MESH,
        )

    def send(self, piece, n, region, **offset):
        copy = self.copy(piece, n, region, self.place.at(**offset))
        copy.start()
        self.started.append(copy)

    def recv(self, piece, n, region):
        self.copy(piece, n, region, self.place.at(dcore=1)).wait_recv()

    def step(self, piece, stage):
        if (piece, stage) in self.done:
            return
        self.done.add((piece, stage))
        z, y, x, core = self.place.z, self.place.y, self.place.x, self.place.core
        far_y, far_x, sibling = 1 - y, 1 - x, 1 - core
        column, low, high = slice(0, Z), slice(0, Z // 2), slice(Z // 2, Z)
        if piece in self.planes:
            if stage == 1:
                self.send(piece, 3, (z, y, x, core), dx=1)
                self.send(piece, 4, (z, y, x, core), dy=1)
                self.send(piece, 6, (z, y, x, core), dy=1, dx=1)
            if stage == 2:
                self.recv(piece, 3, (z, y, far_x, core))
                self.recv(piece, 4, (z, far_y, x, core))
                self.recv(piece, 6, (z, far_y, far_x, core))
                for hop in range(1, Z):
                    self.send(piece, hop - 1, (z, EVERY, EVERY, core), dz=hop)
            if stage == 4:
                for hop in range(1, Z):
                    self.recv(piece, hop - 1, (lax.rem(z + Z - hop, Z), EVERY, EVERY, core))
                self.send(piece, 5, (column, EVERY, EVERY, core), dcore=1)
            if stage == 5:
                self.recv(piece, 5, (column, EVERY, EVERY, sibling))
            return
        if stage == 1:
            for hop in range(1, Z):
                self.send(piece, hop - 1, (z, y, x, core), dz=hop)
        if self.direct:
            if stage == 2:
                for hop in range(1, Z):
                    self.recv(piece, hop - 1, (lax.rem(z + Z - hop, Z), y, x, core))
                self.send(piece, 3, (column, y, x, core), dx=1)
                self.send(piece, 4, (column, y, x, core), dy=1)
                self.send(piece, 6, (column, y, x, core), dy=1, dx=1)
            if stage == 4:
                self.recv(piece, 3, (column, y, far_x, core))
                self.recv(piece, 4, (column, far_y, x, core))
                self.recv(piece, 6, (column, far_y, far_x, core))
                self.send(piece, 5, (column, EVERY, EVERY, core), dcore=1)
            if stage == 5:
                self.recv(piece, 5, (column, EVERY, EVERY, sibling))
            return
        if stage == 2:
            for hop in range(1, Z):
                self.recv(piece, hop - 1, (lax.rem(z + Z - hop, Z), y, x, core))
            self.send(piece, 3, (column, y, x, core), dx=1)
            self.send(piece, 4, (column, y, x, core), dy=1)
            self.send(piece, 5, (column, y, x, core), dcore=1)
        if stage == 3:
            self.recv(piece, 3, (column, y, far_x, core))
            self.send(piece, 6, (low, y, far_x, core), dy=1)
            self.send(piece, 8, (column, y, far_x, core), dcore=1)
            self.recv(piece, 4, (column, far_y, x, core))
            self.send(piece, 7, (high, far_y, x, core), dx=1)
            self.send(piece, 9, (column, far_y, x, core), dcore=1)
        if stage == 4:
            self.recv(piece, 6, (low, far_y, far_x, core))
            self.recv(piece, 7, (high, far_y, far_x, core))
            self.send(piece, 10, (column, far_y, far_x, core), dcore=1)
        if stage == 5:
            self.recv(piece, 5, (column, y, x, sibling))
            self.recv(piece, 8, (column, y, far_x, sibling))
            self.recv(piece, 9, (column, far_y, x, sibling))
            self.recv(piece, 10, (column, far_y, far_x, sibling))

    def finish(self):
        for copy in self.started:
            copy.wait_send()


def add_into(target, *terms):
    def body(n, carry):
        total = target[n].astype(F32)
        for term in terms:
            total = total + term[n].astype(F32)
        target[n] = total.astype(target.dtype)
        return carry

    lax.fori_loop(0, target.shape[0], body, 0)


class Scatter:
    def __init__(self, place, pieces, send_sems, recv_sems):
        self.place, self.pieces = place, pieces
        self.send_sems, self.recv_sems = send_sems, recv_sems
        self.started = []

    def copy(self, piece, n, source, target, **offset):
        return pltpu.make_async_remote_copy(
            src_ref=source,
            dst_ref=target,
            send_sem=self.send_sems.at[piece, n],
            recv_sem=self.recv_sems.at[piece, n],
            device_id=self.place.at(**offset),
            device_id_type=MESH,
        )

    def send(self, piece, n, source, target, **offset):
        copy = self.copy(piece, n, source, target, **offset)
        copy.start()
        self.started.append(copy)

    def recv(self, piece, n, target):
        self.copy(piece, n, target, target, dcore=1).wait_recv()
        return target

    def step(self, piece, stage):
        z, y, x, core = self.place.z, self.place.y, self.place.x, self.place.core
        far_y, far_x, sibling = 1 - y, 1 - x, 1 - core
        column, low, high = slice(0, Z), slice(0, Z // 2), slice(Z // 2, Z)
        part = self.pieces[piece]
        grad = part["grad"]
        if stage == 1:
            self.send(piece, 0, grad(column, EVERY, EVERY, sibling), part["half"], dcore=1)
        if stage == 2:
            add_into(grad(column, EVERY, EVERY, core), self.recv(piece, 0, part["half"]))
            self.send(piece, 1, grad(low, far_y, far_x, core), part["corner"](0), dy=1)
            self.send(piece, 2, grad(high, far_y, far_x, core), part["corner"](1), dx=1)
        if stage == 3:
            add_into(grad(low, y, far_x, core), self.recv(piece, 1, part["corner"](0)))
            self.send(piece, 3, grad(column, y, far_x, core), part["side"](0), dx=1)
            add_into(grad(high, far_y, x, core), self.recv(piece, 2, part["corner"](1)))
            self.send(piece, 4, grad(column, far_y, x, core), part["side"](1), dy=1)
        if stage == 4:
            sides = [self.recv(piece, 3 + n, part["side"](n)) for n in range(2)]
            add_into(grad(column, y, x, core), *sides)
            for hop in range(1, Z):
                self.send(
                    piece, 4 + hop, grad(lax.rem(z + hop, Z), y, x, core), part["hop"](hop - 1), dz=hop
                )
        if stage == 5:
            total = grad(z, y, x, core)[...].astype(F32)
            for hop in range(1, Z):
                total = total + self.recv(piece, 4 + hop, part["hop"](hop - 1))[...].astype(F32)
            part["share"](total)

    def finish(self):
        for copy in self.started:
            copy.wait_send()


def round_rows(source, target):
    def body(n, carry):
        rows = pl.ds(n * ROWS, ROWS)
        target[rows, :] = source[rows, :].astype(target.dtype)
        return carry

    lax.fori_loop(0, IMG, body, 0)


def head_lanes(shape, head):
    lane = lax.broadcasted_iota(jnp.int32, shape, len(shape) - 1)
    return lane < 64 if head == 0 else lane >= 64


def attend(qkv, out, image, pair):
    rows = slice(image * ROWS, (image + 1) * ROWS)
    lanes = 128 * pair
    queries = qkv[rows, lanes : lanes + 128] * BF16(0.125)
    keys = qkv[rows, D + lanes : D + lanes + 128]
    values = qkv[rows, 2 * D + lanes : 2 * D + lanes + 128]
    key_lane = lax.broadcasted_iota(jnp.int32, (1, ROWS), 1)
    parts = []
    for head in range(2):
        scores = nt(jnp.where(head_lanes((ROWS, 128), head), queries, BF16(0)), keys)
        scores = jnp.where(key_lane < TOK, scores, LOWEST)
        weights = jnp.exp(scores - jnp.max(scores, axis=-1, keepdims=True))
        inverse = 1.0 / jnp.sum(weights, axis=-1, keepdims=True)
        parts.append(nn(weights.astype(BF16), values) * inverse)
    out[rows, lanes : lanes + 128] = jnp.where(
        head_lanes((ROWS, 128), 0), parts[0], parts[1]
    ).astype(BF16)


def attend_backward(qkv, grad_out, grad_qkv, image, pair):
    rows = slice(image * ROWS, (image + 1) * ROWS)
    lanes = 128 * pair
    queries = qkv[rows, lanes : lanes + 128] * BF16(0.125)
    keys = qkv[rows, D + lanes : D + lanes + 128]
    values = qkv[rows, 2 * D + lanes : 2 * D + lanes + 128]
    grad = grad_out[rows, lanes : lanes + 128]
    key_row = lax.broadcasted_iota(jnp.int32, (ROWS, 1), 0)
    grad_q, grad_k, grad_v = [], [], []
    for head in range(2):
        own = head_lanes((ROWS, 128), head)
        scores = nt(jnp.where(own, keys, BF16(0)), queries)
        scores = jnp.where(key_row < TOK, scores, LOWEST)
        probs = jnp.exp(scores - jnp.max(scores, axis=0, keepdims=True))
        probs = probs * (1.0 / jnp.sum(probs, axis=0, keepdims=True))
        grad_probs = nt(jnp.where(own, values, BF16(0)), grad)
        total = jnp.sum(probs * grad_probs, axis=0, keepdims=True)
        grad_scores = (probs * (grad_probs - total)).astype(BF16)
        grad_v.append(nn(probs.astype(BF16), grad))
        grad_k.append(nn(grad_scores, queries))
        grad_q.append(tn(grad_scores, keys))
    first = head_lanes((ROWS, 128), 0)
    grad_qkv[rows, lanes : lanes + 128] = (
        jnp.where(first, grad_q[0], grad_q[1]) * 0.125
    ).astype(BF16)
    grad_qkv[rows, D + lanes : D + lanes + 128] = jnp.where(first, grad_k[0], grad_k[1]).astype(
        BF16
    )
    grad_qkv[rows, 2 * D + lanes : 2 * D + lanes + 128] = jnp.where(
        first, grad_v[0], grad_v[1]
    ).astype(BF16)


def mix_images(partners, mix, patches, mixed):
    for image in range(IMG):
        total = None
        for other in range(IMG):
            share = jnp.where(partners[image] == other, 1.0 - mix[image], 0.0)
            if image == other:
                share = share + mix[image]
            term = share * patches[other].astype(F32)
            total = term if total is None else total + term
        padding = jnp.zeros((ROWS - NPATCH, PATCH_DIM), F32)
        mixed[image * ROWS : (image + 1) * ROWS, :] = jnp.concatenate(
            [total, padding], axis=0
        ).astype(BF16)


def head_masks():
    row = lax.broadcasted_iota(jnp.int32, (8, 2 * C), 0)
    lane = lax.broadcasted_iota(jnp.int32, (8, 2 * C), 1)
    is_class = row < IMG
    low_lane = jnp.where(is_class, 0, C)
    high_lane = jnp.where(is_class, C, jnp.where(row < 2 * IMG, 2 * C, 0))
    return row, lane, is_class, (lane >= low_lane) & (lane < high_lane)


def log_softmax(values, used):
    values = jnp.where(used, values, LOWEST)
    shifted = values - jnp.max(values, axis=-1, keepdims=True)
    return shifted - jnp.log(jnp.sum(jnp.exp(shifted), axis=-1, keepdims=True))


def prepare_loss(partners, mix, labels, teacher, head, head_low, wanted, wanted_log):
    def body(n, carry):
        rows = pl.ds(n * 400, 400)
        head_low[rows, :] = head[rows, :].astype(BF16)
        return carry

    lax.fori_loop(0, 2 * C // 400, body, 0)
    row, lane, is_class, used = head_masks()
    taught = jnp.concatenate([jnp.zeros((IMG, C), F32), teacher[...]], axis=1)
    taught = jnp.concatenate(
        [jnp.zeros((IMG, 2 * C), F32), taught, jnp.zeros((8 - 2 * IMG, 2 * C), F32)], axis=0
    )
    teacher_log = log_softmax(taught / TEMPER, used)
    target = jnp.zeros((8, 2 * C), F32)
    for image in range(IMG):
        partner_label = labels[IMG - 1]
        for other in range(IMG - 1):
            partner_label = jnp.where(partners[image] == other, labels[other], partner_label)
        ours = jnp.where(lane == labels[image], mix[image], 0.0) + jnp.where(
            lane == partner_label, 1.0 - mix[image], 0.0
        )
        target = target + jnp.where(row == image, ours, 0.0)
    wanted[...] = jnp.where(is_class, target, jnp.exp(teacher_log))
    wanted_log[...] = teacher_log


def head_and_loss(
    image_count, stream, norms, head_low, wanted, wanted_log, loss, feature, dlogits, dtop, dnorm
):
    picked = [
        stream[image * ROWS + NPATCH + kind : image * ROWS + NPATCH + kind + 1, :]
        for kind in range(2)
        for image in range(IMG)
    ]
    top = jnp.concatenate(picked + [jnp.zeros((2, D), F32)], axis=0)
    gain = norms[4 * L : 4 * L + 1, :]
    normed, _ = unit_norm(top)
    features = (normed * gain + norms[4 * L + 1 : 4 * L + 2, :]).astype(BF16)
    _, _, is_class, used = head_masks()
    logits = nt(features, head_low[...])
    student_log = log_softmax(jnp.where(is_class, logits, logits / TEMPER), used)
    share = wanted[...]
    terms = jnp.where(
        is_class, -0.5 * share * student_log, 0.5 * TEMPER * TEMPER * share * (wanted_log[...] - student_log)
    )
    terms = jnp.where(used, terms, 0.0)
    loss[...] = jnp.broadcast_to(jnp.sum(terms, axis=(0, 1), keepdims=True), (8, 128))
    scale = jnp.where(is_class, 0.5 / image_count, 0.5 * TEMPER / image_count)
    grad_logits = (scale * jnp.where(used, jnp.exp(student_log) - share, 0.0)).astype(BF16)
    feature[...] = features.astype(F32)
    dlogits[...] = grad_logits.astype(F32)
    grad_top, grad_gain, grad_shift = norm_backward(nn(grad_logits, head_low[...]), top, gain)
    dtop[...] = grad_top
    dnorm[...] = jnp.concatenate([grad_gain, grad_shift, jnp.zeros((6, D), F32)], axis=0)


ATTN_SHAPE = (L, Z, Y, X, CORES, 48, D)
MLP_SHAPE = (L, 2, X, CORES, Z, Y, 48, D)
PATCH_SHAPE = (Z, Y, X, CORES, 32, D)
N_PIECES = 1 + 3 * L
PLANES = (1 + 3 * (L - 1),)
QUEUE = tuple(n for n in range(N_PIECES) if n not in PLANES)


def gather_views(patch_w, attn_w, mlp_w):
    def attn(depth):
        return lambda z, y, x, core: attn_w.at[depth, z, y, x, core]

    def mlp(depth, part):
        return lambda z, y, x, core: mlp_w.at[depth, part, x, core, z, y]

    views = [lambda z, y, x, core: patch_w.at[z, y, x, core]]
    for depth in range(L):
        views += [attn(depth), mlp(depth, 0), mlp(depth, 1)]
    return views


def forward_kernel(image_count, sharded, *refs):
    (
        partners, mix, labels, patches_h, teacher, pos, head_h, norms, patch_in, attn_in, mlp_in,
        mixed_h, x_h, a_h, qkv_h, o_h, x1_h, a2_h, z_h, slope_h, attn_h, mlp_h,
        loss, feature, dlogits, dtop, dnorm,
        mixed, x, a, qkv, o, x1, a2, z, slope, attn_w, mlp_w,
        patches, head, stream, patch_w, head_low, wanted, wanted_log, in_sems, out_sems, *rest,
    ) = refs
    outgoing = []
    if sharded:
        place = Place()
        greet(place.partners())

    def keep(source, target):
        copy = pltpu.make_async_copy(source, target, out_sems.at[len(outgoing)])
        copy.start()
        outgoing.append(copy)

    if sharded:
        patch_all, patch_s, attn_s, mlp_s, send_sems, recv_sems = rest
        loads = [(attn_in, attn_s), (mlp_in, mlp_s), (patch_in, patch_s)]
    else:
        loads = [(attn_in, attn_w), (mlp_in, mlp_w), (patch_in, patch_w)]
    loads += [(patches_h, patches), (head_h, head)]
    loads = [
        pltpu.make_async_copy(source, target, in_sems.at[n]) for n, (source, target) in enumerate(loads)
    ]
    for copy in loads:
        copy.start()

    if sharded:
        gather = Gather(place, gather_views(patch_all, attn_w, mlp_w), send_sems, recv_sems, planes=PLANES)
        mine = (place.z, place.y, place.x, place.core)
        loads[2].wait()
        patch_all[mine] = jnp.concatenate([patch_s[...], jnp.zeros((8, D), F32)], axis=0).astype(BF16)
        loads[0].wait()
        for depth in range(L):
            attn_w[(depth,) + mine] = attn_s[depth].astype(BF16)
        loads[1].wait()
        for depth in range(L):
            for part in range(2):
                mlp_w[depth, part, place.x, place.core, place.z, place.y] = mlp_s[depth, part].astype(BF16)
        await_greetings(place.partners())
        for piece in PLANES + QUEUE:
            gather.step(piece, 1)

    def ahead(n, stage):
        if sharded and n < len(QUEUE):
            gather.step(QUEUE[n], stage)

    def need(piece):
        if not sharded:
            return
        if piece in PLANES:
            for stage in (4, 5):
                gather.step(piece, stage)
            return
        n = QUEUE.index(piece)
        ahead(n + 1, 2)
        ahead(n, 3)
        ahead(n + 2, 2)
        ahead(n + 1, 3)
        ahead(n, 4)
        ahead(n, 5)

    def between(piece):
        if not sharded:
            return
        later = [n for n in range(len(QUEUE)) if QUEUE[n] > piece]
        if later:
            ahead(later[0] + 2, 2)
            ahead(later[0] + 1, 3)

    if sharded:
        ahead(0, 2)
        for piece in PLANES:
            gather.step(piece, 2)
        ahead(1, 2)
        ahead(0, 3)
    else:
        for n in range(3):
            loads[n].wait()
    loads[3].wait()
    mix_images(partners, mix, patches, mixed)
    keep(mixed, mixed_h)
    ahead(2, 2)
    loads[4].wait()
    prepare_loss(partners, mix, labels, teacher, head, head_low, wanted, wanted_log)
    need(0)
    if sharded:
        for n in range(Z * Y * X):
            block = patch_all[n // 4, n // 2 % 2, n % 2].astype(F32)
            patch_w[48 * n : 48 * n + 48, :] = jnp.concatenate([block[0, :24], block[1, :24]], axis=0).astype(BF16)
    embedded = nn(mixed[...], patch_w[...])
    added = jnp.concatenate([pos[2:TOK, :], pos[0:2, :], jnp.zeros((ROWS - TOK, D), F32)], axis=0)
    for image in range(IMG):
        rows = slice(image * ROWS, (image + 1) * ROWS)
        x[0, rows, :] = embedded[rows] + added
    for depth in range(L):
        norm = [norms[4 * depth + n : 4 * depth + n + 1, :] for n in range(4)]
        first = 1 + 3 * depth
        keep(x.at[depth], x_h.at[depth])
        a[depth] = (unit_norm(x[depth])[0] * norm[0] + norm[1]).astype(BF16)
        keep(a.at[depth], a_h.at[depth])
        need(first)
        for n in range(3):
            qkv[depth, :, D * n : D * n + D] = nt(a[depth], attn_w[depth, n].reshape(D, D)).astype(BF16)
        keep(qkv.at[depth], qkv_h.at[depth])
        keep(attn_w.at[depth], attn_h.at[depth])
        for image in range(IMG):
            for pair in range(3):
                attend(qkv.at[depth], o.at[depth], image, pair)
            if image == 1:
                between(first)
        keep(o.at[depth], o_h.at[depth])
        x1[depth] = x[depth] + nt(o[depth], attn_w[depth, 3].reshape(D, D))
        keep(x1.at[depth], x1_h.at[depth])
        a2[depth] = (unit_norm(x1[depth])[0] * norm[2] + norm[3]).astype(BF16)
        keep(a2.at[depth], a2_h.at[depth])
        need(first + 1)

        def widen(m, carry):
            hidden = nn(a2[depth], mlp_w[depth, 0, m // 2, lax.rem(m, 2)].reshape(D, D))
            phi = 0.5 * (1.0 + lax.erf(hidden * 2.0**-0.5))
            z[depth, m] = (hidden * phi).astype(BF16)
            density = jnp.exp(-0.5 * hidden * hidden) * 0.3989422804014327
            slope[depth, m] = (phi + hidden * density).astype(BF16)
            return carry

        lax.fori_loop(0, BLOCKS, widen, 0)
        keep(z.at[depth], z_h.at[depth])
        keep(slope.at[depth], slope_h.at[depth])
        need(first + 2)
        keep(mlp_w.at[depth], mlp_h.at[depth])
        total = x1[depth]
        for m in range(BLOCKS):
            total = total + nt(z[depth, m], mlp_w[depth, 1, m // 2, m % 2].reshape(D, D))
        if depth + 1 < L:
            x[depth + 1] = total
        else:
            stream[...] = total
    head_and_loss(
        image_count, stream, norms, head_low, wanted, wanted_log, loss, feature, dlogits, dtop, dnorm
    )
    for copy in outgoing:
        copy.wait()
    if sharded:
        gather.finish()


SAVED = (
    ((ALL, PATCH_DIM), BF16),
    ((L, ALL, D), F32),
    ((L, ALL, D), BF16),
    ((L, ALL, 3 * D), BF16),
    ((L, ALL, D), BF16),
    ((L, ALL, D), F32),
    ((L, ALL, D), BF16),
    ((L, BLOCKS, ALL, D), BF16),
    ((L, BLOCKS, ALL, D), BF16),
    (ATTN_SHAPE, BF16),
    (MLP_SHAPE, BF16),
)
SMALL = (((8, 128), F32), ((8, D), F32), ((8, 2 * C), F32), ((8, D), F32), ((8, D), F32))


def forward(image_count, sharded, *operands):
    scratch = SAVED + (
        ((IMG, NPATCH, PATCH_DIM), BF16),
        ((2 * C, D), F32),
        ((ALL, D), F32),
        ((PATCH_DIM, D), BF16),
        ((2 * C, D), BF16),
        ((8, 2 * C), F32),
        ((8, 2 * C), F32),
    )
    scratch = [pltpu.VMEM(*entry) for entry in scratch]
    scratch += [pltpu.SemaphoreType.DMA((5,)), pltpu.SemaphoreType.DMA((1 + 10 * L,))]
    if sharded:
        scratch += [
            pltpu.VMEM(PATCH_SHAPE, BF16),
            pltpu.VMEM((PATCH_DIM // (Z * Y * X * CORES), D), F32),
            pltpu.VMEM((L, 48, D), F32),
            pltpu.VMEM((L, 2, 48, D), F32),
            pltpu.SemaphoreType.DMA((N_PIECES, PIECES)),
            pltpu.SemaphoreType.DMA((N_PIECES, PIECES)),
        ]
    params = dict(collective_id=0, has_side_effects=True) if sharded else {}
    return pl.pallas_call(
        lambda *refs: forward_kernel(image_count, sharded, *refs),
        out_shape=[jax.ShapeDtypeStruct(*entry) for entry in SAVED + SMALL],
        in_specs=[SMEM] * 3 + [HBM, VMEM, VMEM, HBM, VMEM] + [HBM] * 3,
        out_specs=[HBM] * len(SAVED) + [VMEM] * len(SMALL),
        scratch_shapes=scratch,
        compiler_params=pltpu.CompilerParams(vmem_limit_bytes=62 * 2**20, **params),
        name="forward",
    )(*operands)


SMALL_SHAPE = (Z, Y, X, CORES, 8, D)
HEAD_LANES = 1280
HEAD_AT = 2048
N_GRADS = 3 * L + 2
PATCH_PIECE = 3 * L
SMALL_PIECE = 3 * L + 1
LAYER_DUE = ((0, 2, 5, 8, 11), (3, 5, 7, 11, 15), (8, 10, 12, 15, 18))
FINAL_DUE = ((0, 2, 5, 8, 12), (3, 5, 8, 11, 14), (8, 10, 12, 14, 16))
LAST_DUE = (10, 11, 13, 15, 17)
HEAD_DUE = (-1, 2, 4, 6, 9)


def scatter_pieces(grads, halves, corners, sides, hops, shares):
    patch, attn, mlp, small = range(4)

    def flat(kind):
        return dict(
            grad=lambda z, y, x, core: grads[kind].at[z, y, x, core],
            half=halves[kind],
            corner=lambda n: corners[kind].at[n],
            side=lambda n: sides[kind].at[n],
            hop=lambda n: hops[kind].at[n],
            share=shares[kind],
        )

    def layered(kind, at, grad):
        return dict(
            grad=grad,
            half=halves[kind].at[at],
            corner=lambda n: corners[kind].at[at + (n,)],
            side=lambda n: sides[kind].at[at + (n,)],
            hop=lambda n: hops[kind].at[at + (n,)],
            share=lambda total: shares[kind](at, total),
        )

    def attn_view(depth):
        return lambda z, y, x, core: grads[attn].at[depth, z, y, x, core]

    def mlp_view(depth, part):
        return lambda z, y, x, core: grads[mlp].at[depth, part, x, core, z, y]

    pieces = []
    for depth in reversed(range(L)):
        pieces += [layered(mlp, (depth, part), mlp_view(depth, part)) for part in (1, 0)]
        pieces.append(layered(attn, (depth,), attn_view(depth)))
    return pieces + [flat(patch), flat(small)]


def scatter_scratch():
    cases = (((), 32, BF16), ((L,), 48, BF16), ((L, 2), 48, BF16), ((), 8, F32))
    halves = [
        pltpu.VMEM((Z, Y, X, 32, D), BF16),
        pltpu.VMEM((L, Z, Y, X, 48, D), BF16),
        pltpu.VMEM((L, 2, X, Z, Y, 48, D), BF16),
        pltpu.VMEM((Z, Y, X, 8, D), F32),
    ]
    corners = [pltpu.VMEM(lead + (2, Z // 2, rows, D), kind) for lead, rows, kind in cases]
    sides = [pltpu.VMEM(lead + (2, Z, rows, D), kind) for lead, rows, kind in cases]
    hops = [pltpu.VMEM(lead + (Z - 1, rows, D), kind) for lead, rows, kind in cases]
    return halves + corners + sides + hops


def backward_kernel(sharded, *refs):
    dtop, norms, mixed_h, *refs = refs
    held, refs = refs[:10], refs[10:]
    if sharded:
        loss, feature, dlogits, dnorm, *refs = refs
        patch_share, attn_share, mlp_share, head_out, pos_sum, norm_sum, stats, *refs = refs
    else:
        grad_patch, grad_attn, grad_mlp, grad_norm, grad_pos, *refs = refs
    dx, dy, low, dout, dqkv, mixed, *refs = refs
    kept, sems, refs = refs[:10], refs[10], refs[11:]
    x, a, qkv, o, x1, a2, z, slope, attn_w, mlp_w = kept
    names = ("x", "a", "qkv", "o", "x1", "a2", "z", "slope", "attn", "mlp")

    def fetch(depth, *wanted):
        if depth < 0:
            return
        for name in wanted:
            n = names.index(name)
            pltpu.make_async_copy(held[n].at[depth], kept[n], sems.at[n]).start()

    def arrive(depth, *wanted):
        for name in wanted:
            n = names.index(name)
            pltpu.make_async_copy(held[n].at[depth], kept[n], sems.at[n]).wait()

    if sharded:
        place = Place()
        greet(place.partners())
    fetch(L - 1, "z", "mlp", "slope", "a2", "x1", "o", "attn", "qkv", "a", "x")
    mixed_copy = pltpu.make_async_copy(mixed_h, mixed, sems.at[len(names)])
    mixed_copy.start()
    due = {}
    if sharded:
        grad_patch, grad_attn, grad_mlp, grad_small, grad_norm, heads_all, head_rows, head_sum, gathered, squares, *refs = refs
        buffers, refs = refs[:16], refs[16:]
        send_sems, recv_sems, head_send, head_recv, last_send, last_recv = refs
        mine = (place.z, place.y, place.x, place.core)

        def count(total):
            flat = total.reshape(-1, D)
            squares[0:1, :] += jnp.sum(flat * flat, axis=0, keepdims=True)

        def share_patch(total):
            patch_share[...] = total[: patch_share.shape[0]]
            count(total)

        def share_attn(at, total):
            attn_share[at] = total
            count(total)

        def share_mlp(at, total):
            mlp_share[at] = total
            count(total)

        def share_small(total):
            gathered[mine + (slice(None), slice(0, D))] = total

        scatter = Scatter(
            place,
            scatter_pieces(
                (grad_patch, grad_attn, grad_mlp, grad_small),
                *(buffers[4 * n : 4 * n + 4] for n in range(4)),
                (share_patch, share_attn, share_mlp, share_small),
            ),
            send_sems,
            recv_sems,
        )
        heads = Gather(
            place,
            [lambda z, y, x, core: heads_all.at[z, y, x, core]],
            head_send,
            head_recv,
        )
        plan = [(HEAD_DUE, 0, heads, 0)]
        for turn in range(L):
            times = FINAL_DUE if turn == L - 1 else LAYER_DUE
            plan += [(times[n], turn, scatter, 3 * turn + n) for n in range(3)]
        plan += [(LAST_DUE, L - 1, scatter, piece) for piece in (PATCH_PIECE, SMALL_PIECE)]
        for times, turn, who, piece in plan:
            for stage in range(5):
                due.setdefault(10 * turn + times[stage], []).append((who, piece, stage + 1))
        squares[...] = jnp.zeros_like(squares)
        packed = [dlogits[:, HEAD_LANES:], jnp.zeros((8, HEAD_AT - 2 * C), F32), feature[...]]
        packed = jnp.concatenate(packed + [jnp.zeros((8, 2 * HEAD_LANES - HEAD_AT - D), F32)], axis=1)
        heads_all[mine] = jnp.concatenate([dlogits[:, :HEAD_LANES], packed], axis=0).astype(BF16)
        await_greetings(place.partners())

    def point(now):
        for who, piece, stage in due.pop(now, ()):
            who.step(piece, stage)

    point(-1)
    dx[...] = jnp.zeros((ALL, D), F32)
    for kind in range(2):
        for image in range(IMG):
            row = image * ROWS + NPATCH + kind
            dx[row : row + 1, :] = dtop[kind * IMG + image : kind * IMG + image + 1, :]
    grad_norm[...] = jnp.zeros((16, D), F32)
    for turn in range(L):
        depth = L - 1 - turn
        start = 10 * turn
        round_rows(dx, low)
        arrive(depth, "z")
        for m in range(BLOCKS):
            at = (m // 2, m % 2)
            grad_mlp[(depth, 1) + at] = tn(low[...], z[m]).astype(BF16).reshape(Z, Y, 48, D)
        point(start)
        arrive(depth, "mlp", "slope", "a2")
        for m in range(BLOCKS):
            at = (m // 2, m % 2)
            grad_gelu = nn(low[...], mlp_w[(1,) + at].reshape(D, D))
            grad_hidden = (grad_gelu * slope[m].astype(F32)).astype(BF16)
            grad_mlp[(depth, 0) + at] = tn(a2[...], grad_hidden).astype(BF16).reshape(Z, Y, 48, D)
            term = nt(grad_hidden, mlp_w[(0,) + at].reshape(D, D))
            dy[...] = term if m == 0 else dy[...] + term
            if m > 0:
                point(start + m)
        fetch(depth - 1, "z", "mlp", "slope", "a2")
        arrive(depth, "x1", "o", "attn")
        grad_in, gain, shift = norm_backward(dy[...], x1[...], norms[4 * depth + 2 : 4 * depth + 3, :])
        grad_norm[4 * depth + 2 : 4 * depth + 3, :] = gain
        grad_norm[4 * depth + 3 : 4 * depth + 4, :] = shift
        dx[...] += grad_in
        round_rows(dx, low)
        point(start + 4)
        grad_attn[depth, 3] = tn(low[...], o[...]).astype(BF16).reshape(Y, X, CORES, 48, D)
        dout[...] = nn(low[...], attn_w[3].reshape(D, D)).astype(BF16)
        fetch(depth - 1, "x1", "o")
        arrive(depth, "qkv")
        for image in range(IMG):
            for pair in range(3):
                attend_backward(qkv, dout, dqkv, image, pair)
            point(start + 5 + image)
        fetch(depth - 1, "qkv")
        arrive(depth, "a", "x")
        for n in range(3):
            part = dqkv[:, D * n : D * n + D]
            grad_attn[depth, n] = tn(part, a[...]).astype(BF16).reshape(Y, X, CORES, 48, D)
        point(start + 8)
        total = None
        for n in range(3):
            term = nn(dqkv[:, D * n : D * n + D], attn_w[n].reshape(D, D))
            total = term if total is None else total + term
        fetch(depth - 1, "attn", "a")
        grad_in, gain, shift = norm_backward(total, x[...], norms[4 * depth : 4 * depth + 1, :])
        grad_norm[4 * depth : 4 * depth + 1, :] = gain
        grad_norm[4 * depth + 1 : 4 * depth + 2, :] = shift
        dx[...] += grad_in
        fetch(depth - 1, "x")
        point(start + 9)
    total = dx[0:ROWS] + dx[ROWS : 2 * ROWS] + dx[2 * ROWS :]
    round_rows(dx, low)
    mixed_copy.wait()
    patch = tn(mixed[...], low[...])
    rows = PATCH_DIM // (Z * Y * X * CORES)
    for n in range(Z * Y * X * CORES):
        block = jnp.concatenate([patch[rows * n : rows * n + rows], jnp.zeros((32 - rows, D), F32)], axis=0)
        grad_patch[n // 8, n // 4 % 2, n // 2 % 2, n % 2] = block.astype(BF16)
    if not sharded:
        grad_pos[...] = total
        return
    small = [total[8 * n : 8 * n + 8] for n in range(ROWS // 8)]
    small += [grad_norm[0:8, :], jnp.concatenate([grad_norm[8:12, :], dnorm[0:2, :], jnp.zeros((2, D), F32)], axis=0)]
    small.append(jnp.concatenate([loss[...], jnp.zeros((8, D - 128), F32)], axis=1))
    for n in range(Z * Y * X * CORES):
        grad_small[n // 8, n // 4 % 2, n // 2 % 2, n % 2] = small[n] if n < len(small) else jnp.zeros((8, D), F32)
    left = sorted(due)
    for now in left[:2]:
        point(now)
    per_plane = head_rows.shape[0] // Z

    def unpack(n, carry):
        plane = heads_all[n].astype(F32).reshape(Y * X * CORES, 16, HEAD_LANES)
        for part in range(2):
            block = plane[:, 8 * part : 8 * part + 8].reshape(per_plane, HEAD_LANES)
            lanes = slice(part * HEAD_LANES, (part + 1) * HEAD_LANES)
            head_rows[pl.ds(n * per_plane, per_plane), lanes] = block.astype(BF16)
        return carry

    lax.fori_loop(0, Z, unpack, 0)
    features = head_rows[:, HEAD_AT : HEAD_AT + D]
    for n in range(0, 2 * C, 512):
        lanes = slice(n, min(n + 512, 2 * C))
        part = tn(head_rows[:, lanes], features)
        head_sum[lanes, :] = part
        squares[1:2, :] += jnp.sum(part * part, axis=0, keepdims=True)
    head_copy = pltpu.make_async_copy(head_sum, head_out, sems.at[len(names)])
    head_copy.start()
    for now in left[2:]:
        point(now)
    own = jnp.sum(squares[0:1, :], axis=(0, 1), keepdims=True)
    gathered[mine + (slice(None), slice(D, D + 128))] = jnp.broadcast_to(own, (8, 128))
    last = Gather(
        place, [lambda z, y, x, core: gathered.at[z, y, x, core]], last_send, last_recv, direct=True
    )
    for stage in range(1, 6):
        last.step(0, stage)
    blocks = [gathered[n // 8, n // 4 % 2, n // 2 % 2, n % 2] for n in range(Z * Y * X * CORES)]
    pos = jnp.concatenate([block[:, :D] for block in blocks[: ROWS // 8]], axis=0)
    norm = jnp.concatenate([block[:, :D] for block in blocks[ROWS // 8 : ROWS // 8 + 2]], axis=0)
    pos_sum[...] = jnp.concatenate([pos[NPATCH:TOK], pos[:NPATCH]], axis=0)
    norm_sum[...] = norm[: 4 * L + 2]
    total = blocks[0][:, D:]
    for block in blocks[1:]:
        total = total + block[:, D:]
    rest = jnp.sum(pos * pos, axis=0, keepdims=True) + jnp.sum(norm * norm, axis=0, keepdims=True) + squares[1:2, :]
    total = total[0:1, :] + jnp.sum(rest, axis=(0, 1), keepdims=True)
    norm_all = jnp.sqrt(total)
    stats[...] = jnp.concatenate(
        [blocks[ROWS // 8 + 2][0:1, :128], norm_all, jnp.minimum(1.0, MAX_NORM / norm_all), jnp.zeros((5, 128), F32)],
        axis=0,
    )
    head_copy.wait()
    scatter.finish()
    heads.finish()
    last.finish()


def backward(sharded, *operands):
    full = ((PATCH_SHAPE, BF16), (ATTN_SHAPE, BF16), (MLP_SHAPE, BF16))
    if sharded:
        outs = (
            ((PATCH_DIM // (Z * Y * X * CORES), D), F32),
            ((L, 48, D), F32),
            ((L, 2, 48, D), F32),
            ((2 * C, D), F32),
            ((TOK, D), F32),
            ((4 * L + 2, D), F32),
            ((8, 128), F32),
        )
    else:
        outs = full + (((16, D), F32), ((ROWS, D), F32))
    scratch = [((ALL, D), F32), ((ALL, D), F32), ((ALL, D), BF16), ((ALL, D), BF16), ((ALL, 3 * D), BF16), SAVED[0]]
    scratch = [pltpu.VMEM(*entry) for entry in scratch]
    scratch += [pltpu.VMEM(shape[1:], kind) for shape, kind in SAVED[1:]]
    scratch += [pltpu.SemaphoreType.DMA((11,))]
    if sharded:
        scratch += [pltpu.VMEM(*entry) for entry in full]
        scratch += [
            pltpu.VMEM(SMALL_SHAPE, F32),
            pltpu.VMEM((16, D), F32),
            pltpu.VMEM((Z, Y, X, CORES, 16, HEAD_LANES), BF16),
            pltpu.VMEM((Z * Y * X * CORES * 8, 2 * HEAD_LANES), BF16),
            pltpu.VMEM((2 * C, D), F32),
            pltpu.VMEM((Z, Y, X, CORES, 8, D + 128), F32),
            pltpu.VMEM((8, D), F32),
        ]
        scratch += scatter_scratch()
        scratch += [pltpu.SemaphoreType.DMA((N_GRADS, 8))] * 2
        scratch += [pltpu.SemaphoreType.DMA((1, PIECES))] * 4
    params = dict(collective_id=1, has_side_effects=True) if sharded else {}
    return pl.pallas_call(
        lambda *refs: backward_kernel(sharded, *refs),
        out_shape=[jax.ShapeDtypeStruct(*entry) for entry in outs],
        in_specs=[VMEM] * 2 + [HBM] * 11 + [VMEM] * (4 if sharded else 0),
        out_specs=[HBM if entry == ((2 * C, D), F32) else VMEM for entry in outs],
        scratch_shapes=scratch,
        compiler_params=pltpu.CompilerParams(vmem_limit_bytes=63 * 2**20, **params),
        name="backward",
    )(*operands)


def adam_kernel(*refs):
    stats_h, refs = refs[0], refs[1:]
    count = len(STEP_RATES)
    grads, weights, firsts, seconds = (refs[n * count : (n + 1) * count] for n in range(4))
    outs, (loss, norm), refs = refs[4 * count : 7 * count], refs[7 * count : 7 * count + 2], refs[7 * count + 2 :]
    stats, buffers, (stats_sem, in_sems, out_sems) = refs[0], refs[1 : 1 + 4 * count], refs[1 + 4 * count :]
    stats_copy = pltpu.make_async_copy(stats_h, stats, stats_sem.at[0])
    stats_copy.start()
    chunks = []
    for n in ADAM_ORDER:
        rows = grads[n].shape[0]
        step = HEAD_ROWS if rows > HEAD_ROWS else rows
        chunks += [(n, pl.ds(first, step)) for first in range(0, rows, step)]
    loads = []
    for at, (n, rows) in enumerate(chunks):
        sources = (weights[n], firsts[n], seconds[n], grads[n])
        loads.append(
            [
                pltpu.make_async_copy(source.at[rows], buffers[4 * n + k].at[rows], in_sems.at[at, k])
                for k, source in enumerate(sources)
            ]
        )
        for copy in loads[-1]:
            copy.start()
    stats_copy.wait()
    loss[...] = stats[0:1, 0:1]
    norm[...] = stats[1:2, 0:1]
    factor = stats[2:3, 0:1]
    stores = []
    for at, (n, rows) in enumerate(chunks):
        for copy in loads[at]:
            copy.wait()
        weight, first, second, grad = (buffers[4 * n + k].at[rows] for k in range(4))
        old = weight[...]
        clipped = grad[...] * factor.reshape((1,) * old.ndim)
        new_first = BETA_ONE * first[...] + (1.0 - BETA_ONE) * clipped
        new_second = BETA_TWO * second[...] + (1.0 - BETA_TWO) * clipped * clipped
        root = jnp.sqrt(new_second * (1.0 / (1.0 - BETA_TWO**ADAM_STEP))) + ADAM_EPS
        move = new_first * (1.0 / (1.0 - BETA_ONE**ADAM_STEP)) / root
        weight[...] = old - STEP_RATES[n] * (move + DECAY * old)
        first[...] = new_first
        second[...] = new_second
        for k in range(3):
            copy = pltpu.make_async_copy(
                buffers[4 * n + k].at[rows], outs[k * count + n].at[rows], out_sems.at[at, k]
            )
            copy.start()
            stores.append(copy)
    for copy in stores:
        copy.wait()


HEAD_ROWS = 400
ADAM_ORDER = (4, 2, 1, 3, 0, 5)


def adam(stats, grads, weights, firsts, seconds):
    shapes = [weight.shape for weight in weights]
    chunk_count = len(shapes) - 1 + 2 * C // HEAD_ROWS
    return pl.pallas_call(
        adam_kernel,
        out_shape=[jax.ShapeDtypeStruct(shape, F32) for shape in shapes * 3 + [(1, 1)] * 2],
        in_specs=[HBM] * (1 + 4 * len(shapes)),
        out_specs=[HBM] * (3 * len(shapes)) + [VMEM] * 2,
        scratch_shapes=[pltpu.VMEM((8, 128), F32)]
        + [pltpu.VMEM(shape, F32) for shape in shapes for _ in range(4)]
        + [pltpu.SemaphoreType.DMA((1,))]
        + [pltpu.SemaphoreType.DMA((chunk_count, 4)), pltpu.SemaphoreType.DMA((chunk_count, 3))],
        compiler_params=pltpu.CompilerParams(vmem_limit_bytes=63 * 2**20),
        name="adam",
    )(stats, *grads, *weights, *firsts, *seconds)


def per_device(
    patches, partners, mix_weight, labels, teacher_logits,
    patch_weight, attn_weight, mlp_weight, positions, head_weight, norm_params,
    patch_first, attn_first, mlp_first, pos_first, head_first, norm_first,
    patch_second, attn_second, mlp_second, pos_second, head_second, norm_second,
):
    axes = ("dp", "mp")
    image_count = patches.shape[0] * lax.axis_size("dp") * lax.axis_size("mp")
    sharded = (lax.axis_size("dp"), lax.axis_size("mp")) == (Z * Y, X * CORES)
    attn_t = jnp.swapaxes(attn_weight, 1, 2)
    if sharded:
        weights_in = (patch_weight, attn_t, mlp_weight)
    else:
        patch_low = lax.all_gather(patch_weight.astype(BF16), axes, axis=0, tiled=True)
        attn_low = lax.all_gather(attn_t.astype(BF16), axes, axis=1, tiled=True)
        mlp_low = lax.all_gather(mlp_weight.astype(BF16), "dp", axis=2, tiled=True)
        mlp_low = lax.all_gather(mlp_low, "mp", axis=2, tiled=False)
        weights_in = (patch_low, attn_low.reshape(ATTN_SHAPE), mlp_low.reshape(MLP_SHAPE))
    results = forward(
        image_count, sharded, partners, mix_weight, labels, patches, teacher_logits, positions,
        head_weight.T, norm_params, *weights_in,
    )
    saved, (loss, feature, dlogits, dtop, dnorm) = results[: len(SAVED)], results[len(SAVED) :]
    operands = (dtop, norm_params, *saved)
    if sharded:
        patch_share, attn_share, mlp_share, head_sum, pos_sum, norm_sum, stats = backward(
            True, *operands, loss, feature, dlogits, dnorm
        )
        mlp_share = mlp_share.reshape(mlp_weight.shape)
    else:
        grad_patch, grad_attn, grad_mlp, grad_norm, grad_pos = backward(False, *operands)
        rows = PATCH_DIM // (Z * Y * X * CORES)
        grad_patch = grad_patch.reshape(-1, 32, D)[:, :rows].reshape(PATCH_DIM, D).astype(F32)
        patch_share = lax.psum_scatter(grad_patch, axes, scatter_dimension=0, tiled=True)
        grad_attn = grad_attn.reshape(L, 4 * D, D).astype(F32)
        attn_share = lax.psum_scatter(grad_attn, axes, scatter_dimension=1, tiled=True)
        grad_mlp = grad_mlp.reshape(L, 2, BLOCKS, D, D).astype(F32)
        mlp_share = lax.psum_scatter(grad_mlp, "mp", scatter_dimension=2, tiled=True)
        mlp_share = lax.psum_scatter(mlp_share, "dp", scatter_dimension=3, tiled=True)
        mlp_share = mlp_share.reshape(mlp_weight.shape)
        features = lax.all_gather(feature.astype(BF16), axes, axis=0, tiled=True)
        all_dlogits = lax.all_gather(dlogits.astype(BF16), axes, axis=0, tiled=True)
        head_sum = tn(all_dlogits, features)
        grad_norms = jnp.concatenate([grad_norm[: 4 * L], dnorm[:2]], axis=0)
        grad_pos = jnp.concatenate([grad_pos[NPATCH:TOK], grad_pos[:NPATCH]], axis=0)
        pos_sum, norm_sum, loss_sum = lax.psum((grad_pos, grad_norms, loss[0, 0]), axes)
        own_squares = sum(jnp.sum(share * share) for share in (patch_share, attn_share, mlp_share))
        shared = sum(jnp.sum(total * total) for total in (pos_sum, head_sum, norm_sum))
        global_norm = jnp.sqrt(lax.psum(own_squares, axes) + shared)
        factor = jnp.minimum(1.0, MAX_NORM / global_norm)
        stats = jnp.stack([loss_sum, global_norm, factor] + [jnp.float32(0.0)] * 5)
        stats = jnp.broadcast_to(stats[:, None], (8, 128))
    weights = (patch_weight, attn_weight, mlp_weight, positions, head_weight, norm_params)
    firsts = (patch_first, attn_first, mlp_first, pos_first, head_first, norm_first)
    seconds = (patch_second, attn_second, mlp_second, pos_second, head_second, norm_second)

    def turned(arrays):
        return (arrays[0], jnp.swapaxes(arrays[1], 1, 2), arrays[2], arrays[3], arrays[4].T, arrays[5])

    grads = (patch_share, attn_share, mlp_share, pos_sum, head_sum, norm_sum)
    *updated, loss_sum, global_norm = adam(stats, grads, turned(weights), turned(firsts), turned(seconds))
    return (loss_sum.reshape(()), global_norm.reshape(()), *(out for n in range(3) for out in turned(updated[6 * n : 6 * n + 6])))


def solution(mesh):
    images = (P(("dp", "mp"), None, None), P(("dp", "mp")), P(("dp", "mp")), P(("dp", "mp")), P(("dp", "mp"), None))
    weights = (P(("dp", "mp"), None), P(None, None, ("dp", "mp")), P(None, None, "dp", "mp"), P(), P(), P())
    return jax.shard_map(
        per_device,
        mesh=mesh,
        in_specs=images + weights * 3,
        out_specs=(P(), P()) + weights * 3,
        check_vma=False,
    )
```

```python
import jax
import jax.numpy as jnp
from jax import lax
from jax.experimental import pallas as pl
from jax.experimental.pallas import tpu as pltpu
from jax.sharding import PartitionSpec as P

D = 384
C = 1000
PATCH_DIM = 768
NPATCH = 196
L = 3
TOK = 198
IMG = 3
ROWS = 208
ALL = IMG * ROWS
BLOCKS = 4

Z = 4
Y = 2
X = 2
CORES = 2
EVERY = slice(0, 2)
PIECES = 11

LN_EPS = 1e-06
TEMPER = 3.0
MAX_NORM = 0.02
BETA_ONE = 0.9
BETA_TWO = 0.999
STEP_RATES = (0.05, 0.05, 0.05, 0.4, 0.12, 0.5)
DECAY = 0.05
ADAM_EPS = 1e-08
ADAM_STEP = 10.0
LOWEST = -1e30

BF16 = jnp.bfloat16
F32 = jnp.float32
VMEM = pl.BlockSpec(memory_space=pltpu.VMEM)
SMEM = pl.BlockSpec(memory_space=pltpu.SMEM)
HBM = pl.BlockSpec(memory_space=pl.ANY)
MESH = pl.DeviceIdType.MESH


def nn(left, right):
    return jnp.dot(left, right, preferred_element_type=F32)


def nt(left, right):
    return lax.dot_general(left, right, (((1,), (1,)), ((), ())), preferred_element_type=F32)


def tn(left, right):
    return lax.dot_general(left, right, (((0,), (0,)), ((), ())), preferred_element_type=F32)


def unit_norm(inputs):
    centred = inputs - jnp.mean(inputs, axis=-1, keepdims=True)
    inverse = lax.rsqrt(jnp.mean(centred * centred, axis=-1, keepdims=True) + LN_EPS)
    return centred * inverse, inverse


def norm_backward(grad_out, inputs, gain):
    normed, inverse = unit_norm(inputs)
    grad_gain = jnp.sum(grad_out * normed, axis=0, keepdims=True)
    grad_shift = jnp.sum(grad_out, axis=0, keepdims=True)
    scaled = grad_out * gain
    grad_in = inverse * (
        scaled
        - jnp.mean(scaled, axis=-1, keepdims=True)
        - normed * jnp.mean(scaled * normed, axis=-1, keepdims=True)
    )
    return grad_in, grad_gain, grad_shift


class Place:
    def __init__(self):
        dp, mp = lax.axis_index("dp"), lax.axis_index("mp")
        self.z, self.y = dp // Y, dp % Y
        self.x, self.core = mp // CORES, mp % CORES

    def at(self, dz=0, dy=0, dx=0, dcore=0):
        z = lax.rem(self.z + dz, Z)
        y = 1 - self.y if dy else self.y
        x = 1 - self.x if dx else self.x
        core = 1 - self.core if dcore else self.core
        return {"dp": z * Y + y, "mp": x * CORES + core}

    def partners(self):
        column = [self.at(dz=step) for step in range(1, Z)]
        return column + [self.at(dx=1), self.at(dy=1), self.at(dcore=1), self.at(dy=1, dx=1)]


def greet(partners):
    for partner in partners:
        pl.semaphore_signal(pltpu.get_barrier_semaphore(), inc=1, device_id=partner, device_id_type=MESH)


def await_greetings(partners):
    pl.semaphore_wait(pltpu.get_barrier_semaphore(), len(partners))


class Gather:
    def __init__(self, place, pieces, send_sems, recv_sems, planes=(), direct=False):
        self.place, self.pieces, self.planes, self.direct = place, pieces, planes, direct
        self.send_sems, self.recv_sems = send_sems, recv_sems
        self.started = []
        self.done = set()

    def copy(self, piece, n, region, target):
        view = self.pieces[piece](*region)
        return pltpu.make_async_remote_copy(
            src_ref=view,
            dst_ref=view,
            send_sem=self.send_sems.at[piece, n],
            recv_sem=self.recv_sems.at[piece, n],
            device_id=target,
            device_id_type=MESH,
        )

    def send(self, piece, n, region, **offset):
        copy = self.copy(piece, n, region, self.place.at(**offset))
        copy.start()
        self.started.append(copy)

    def recv(self, piece, n, region):
        self.copy(piece, n, region, self.place.at(dcore=1)).wait_recv()

    def step(self, piece, stage):
        if (piece, stage) in self.done:
            return
        self.done.add((piece, stage))
        z, y, x, core = self.place.z, self.place.y, self.place.x, self.place.core
        far_y, far_x, sibling = 1 - y, 1 - x, 1 - core
        column, low, high = slice(0, Z), slice(0, Z // 2), slice(Z // 2, Z)
        if piece in self.planes:
            if stage == 1:
                self.send(piece, 3, (z, y, x, core), dx=1)
                self.send(piece, 4, (z, y, x, core), dy=1)
                self.send(piece, 6, (z, y, x, core), dy=1, dx=1)
            if stage == 2:
                self.recv(piece, 3, (z, y, far_x, core))
                self.recv(piece, 4, (z, far_y, x, core))
                self.recv(piece, 6, (z, far_y, far_x, core))
                for hop in range(1, Z):
                    self.send(piece, hop - 1, (z, EVERY, EVERY, core), dz=hop)
            if stage == 4:
                for hop in range(1, Z):
                    self.recv(piece, hop - 1, (lax.rem(z + Z - hop, Z), EVERY, EVERY, core))
                self.send(piece, 5, (column, EVERY, EVERY, core), dcore=1)
            if stage == 5:
                self.recv(piece, 5, (column, EVERY, EVERY, sibling))
            return
        if stage == 1:
            for hop in range(1, Z):
                self.send(piece, hop - 1, (z, y, x, core), dz=hop)
        if self.direct:
            if stage == 2:
                for hop in range(1, Z):
                    self.recv(piece, hop - 1, (lax.rem(z + Z - hop, Z), y, x, core))
                self.send(piece, 3, (column, y, x, core), dx=1)
                self.send(piece, 4, (column, y, x, core), dy=1)
                self.send(piece, 6, (column, y, x, core), dy=1, dx=1)
            if stage == 4:
                self.recv(piece, 3, (column, y, far_x, core))
                self.recv(piece, 4, (column, far_y, x, core))
                self.recv(piece, 6, (column, far_y, far_x, core))
                self.send(piece, 5, (column, EVERY, EVERY, core), dcore=1)
            if stage == 5:
                self.recv(piece, 5, (column, EVERY, EVERY, sibling))
            return
        if stage == 2:
            for hop in range(1, Z):
                self.recv(piece, hop - 1, (lax.rem(z + Z - hop, Z), y, x, core))
            self.send(piece, 3, (column, y, x, core), dx=1)
            self.send(piece, 4, (column, y, x, core), dy=1)
            self.send(piece, 5, (column, y, x, core), dcore=1)
        if stage == 3:
            self.recv(piece, 3, (column, y, far_x, core))
            self.send(piece, 6, (low, y, far_x, core), dy=1)
            self.send(piece, 8, (column, y, far_x, core), dcore=1)
            self.recv(piece, 4, (column, far_y, x, core))
            self.send(piece, 7, (high, far_y, x, core), dx=1)
            self.send(piece, 9, (column, far_y, x, core), dcore=1)
        if stage == 4:
            self.recv(piece, 6, (low, far_y, far_x, core))
            self.recv(piece, 7, (high, far_y, far_x, core))
            self.send(piece, 10, (column, far_y, far_x, core), dcore=1)
        if stage == 5:
            self.recv(piece, 5, (column, y, x, sibling))
            self.recv(piece, 8, (column, y, far_x, sibling))
            self.recv(piece, 9, (column, far_y, x, sibling))
            self.recv(piece, 10, (column, far_y, far_x, sibling))

    def finish(self):
        for copy in self.started:
            copy.wait_send()


def add_into(target, *terms):
    def body(n, carry):
        total = target[n].astype(F32)
        for term in terms:
            total = total + term[n].astype(F32)
        target[n] = total.astype(target.dtype)
        return carry

    lax.fori_loop(0, target.shape[0], body, 0)


class Scatter:
    def __init__(self, place, pieces, send_sems, recv_sems):
        self.place, self.pieces = place, pieces
        self.send_sems, self.recv_sems = send_sems, recv_sems
        self.started = []

    def copy(self, piece, n, source, target, **offset):
        return pltpu.make_async_remote_copy(
            src_ref=source,
            dst_ref=target,
            send_sem=self.send_sems.at[piece, n],
            recv_sem=self.recv_sems.at[piece, n],
            device_id=self.place.at(**offset),
            device_id_type=MESH,
        )

    def send(self, piece, n, source, target, **offset):
        copy = self.copy(piece, n, source, target, **offset)
        copy.start()
        self.started.append(copy)

    def recv(self, piece, n, target):
        self.copy(piece, n, target, target, dcore=1).wait_recv()
        return target

    def step(self, piece, stage):
        z, y, x, core = self.place.z, self.place.y, self.place.x, self.place.core
        far_y, far_x, sibling = 1 - y, 1 - x, 1 - core
        column, low, high = slice(0, Z), slice(0, Z // 2), slice(Z // 2, Z)
        part = self.pieces[piece]
        grad = part["grad"]
        if stage == 1:
            self.send(piece, 0, grad(column, EVERY, EVERY, sibling), part["half"], dcore=1)
        if stage == 2:
            add_into(grad(column, EVERY, EVERY, core), self.recv(piece, 0, part["half"]))
            self.send(piece, 1, grad(low, far_y, far_x, core), part["corner"](0), dy=1)
            self.send(piece, 2, grad(high, far_y, far_x, core), part["corner"](1), dx=1)
        if stage == 3:
            add_into(grad(low, y, far_x, core), self.recv(piece, 1, part["corner"](0)))
            self.send(piece, 3, grad(column, y, far_x, core), part["side"](0), dx=1)
            add_into(grad(high, far_y, x, core), self.recv(piece, 2, part["corner"](1)))
            self.send(piece, 4, grad(column, far_y, x, core), part["side"](1), dy=1)
        if stage == 4:
            sides = [self.recv(piece, 3 + n, part["side"](n)) for n in range(2)]
            add_into(grad(column, y, x, core), *sides)
            for hop in range(1, Z):
                self.send(
                    piece, 4 + hop, grad(lax.rem(z + hop, Z), y, x, core), part["hop"](hop - 1), dz=hop
                )
        if stage == 5:
            total = grad(z, y, x, core)[...].astype(F32)
            for hop in range(1, Z):
                total = total + self.recv(piece, 4 + hop, part["hop"](hop - 1))[...].astype(F32)
            part["share"](total)

    def finish(self):
        for copy in self.started:
            copy.wait_send()


def round_rows(source, target):
    def body(n, carry):
        rows = pl.ds(n * ROWS, ROWS)
        target[rows, :] = source[rows, :].astype(target.dtype)
        return carry

    lax.fori_loop(0, IMG, body, 0)


def head_lanes(shape, head):
    lane = lax.broadcasted_iota(jnp.int32, shape, len(shape) - 1)
    return lane < 64 if head == 0 else lane >= 64


def attend(qkv, out, image, pair):
    rows = slice(image * ROWS, (image + 1) * ROWS)
    lanes = 128 * pair
    queries = qkv[rows, lanes : lanes + 128] * BF16(0.125)
    keys = qkv[rows, D + lanes : D + lanes + 128]
    values = qkv[rows, 2 * D + lanes : 2 * D + lanes + 128]
    key_lane = lax.broadcasted_iota(jnp.int32, (1, ROWS), 1)
    parts = []
    for head in range(2):
        scores = nt(jnp.where(head_lanes((ROWS, 128), head), queries, BF16(0)), keys)
        scores = jnp.where(key_lane < TOK, scores, LOWEST)
        weights = jnp.exp(scores - jnp.max(scores, axis=-1, keepdims=True))
        inverse = 1.0 / jnp.sum(weights, axis=-1, keepdims=True)
        parts.append(nn(weights.astype(BF16), values) * inverse)
    out[rows, lanes : lanes + 128] = jnp.where(
        head_lanes((ROWS, 128), 0), parts[0], parts[1]
    ).astype(BF16)


def attend_backward(qkv, grad_out, grad_qkv, image, pair):
    rows = slice(image * ROWS, (image + 1) * ROWS)
    lanes = 128 * pair
    queries = qkv[rows, lanes : lanes + 128] * BF16(0.125)
    keys = qkv[rows, D + lanes : D + lanes + 128]
    values = qkv[rows, 2 * D + lanes : 2 * D + lanes + 128]
    grad = grad_out[rows, lanes : lanes + 128]
    key_row = lax.broadcasted_iota(jnp.int32, (ROWS, 1), 0)
    grad_q, grad_k, grad_v = [], [], []
    for head in range(2):
        own = head_lanes((ROWS, 128), head)
        scores = nt(jnp.where(own, keys, BF16(0)), queries)
        scores = jnp.where(key_row < TOK, scores, LOWEST)
        probs = jnp.exp(scores - jnp.max(scores, axis=0, keepdims=True))
        probs = probs * (1.0 / jnp.sum(probs, axis=0, keepdims=True))
        grad_probs = nt(jnp.where(own, values, BF16(0)), grad)
        total = jnp.sum(probs * grad_probs, axis=0, keepdims=True)
        grad_scores = (probs * (grad_probs - total)).astype(BF16)
        grad_v.append(nn(probs.astype(BF16), grad))
        grad_k.append(nn(grad_scores, queries))
        grad_q.append(tn(grad_scores, keys))
    first = head_lanes((ROWS, 128), 0)
    grad_qkv[rows, lanes : lanes + 128] = (
        jnp.where(first, grad_q[0], grad_q[1]) * 0.125
    ).astype(BF16)
    grad_qkv[rows, D + lanes : D + lanes + 128] = jnp.where(first, grad_k[0], grad_k[1]).astype(
        BF16
    )
    grad_qkv[rows, 2 * D + lanes : 2 * D + lanes + 128] = jnp.where(
        first, grad_v[0], grad_v[1]
    ).astype(BF16)


def mix_images(partners, mix, patches, mixed):
    for image in range(IMG):
        total = None
        for other in range(IMG):
            share = jnp.where(partners[image] == other, 1.0 - mix[image], 0.0)
            if image == other:
                share = share + mix[image]
            term = share * patches[other].astype(F32)
            total = term if total is None else total + term
        padding = jnp.zeros((ROWS - NPATCH, PATCH_DIM), F32)
        mixed[image * ROWS : (image + 1) * ROWS, :] = jnp.concatenate(
            [total, padding], axis=0
        ).astype(BF16)


def head_masks():
    row = lax.broadcasted_iota(jnp.int32, (8, 2 * C), 0)
    lane = lax.broadcasted_iota(jnp.int32, (8, 2 * C), 1)
    is_class = row < IMG
    low_lane = jnp.where(is_class, 0, C)
    high_lane = jnp.where(is_class, C, jnp.where(row < 2 * IMG, 2 * C, 0))
    return row, lane, is_class, (lane >= low_lane) & (lane < high_lane)


def log_softmax(values, used):
    values = jnp.where(used, values, LOWEST)
    shifted = values - jnp.max(values, axis=-1, keepdims=True)
    return shifted - jnp.log(jnp.sum(jnp.exp(shifted), axis=-1, keepdims=True))


def prepare_loss(partners, mix, labels, teacher, head, head_low, wanted, wanted_log):
    def body(n, carry):
        rows = pl.ds(n * 400, 400)
        head_low[rows, :] = head[rows, :].astype(BF16)
        return carry

    lax.fori_loop(0, 2 * C // 400, body, 0)
    row, lane, is_class, used = head_masks()
    taught = jnp.concatenate([jnp.zeros((IMG, C), F32), teacher[...]], axis=1)
    taught = jnp.concatenate(
        [jnp.zeros((IMG, 2 * C), F32), taught, jnp.zeros((8 - 2 * IMG, 2 * C), F32)], axis=0
    )
    teacher_log = log_softmax(taught / TEMPER, used)
    target = jnp.zeros((8, 2 * C), F32)
    for image in range(IMG):
        partner_label = labels[IMG - 1]
        for other in range(IMG - 1):
            partner_label = jnp.where(partners[image] == other, labels[other], partner_label)
        ours = jnp.where(lane == labels[image], mix[image], 0.0) + jnp.where(
            lane == partner_label, 1.0 - mix[image], 0.0
        )
        target = target + jnp.where(row == image, ours, 0.0)
    wanted[...] = jnp.where(is_class, target, jnp.exp(teacher_log))
    wanted_log[...] = teacher_log


def head_and_loss(
    image_count, stream, norms, head_low, wanted, wanted_log, loss, feature, dlogits, dtop, dnorm
):
    picked = [
        stream[image * ROWS + NPATCH + kind : image * ROWS + NPATCH + kind + 1, :]
        for kind in range(2)
        for image in range(IMG)
    ]
    top = jnp.concatenate(picked + [jnp.zeros((2, D), F32)], axis=0)
    gain = norms[4 * L : 4 * L + 1, :]
    normed, _ = unit_norm(top)
    features = (normed * gain + norms[4 * L + 1 : 4 * L + 2, :]).astype(BF16)
    _, _, is_class, used = head_masks()
    logits = nt(features, head_low[...])
    student_log = log_softmax(jnp.where(is_class, logits, logits / TEMPER), used)
    share = wanted[...]
    terms = jnp.where(
        is_class, -0.5 * share * student_log, 0.5 * TEMPER * TEMPER * share * (wanted_log[...] - student_log)
    )
    terms = jnp.where(used, terms, 0.0)
    loss[...] = jnp.broadcast_to(jnp.sum(terms, axis=(0, 1), keepdims=True), (8, 128))
    scale = jnp.where(is_class, 0.5 / image_count, 0.5 * TEMPER / image_count)
    grad_logits = (scale * jnp.where(used, jnp.exp(student_log) - share, 0.0)).astype(BF16)
    feature[...] = features.astype(F32)
    dlogits[...] = grad_logits.astype(F32)
    grad_top, grad_gain, grad_shift = norm_backward(nn(grad_logits, head_low[...]), top, gain)
    dtop[...] = grad_top
    dnorm[...] = jnp.concatenate([grad_gain, grad_shift, jnp.zeros((6, D), F32)], axis=0)


ATTN_SHAPE = (L, Z, Y, X, CORES, 48, D)
MLP_SHAPE = (L, 2, X, CORES, Z, Y, 48, D)
PATCH_SHAPE = (Z, Y, X, CORES, 32, D)
N_PIECES = 1 + 3 * L
PLANES = (1 + 3 * (L - 1),)
QUEUE = tuple(n for n in range(N_PIECES) if n not in PLANES)


def gather_views(patch_w, attn_w, mlp_w):
    def attn(depth):
        return lambda z, y, x, core: attn_w.at[depth, z, y, x, core]

    def mlp(depth, part):
        return lambda z, y, x, core: mlp_w.at[depth, part, x, core, z, y]

    views = [lambda z, y, x, core: patch_w.at[z, y, x, core]]
    for depth in range(L):
        views += [attn(depth), mlp(depth, 0), mlp(depth, 1)]
    return views


def forward_kernel(image_count, sharded, *refs):
    (
        partners, mix, labels, patches_h, teacher, pos, head_h, norms, patch_in, attn_in, mlp_in,
        mixed_h, x_h, a_h, qkv_h, o_h, x1_h, a2_h, z_h, slope_h, attn_h, mlp_h,
        loss, feature, dlogits, dtop, dnorm,
        mixed, x, a, qkv, o, x1, a2, z, slope, attn_w, mlp_w,
        patches, head, stream, patch_w, head_low, wanted, wanted_log, in_sems, out_sems, *rest,
    ) = refs
    outgoing = []
    if sharded:
        place = Place()
        greet(place.partners())

    def keep(source, target):
        copy = pltpu.make_async_copy(source, target, out_sems.at[len(outgoing)])
        copy.start()
        outgoing.append(copy)

    if sharded:
        patch_all, patch_s, attn_s, mlp_s, send_sems, recv_sems = rest
        loads = [(attn_in, attn_s), (mlp_in, mlp_s), (patch_in, patch_s)]
    else:
        loads = [(attn_in, attn_w), (mlp_in, mlp_w), (patch_in, patch_w)]
    loads += [(patches_h, patches), (head_h, head)]
    loads = [
        pltpu.make_async_copy(source, target, in_sems.at[n]) for n, (source, target) in enumerate(loads)
    ]
    for copy in loads:
        copy.start()

    if sharded:
        gather = Gather(place, gather_views(patch_all, attn_w, mlp_w), send_sems, recv_sems, planes=PLANES)
        mine = (place.z, place.y, place.x, place.core)
        loads[2].wait()
        patch_all[mine] = jnp.concatenate([patch_s[...], jnp.zeros((8, D), F32)], axis=0).astype(BF16)
        loads[0].wait()
        for depth in range(L):
            attn_w[(depth,) + mine] = attn_s[depth].astype(BF16)
        loads[1].wait()
        for depth in range(L):
            for part in range(2):
                mlp_w[depth, part, place.x, place.core, place.z, place.y] = mlp_s[depth, part].astype(BF16)
        await_greetings(place.partners())
        for piece in PLANES + QUEUE:
            gather.step(piece, 1)

    def ahead(n, stage):
        if sharded and n < len(QUEUE):
            gather.step(QUEUE[n], stage)

    def need(piece):
        if not sharded:
            return
        if piece in PLANES:
            for stage in (4, 5):
                gather.step(piece, stage)
            return
        n = QUEUE.index(piece)
        ahead(n + 1, 2)
        ahead(n, 3)
        ahead(n + 2, 2)
        ahead(n + 1, 3)
        ahead(n, 4)
        ahead(n, 5)

    def between(piece):
        if not sharded:
            return
        later = [n for n in range(len(QUEUE)) if QUEUE[n] > piece]
        if later:
            ahead(later[0] + 2, 2)
            ahead(later[0] + 1, 3)

    if sharded:
        ahead(0, 2)
        for piece in PLANES:
            gather.step(piece, 2)
        ahead(1, 2)
        ahead(0, 3)
    else:
        for n in range(3):
            loads[n].wait()
    loads[3].wait()
    mix_images(partners, mix, patches, mixed)
    keep(mixed, mixed_h)
    ahead(2, 2)
    loads[4].wait()
    prepare_loss(partners, mix, labels, teacher, head, head_low, wanted, wanted_log)
    need(0)
    if sharded:
        for n in range(Z * Y * X):
            block = patch_all[n // 4, n // 2 % 2, n % 2].astype(F32)
            patch_w[48 * n : 48 * n + 48, :] = jnp.concatenate([block[0, :24], block[1, :24]], axis=0).astype(BF16)
    embedded = nn(mixed[...], patch_w[...])
    added = jnp.concatenate([pos[2:TOK, :], pos[0:2, :], jnp.zeros((ROWS - TOK, D), F32)], axis=0)
    for image in range(IMG):
        rows = slice(image * ROWS, (image + 1) * ROWS)
        x[0, rows, :] = embedded[rows] + added
    for depth in range(L):
        norm = [norms[4 * depth + n : 4 * depth + n + 1, :] for n in range(4)]
        first = 1 + 3 * depth
        keep(x.at[depth], x_h.at[depth])
        a[depth] = (unit_norm(x[depth])[0] * norm[0] + norm[1]).astype(BF16)
        keep(a.at[depth], a_h.at[depth])
        need(first)
        for n in range(3):
            qkv[depth, :, D * n : D * n + D] = nt(a[depth], attn_w[depth, n].reshape(D, D)).astype(BF16)
        keep(qkv.at[depth], qkv_h.at[depth])
        keep(attn_w.at[depth], attn_h.at[depth])
        for image in range(IMG):
            for pair in range(3):
                attend(qkv.at[depth], o.at[depth], image, pair)
            if image == 1:
                between(first)
        keep(o.at[depth], o_h.at[depth])
        x1[depth] = x[depth] + nt(o[depth], attn_w[depth, 3].reshape(D, D))
        keep(x1.at[depth], x1_h.at[depth])
        a2[depth] = (unit_norm(x1[depth])[0] * norm[2] + norm[3]).astype(BF16)
        keep(a2.at[depth], a2_h.at[depth])
        need(first + 1)

        def widen(m, carry):
            hidden = nn(a2[depth], mlp_w[depth, 0, m // 2, lax.rem(m, 2)].reshape(D, D))
            phi = 0.5 * (1.0 + lax.erf(hidden * 2.0**-0.5))
            z[depth, m] = (hidden * phi).astype(BF16)
            density = jnp.exp(-0.5 * hidden * hidden) * 0.3989422804014327
            slope[depth, m] = (phi + hidden * density).astype(BF16)
            return carry

        lax.fori_loop(0, BLOCKS, widen, 0)
        keep(z.at[depth], z_h.at[depth])
        keep(slope.at[depth], slope_h.at[depth])
        need(first + 2)
        keep(mlp_w.at[depth], mlp_h.at[depth])
        total = x1[depth]
        for m in range(BLOCKS):
            total = total + nt(z[depth, m], mlp_w[depth, 1, m // 2, m % 2].reshape(D, D))
        if depth + 1 < L:
            x[depth + 1] = total
        else:
            stream[...] = total
    head_and_loss(
        image_count, stream, norms, head_low, wanted, wanted_log, loss, feature, dlogits, dtop, dnorm
    )
    for copy in outgoing:
        copy.wait()
    if sharded:
        gather.finish()


SAVED = (
    ((ALL, PATCH_DIM), BF16),
    ((L, ALL, D), F32),
    ((L, ALL, D), BF16),
    ((L, ALL, 3 * D), BF16),
    ((L, ALL, D), BF16),
    ((L, ALL, D), F32),
    ((L, ALL, D), BF16),
    ((L, BLOCKS, ALL, D), BF16),
    ((L, BLOCKS, ALL, D), BF16),
    (ATTN_SHAPE, BF16),
    (MLP_SHAPE, BF16),
)
SMALL = (((8, 128), F32), ((8, D), F32), ((8, 2 * C), F32), ((8, D), F32), ((8, D), F32))


def forward(image_count, sharded, *operands):
    scratch = SAVED + (
        ((IMG, NPATCH, PATCH_DIM), BF16),
        ((2 * C, D), F32),
        ((ALL, D), F32),
        ((PATCH_DIM, D), BF16),
        ((2 * C, D), BF16),
        ((8, 2 * C), F32),
        ((8, 2 * C), F32),
    )
    scratch = [pltpu.VMEM(*entry) for entry in scratch]
    scratch += [pltpu.SemaphoreType.DMA((5,)), pltpu.SemaphoreType.DMA((1 + 10 * L,))]
    if sharded:
        scratch += [
            pltpu.VMEM(PATCH_SHAPE, BF16),
            pltpu.VMEM((PATCH_DIM // (Z * Y * X * CORES), D), F32),
            pltpu.VMEM((L, 48, D), F32),
            pltpu.VMEM((L, 2, 48, D), F32),
            pltpu.SemaphoreType.DMA((N_PIECES, PIECES)),
            pltpu.SemaphoreType.DMA((N_PIECES, PIECES)),
        ]
    params = dict(collective_id=0, has_side_effects=True) if sharded else {}
    return pl.pallas_call(
        lambda *refs: forward_kernel(image_count, sharded, *refs),
        out_shape=[jax.ShapeDtypeStruct(*entry) for entry in SAVED + SMALL],
        in_specs=[SMEM] * 3 + [HBM, VMEM, VMEM, HBM, VMEM] + [HBM] * 3,
        out_specs=[HBM] * len(SAVED) + [VMEM] * len(SMALL),
        scratch_shapes=scratch,
        compiler_params=pltpu.CompilerParams(vmem_limit_bytes=62 * 2**20, **params),
        name="forward",
    )(*operands)


SMALL_SHAPE = (Z, Y, X, CORES, 8, D)
HEAD_LANES = 1280
HEAD_AT = 2048
N_GRADS = 3 * L + 2
PATCH_PIECE = 3 * L
SMALL_PIECE = 3 * L + 1
LAYER_DUE = ((0, 2, 5, 8, 11), (3, 5, 7, 11, 15), (8, 10, 12, 15, 18))
FINAL_DUE = ((0, 2, 5, 8, 12), (3, 5, 8, 11, 14), (8, 10, 12, 14, 16))
LAST_DUE = (10, 11, 13, 15, 17)
HEAD_DUE = (-1, 2, 4, 6, 9)


def scatter_pieces(grads, halves, corners, sides, hops, shares):
    patch, attn, mlp, small = range(4)

    def flat(kind):
        return dict(
            grad=lambda z, y, x, core: grads[kind].at[z, y, x, core],
            half=halves[kind],
            corner=lambda n: corners[kind].at[n],
            side=lambda n: sides[kind].at[n],
            hop=lambda n: hops[kind].at[n],
            share=shares[kind],
        )

    def layered(kind, at, grad):
        return dict(
            grad=grad,
            half=halves[kind].at[at],
            corner=lambda n: corners[kind].at[at + (n,)],
            side=lambda n: sides[kind].at[at + (n,)],
            hop=lambda n: hops[kind].at[at + (n,)],
            share=lambda total: shares[kind](at, total),
        )

    def attn_view(depth):
        return lambda z, y, x, core: grads[attn].at[depth, z, y, x, core]

    def mlp_view(depth, part):
        return lambda z, y, x, core: grads[mlp].at[depth, part, x, core, z, y]

    pieces = []
    for depth in reversed(range(L)):
        pieces += [layered(mlp, (depth, part), mlp_view(depth, part)) for part in (1, 0)]
        pieces.append(layered(attn, (depth,), attn_view(depth)))
    return pieces + [flat(patch), flat(small)]


def scatter_scratch():
    cases = (((), 32, BF16), ((L,), 48, BF16), ((L, 2), 48, BF16), ((), 8, F32))
    halves = [
        pltpu.VMEM((Z, Y, X, 32, D), BF16),
        pltpu.VMEM((L, Z, Y, X, 48, D), BF16),
        pltpu.VMEM((L, 2, X, Z, Y, 48, D), BF16),
        pltpu.VMEM((Z, Y, X, 8, D), F32),
    ]
    corners = [pltpu.VMEM(lead + (2, Z // 2, rows, D), kind) for lead, rows, kind in cases]
    sides = [pltpu.VMEM(lead + (2, Z, rows, D), kind) for lead, rows, kind in cases]
    hops = [pltpu.VMEM(lead + (Z - 1, rows, D), kind) for lead, rows, kind in cases]
    return halves + corners + sides + hops


def backward_kernel(sharded, *refs):
    dtop, norms, mixed_h, *refs = refs
    held, refs = refs[:10], refs[10:]
    if sharded:
        loss, feature, dlogits, dnorm, *refs = refs
        patch_share, attn_share, mlp_share, head_out, pos_sum, norm_sum, stats, *refs = refs
    else:
        grad_patch, grad_attn, grad_mlp, grad_norm, grad_pos, *refs = refs
    dx, dy, low, dout, dqkv, mixed, *refs = refs
    kept, sems, refs = refs[:10], refs[10], refs[11:]
    x, a, qkv, o, x1, a2, z, slope, attn_w, mlp_w = kept
    names = ("x", "a", "qkv", "o", "x1", "a2", "z", "slope", "attn", "mlp")

    def fetch(depth, *wanted):
        if depth < 0:
            return
        for name in wanted:
            n = names.index(name)
            pltpu.make_async_copy(held[n].at[depth], kept[n], sems.at[n]).start()

    def arrive(depth, *wanted):
        for name in wanted:
            n = names.index(name)
            pltpu.make_async_copy(held[n].at[depth], kept[n], sems.at[n]).wait()

    if sharded:
        place = Place()
        greet(place.partners())
    fetch(L - 1, "z", "mlp", "slope", "a2", "x1", "o", "attn", "qkv", "a", "x")
    mixed_copy = pltpu.make_async_copy(mixed_h, mixed, sems.at[len(names)])
    mixed_copy.start()
    due = {}
    if sharded:
        grad_patch, grad_attn, grad_mlp, grad_small, grad_norm, heads_all, head_rows, head_sum, gathered, squares, *refs = refs
        buffers, refs = refs[:16], refs[16:]
        send_sems, recv_sems, head_send, head_recv, last_send, last_recv = refs
        mine = (place.z, place.y, place.x, place.core)

        def count(total):
            flat = total.reshape(-1, D)
            squares[0:1, :] += jnp.sum(flat * flat, axis=0, keepdims=True)

        def share_patch(total):
            patch_share[...] = total[: patch_share.shape[0]]
            count(total)

        def share_attn(at, total):
            attn_share[at] = total
            count(total)

        def share_mlp(at, total):
            mlp_share[at] = total
            count(total)

        def share_small(total):
            gathered[mine + (slice(None), slice(0, D))] = total

        scatter = Scatter(
            place,
            scatter_pieces(
                (grad_patch, grad_attn, grad_mlp, grad_small),
                *(buffers[4 * n : 4 * n + 4] for n in range(4)),
                (share_patch, share_attn, share_mlp, share_small),
            ),
            send_sems,
            recv_sems,
        )
        heads = Gather(
            place,
            [lambda z, y, x, core: heads_all.at[z, y, x, core]],
            head_send,
            head_recv,
        )
        plan = [(HEAD_DUE, 0, heads, 0)]
        for turn in range(L):
            times = FINAL_DUE if turn == L - 1 else LAYER_DUE
            plan += [(times[n], turn, scatter, 3 * turn + n) for n in range(3)]
        plan += [(LAST_DUE, L - 1, scatter, piece) for piece in (PATCH_PIECE, SMALL_PIECE)]
        for times, turn, who, piece in plan:
            for stage in range(5):
                due.setdefault(10 * turn + times[stage], []).append((who, piece, stage + 1))
        squares[...] = jnp.zeros_like(squares)
        packed = [dlogits[:, HEAD_LANES:], jnp.zeros((8, HEAD_AT - 2 * C), F32), feature[...]]
        packed = jnp.concatenate(packed + [jnp.zeros((8, 2 * HEAD_LANES - HEAD_AT - D), F32)], axis=1)
        heads_all[mine] = jnp.concatenate([dlogits[:, :HEAD_LANES], packed], axis=0).astype(BF16)
        await_greetings(place.partners())

    def point(now):
        for who, piece, stage in due.pop(now, ()):
            who.step(piece, stage)

    point(-1)
    dx[...] = jnp.zeros((ALL, D), F32)
    for kind in range(2):
        for image in range(IMG):
            row = image * ROWS + NPATCH + kind
            dx[row : row + 1, :] = dtop[kind * IMG + image : kind * IMG + image + 1, :]
    grad_norm[...] = jnp.zeros((16, D), F32)
    for turn in range(L):
        depth = L - 1 - turn
        start = 10 * turn
        round_rows(dx, low)
        arrive(depth, "z")
        for m in range(BLOCKS):
            at = (m // 2, m % 2)
            grad_mlp[(depth, 1) + at] = tn(low[...], z[m]).astype(BF16).reshape(Z, Y, 48, D)
        point(start)
        arrive(depth, "mlp", "slope", "a2")
        for m in range(BLOCKS):
            at = (m // 2, m % 2)
            grad_gelu = nn(low[...], mlp_w[(1,) + at].reshape(D, D))
            grad_hidden = (grad_gelu * slope[m].astype(F32)).astype(BF16)
            grad_mlp[(depth, 0) + at] = tn(a2[...], grad_hidden).astype(BF16).reshape(Z, Y, 48, D)
            term = nt(grad_hidden, mlp_w[(0,) + at].reshape(D, D))
            dy[...] = term if m == 0 else dy[...] + term
            if m > 0:
                point(start + m)
        fetch(depth - 1, "z", "mlp", "slope", "a2")
        arrive(depth, "x1", "o", "attn")
        grad_in, gain, shift = norm_backward(dy[...], x1[...], norms[4 * depth + 2 : 4 * depth + 3, :])
        grad_norm[4 * depth + 2 : 4 * depth + 3, :] = gain
        grad_norm[4 * depth + 3 : 4 * depth + 4, :] = shift
        dx[...] += grad_in
        round_rows(dx, low)
        point(start + 4)
        grad_attn[depth, 3] = tn(low[...], o[...]).astype(BF16).reshape(Y, X, CORES, 48, D)
        dout[...] = nn(low[...], attn_w[3].reshape(D, D)).astype(BF16)
        fetch(depth - 1, "x1", "o")
        arrive(depth, "qkv")
        for image in range(IMG):
            for pair in range(3):
                attend_backward(qkv, dout, dqkv, image, pair)
            point(start + 5 + image)
        fetch(depth - 1, "qkv")
        arrive(depth, "a", "x")
        for n in range(3):
            part = dqkv[:, D * n : D * n + D]
            grad_attn[depth, n] = tn(part, a[...]).astype(BF16).reshape(Y, X, CORES, 48, D)
        point(start + 8)
        total = None
        for n in range(3):
            term = nn(dqkv[:, D * n : D * n + D], attn_w[n].reshape(D, D))
            total = term if total is None else total + term
        fetch(depth - 1, "attn", "a")
        grad_in, gain, shift = norm_backward(total, x[...], norms[4 * depth : 4 * depth + 1, :])
        grad_norm[4 * depth : 4 * depth + 1, :] = gain
        grad_norm[4 * depth + 1 : 4 * depth + 2, :] = shift
        dx[...] += grad_in
        fetch(depth - 1, "x")
        point(start + 9)
    total = dx[0:ROWS] + dx[ROWS : 2 * ROWS] + dx[2 * ROWS :]
    round_rows(dx, low)
    mixed_copy.wait()
    patch = tn(mixed[...], low[...])
    rows = PATCH_DIM // (Z * Y * X * CORES)
    for n in range(Z * Y * X * CORES):
        block = jnp.concatenate([patch[rows * n : rows * n + rows], jnp.zeros((32 - rows, D), F32)], axis=0)
        grad_patch[n // 8, n // 4 % 2, n // 2 % 2, n % 2] = block.astype(BF16)
    if not sharded:
        grad_pos[...] = total
        return
    small = [total[8 * n : 8 * n + 8] for n in range(ROWS // 8)]
    small += [grad_norm[0:8, :], jnp.concatenate([grad_norm[8:12, :], dnorm[0:2, :], jnp.zeros((2, D), F32)], axis=0)]
    small.append(jnp.concatenate([loss[...], jnp.zeros((8, D - 128), F32)], axis=1))
    for n in range(Z * Y * X * CORES):
        grad_small[n // 8, n // 4 % 2, n // 2 % 2, n % 2] = small[n] if n < len(small) else jnp.zeros((8, D), F32)
    left = sorted(due)
    for now in left[:2]:
        point(now)
    per_plane = head_rows.shape[0] // Z

    def unpack(n, carry):
        plane = heads_all[n].astype(F32).reshape(Y * X * CORES, 16, HEAD_LANES)
        for part in range(2):
            block = plane[:, 8 * part : 8 * part + 8].reshape(per_plane, HEAD_LANES)
            lanes = slice(part * HEAD_LANES, (part + 1) * HEAD_LANES)
            head_rows[pl.ds(n * per_plane, per_plane), lanes] = block.astype(BF16)
        return carry

    lax.fori_loop(0, Z, unpack, 0)
    features = head_rows[:, HEAD_AT : HEAD_AT + D]
    for n in range(0, 2 * C, 512):
        lanes = slice(n, min(n + 512, 2 * C))
        part = tn(head_rows[:, lanes], features)
        head_sum[lanes, :] = part
        squares[1:2, :] += jnp.sum(part * part, axis=0, keepdims=True)
    head_copy = pltpu.make_async_copy(head_sum, head_out, sems.at[len(names)])
    head_copy.start()
    for now in left[2:]:
        point(now)
    own = jnp.sum(squares[0:1, :], axis=(0, 1), keepdims=True)
    gathered[mine + (slice(None), slice(D, D + 128))] = jnp.broadcast_to(own, (8, 128))
    last = Gather(
        place, [lambda z, y, x, core: gathered.at[z, y, x, core]], last_send, last_recv, direct=True
    )
    for stage in range(1, 6):
        last.step(0, stage)
    blocks = [gathered[n // 8, n // 4 % 2, n // 2 % 2, n % 2] for n in range(Z * Y * X * CORES)]
    pos = jnp.concatenate([block[:, :D] for block in blocks[: ROWS // 8]], axis=0)
    norm = jnp.concatenate([block[:, :D] for block in blocks[ROWS // 8 : ROWS // 8 + 2]], axis=0)
    pos_sum[...] = jnp.concatenate([pos[NPATCH:TOK], pos[:NPATCH]], axis=0)
    norm_sum[...] = norm[: 4 * L + 2]
    total = blocks[0][:, D:]
    for block in blocks[1:]:
        total = total + block[:, D:]
    rest = jnp.sum(pos * pos, axis=0, keepdims=True) + jnp.sum(norm * norm, axis=0, keepdims=True) + squares[1:2, :]
    total = total[0:1, :] + jnp.sum(rest, axis=(0, 1), keepdims=True)
    norm_all = jnp.sqrt(total)
    stats[...] = jnp.concatenate(
        [blocks[ROWS // 8 + 2][0:1, :128], norm_all, jnp.minimum(1.0, MAX_NORM / norm_all), jnp.zeros((5, 128), F32)],
        axis=0,
    )
    head_copy.wait()
    scatter.finish()
    heads.finish()
    last.finish()


def backward(sharded, *operands):
    full = ((PATCH_SHAPE, BF16), (ATTN_SHAPE, BF16), (MLP_SHAPE, BF16))
    if sharded:
        outs = (
            ((PATCH_DIM // (Z * Y * X * CORES), D), F32),
            ((L, 48, D), F32),
            ((L, 2, 48, D), F32),
            ((2 * C, D), F32),
            ((TOK, D), F32),
            ((4 * L + 2, D), F32),
            ((8, 128), F32),
        )
    else:
        outs = full + (((16, D), F32), ((ROWS, D), F32))
    scratch = [((ALL, D), F32), ((ALL, D), F32), ((ALL, D), BF16), ((ALL, D), BF16), ((ALL, 3 * D), BF16), SAVED[0]]
    scratch = [pltpu.VMEM(*entry) for entry in scratch]
    scratch += [pltpu.VMEM(shape[1:], kind) for shape, kind in SAVED[1:]]
    scratch += [pltpu.SemaphoreType.DMA((11,))]
    if sharded:
        scratch += [pltpu.VMEM(*entry) for entry in full]
        scratch += [
            pltpu.VMEM(SMALL_SHAPE, F32),
            pltpu.VMEM((16, D), F32),
            pltpu.VMEM((Z, Y, X, CORES, 16, HEAD_LANES), BF16),
            pltpu.VMEM((Z * Y * X * CORES * 8, 2 * HEAD_LANES), BF16),
            pltpu.VMEM((2 * C, D), F32),
            pltpu.VMEM((Z, Y, X, CORES, 8, D + 128), F32),
            pltpu.VMEM((8, D), F32),
        ]
        scratch += scatter_scratch()
        scratch += [pltpu.SemaphoreType.DMA((N_GRADS, 8))] * 2
        scratch += [pltpu.SemaphoreType.DMA((1, PIECES))] * 4
    params = dict(collective_id=1, has_side_effects=True) if sharded else {}
    return pl.pallas_call(
        lambda *refs: backward_kernel(sharded, *refs),
        out_shape=[jax.ShapeDtypeStruct(*entry) for entry in outs],
        in_specs=[VMEM] * 2 + [HBM] * 11 + [VMEM] * (4 if sharded else 0),
        out_specs=[HBM if entry == ((2 * C, D), F32) else VMEM for entry in outs],
        scratch_shapes=scratch,
        compiler_params=pltpu.CompilerParams(vmem_limit_bytes=63 * 2**20, **params),
        name="backward",
    )(*operands)


def adam_kernel(*refs):
    stats_h, refs = refs[0], refs[1:]
    count = len(STEP_RATES)
    grads, weights, firsts, seconds = (refs[n * count : (n + 1) * count] for n in range(4))
    outs, (loss, norm), refs = refs[4 * count : 7 * count], refs[7 * count : 7 * count + 2], refs[7 * count + 2 :]
    stats, buffers, (stats_sem, in_sems, out_sems) = refs[0], refs[1 : 1 + 4 * count], refs[1 + 4 * count :]
    stats_copy = pltpu.make_async_copy(stats_h, stats, stats_sem.at[0])
    stats_copy.start()
    chunks = []
    for n in ADAM_ORDER:
        rows = grads[n].shape[0]
        step = HEAD_ROWS if rows > HEAD_ROWS else rows
        chunks += [(n, pl.ds(first, step)) for first in range(0, rows, step)]
    loads = []
    for at, (n, rows) in enumerate(chunks):
        sources = (weights[n], firsts[n], seconds[n], grads[n])
        loads.append(
            [
                pltpu.make_async_copy(source.at[rows], buffers[4 * n + k].at[rows], in_sems.at[at, k])
                for k, source in enumerate(sources)
            ]
        )
        for copy in loads[-1]:
            copy.start()
    stats_copy.wait()
    loss[...] = stats[0:1, 0:1]
    norm[...] = stats[1:2, 0:1]
    factor = stats[2:3, 0:1]
    stores = []
    for at, (n, rows) in enumerate(chunks):
        for copy in loads[at]:
            copy.wait()
        weight, first, second, grad = (buffers[4 * n + k].at[rows] for k in range(4))
        old = weight[...]
        clipped = grad[...] * factor.reshape((1,) * old.ndim)
        new_first = BETA_ONE * first[...] + (1.0 - BETA_ONE) * clipped
        new_second = BETA_TWO * second[...] + (1.0 - BETA_TWO) * clipped * clipped
        root = jnp.sqrt(new_second * (1.0 / (1.0 - BETA_TWO**ADAM_STEP))) + ADAM_EPS
        move = new_first * (1.0 / (1.0 - BETA_ONE**ADAM_STEP)) / root
        weight[...] = old - STEP_RATES[n] * (move + DECAY * old)
        first[...] = new_first
        second[...] = new_second
        for k in range(3):
            copy = pltpu.make_async_copy(
                buffers[4 * n + k].at[rows], outs[k * count + n].at[rows], out_sems.at[at, k]
            )
            copy.start()
            stores.append(copy)
    for copy in stores:
        copy.wait()


HEAD_ROWS = 400
ADAM_ORDER = (5, 0, 3, 1, 2, 4)


def adam(stats, grads, weights, firsts, seconds):
    shapes = [weight.shape for weight in weights]
    chunk_count = len(shapes) - 1 + 2 * C // HEAD_ROWS
    return pl.pallas_call(
        adam_kernel,
        out_shape=[jax.ShapeDtypeStruct(shape, F32) for shape in shapes * 3 + [(1, 1)] * 2],
        in_specs=[HBM] * (1 + 4 * len(shapes)),
        out_specs=[HBM] * (3 * len(shapes)) + [VMEM] * 2,
        scratch_shapes=[pltpu.VMEM((8, 128), F32)]
        + [pltpu.VMEM(shape, F32) for shape in shapes for _ in range(4)]
        + [pltpu.SemaphoreType.DMA((1,))]
        + [pltpu.SemaphoreType.DMA((chunk_count, 4)), pltpu.SemaphoreType.DMA((chunk_count, 3))],
        compiler_params=pltpu.CompilerParams(vmem_limit_bytes=63 * 2**20),
        name="adam",
    )(stats, *grads, *weights, *firsts, *seconds)


def per_device(
    patches, partners, mix_weight, labels, teacher_logits,
    patch_weight, attn_weight, mlp_weight, positions, head_weight, norm_params,
    patch_first, attn_first, mlp_first, pos_first, head_first, norm_first,
    patch_second, attn_second, mlp_second, pos_second, head_second, norm_second,
):
    axes = ("dp", "mp")
    image_count = patches.shape[0] * lax.axis_size("dp") * lax.axis_size("mp")
    sharded = (lax.axis_size("dp"), lax.axis_size("mp")) == (Z * Y, X * CORES)
    attn_t = jnp.swapaxes(attn_weight, 1, 2)
    if sharded:
        weights_in = (patch_weight, attn_t, mlp_weight)
    else:
        patch_low = lax.all_gather(patch_weight.astype(BF16), axes, axis=0, tiled=True)
        attn_low = lax.all_gather(attn_t.astype(BF16), axes, axis=1, tiled=True)
        mlp_low = lax.all_gather(mlp_weight.astype(BF16), "dp", axis=2, tiled=True)
        mlp_low = lax.all_gather(mlp_low, "mp", axis=2, tiled=False)
        weights_in = (patch_low, attn_low.reshape(ATTN_SHAPE), mlp_low.reshape(MLP_SHAPE))
    results = forward(
        image_count, sharded, partners, mix_weight, labels, patches, teacher_logits, positions,
        head_weight.T, norm_params, *weights_in,
    )
    saved, (loss, feature, dlogits, dtop, dnorm) = results[: len(SAVED)], results[len(SAVED) :]
    operands = (dtop, norm_params, *saved)
    if sharded:
        patch_share, attn_share, mlp_share, head_sum, pos_sum, norm_sum, stats = backward(
            True, *operands, loss, feature, dlogits, dnorm
        )
        mlp_share = mlp_share.reshape(mlp_weight.shape)
    else:
        grad_patch, grad_attn, grad_mlp, grad_norm, grad_pos = backward(False, *operands)
        rows = PATCH_DIM // (Z * Y * X * CORES)
        grad_patch = grad_patch.reshape(-1, 32, D)[:, :rows].reshape(PATCH_DIM, D).astype(F32)
        patch_share = lax.psum_scatter(grad_patch, axes, scatter_dimension=0, tiled=True)
        grad_attn = grad_attn.reshape(L, 4 * D, D).astype(F32)
        attn_share = lax.psum_scatter(grad_attn, axes, scatter_dimension=1, tiled=True)
        grad_mlp = grad_mlp.reshape(L, 2, BLOCKS, D, D).astype(F32)
        mlp_share = lax.psum_scatter(grad_mlp, "mp", scatter_dimension=2, tiled=True)
        mlp_share = lax.psum_scatter(mlp_share, "dp", scatter_dimension=3, tiled=True)
        mlp_share = mlp_share.reshape(mlp_weight.shape)
        features = lax.all_gather(feature.astype(BF16), axes, axis=0, tiled=True)
        all_dlogits = lax.all_gather(dlogits.astype(BF16), axes, axis=0, tiled=True)
        head_sum = tn(all_dlogits, features)
        grad_norms = jnp.concatenate([grad_norm[: 4 * L], dnorm[:2]], axis=0)
        grad_pos = jnp.concatenate([grad_pos[NPATCH:TOK], grad_pos[:NPATCH]], axis=0)
        pos_sum, norm_sum, loss_sum = lax.psum((grad_pos, grad_norms, loss[0, 0]), axes)
        own_squares = sum(jnp.sum(share * share) for share in (patch_share, attn_share, mlp_share))
        shared = sum(jnp.sum(total * total) for total in (pos_sum, head_sum, norm_sum))
        global_norm = jnp.sqrt(lax.psum(own_squares, axes) + shared)
        factor = jnp.minimum(1.0, MAX_NORM / global_norm)
        stats = jnp.stack([loss_sum, global_norm, factor] + [jnp.float32(0.0)] * 5)
        stats = jnp.broadcast_to(stats[:, None], (8, 128))
    weights = (patch_weight, attn_weight, mlp_weight, positions, head_weight, norm_params)
    firsts = (patch_first, attn_first, mlp_first, pos_first, head_first, norm_first)
    seconds = (patch_second, attn_second, mlp_second, pos_second, head_second, norm_second)

    def turned(arrays):
        return (arrays[0], jnp.swapaxes(arrays[1], 1, 2), arrays[2], arrays[3], arrays[4].T, arrays[5])

    grads = (patch_share, attn_share, mlp_share, pos_sum, head_sum, norm_sum)
    *updated, loss_sum, global_norm = adam(stats, grads, turned(weights), turned(firsts), turned(seconds))
    return (loss_sum.reshape(()), global_norm.reshape(()), *(out for n in range(3) for out in turned(updated[6 * n : 6 * n + 6])))


def solution(mesh):
    images = (P(("dp", "mp"), None, None), P(("dp", "mp")), P(("dp", "mp")), P(("dp", "mp")), P(("dp", "mp"), None))
    weights = (P(("dp", "mp"), None), P(None, None, ("dp", "mp")), P(None, None, "dp", "mp"), P(), P(), P())
    return jax.shard_map(
        per_device,
        mesh=mesh,
        in_specs=images + weights * 3,
        out_specs=(P(), P()) + weights * 3,
        check_vma=False,
    )
```
